32 devices in a mesh: space: 8 (over z, x), slab: 4 (over y, core).
Axes of the slice: x: 2, y: 2, z: 4, core: 2. Of those that a mesh axis runs over, the one named last changes fastest.
Arguments:
- tokens: float32 [8192, 512], P(('space', 'slab')), may hold values from -6 to 6
- gain: float32 [512], replicated, may hold values from 0.25 to 1.75
- query_weight: float32 [512, 512], replicated, may hold values from -3.1 to 3.1
- key_weight: float32 [512, 512], replicated, may hold values from -0.25 to 0.25
- value_weight: float32 [512, 512], replicated, may hold values from -0.25 to 0.25
- output_weight: float32 [512, 512], replicated, may hold values from -0.25 to 0.25
- neighbour_list: int32 [64, 3], P(('space', 'slab')), may hold values from 0 to 5, as said below
- neighbour_count: int32 [64], P(('space', 'slab')), may hold values from 1 to 3, as said below
- cotangent: float32 [8192, 512], P(('space', 'slab')), may hold values from -6 to 6
Outputs:
- result: float32 [8192, 512], P(('space', 'slab'))
- d_tokens: float32 [8192, 512], P(('space', 'slab'))
- d_gain: float32 [512], replicated
- d_query: float32 [512, 512], replicated
- d_key: float32 [512, 512], replicated
- d_value: float32 [512, 512], replicated
- d_output: float32 [512, 512], replicated
The draws below stay inside these ranges and needn't reach their ends.
Inputs may be any that keep to these rules, and one draw needn't show every extreme that they name: `neighbour_list`: each row holds distinct window indices, never the patch's own index 2 + p % 2. Only the first neighbour_count[p] entries of a row are live.
All inputs are finite; a program needn't handle non-finite values.
Results may differ from the reference program's by a relative error of at most 0.0003.
Values sent between devices are 32-bit elements; how exact they have to be, the bound alone decides.
No kernel may reach another device: no remote copies, remote signals or barrier semaphores. Data moves between devices by JAX's collectives and lax.ppermute only.
A program may use at most 128 MiB of HBM per device.

```python
import jax
import jax.numpy as jnp
from jax import lax

D = 512
HEADS = 8
PT = 128
NB = 3
P_DEV = 2
PATCHES = 64
TOKENS = 8192
N_SPACE = 8
N_SLAB = 4


def draw_query_weight(key, part):
    return jnp.clip(jax.random.normal(key, (D, D), jnp.float32), -6.0, 6.0) * D ** (-0.5)


def draw_neighbour_list(key, part):
    candidates = 3 * P_DEV - 1
    row_keys = jax.random.split(jax.random.fold_in(key, 11), PATCHES)
    picked = jax.vmap(lambda row_key: jax.random.permutation(row_key, candidates))(row_keys)[:, :NB]
    own_blocks = P_DEV + jnp.arange(PATCHES, dtype=jnp.int32) % P_DEV
    return jnp.where(picked >= own_blocks[:, None], picked + 1, picked).astype(jnp.int32)


def draw_neighbour_count(key, part):
    base = jax.random.randint(jax.random.fold_in(key, 5), (PATCHES,), 1, NB + 1)
    start = jax.random.randint(jax.random.fold_in(key, 3), (), 0, PATCHES)
    distance = (jnp.arange(PATCHES, dtype=jnp.int32) - start) % PATCHES
    return jnp.where(distance < PATCHES // 8, NB, base).astype(jnp.int32)


def steps_of(own_key, shape, cuts, smallest, high):
    loudness, own = 1.0, jax.random.fold_in(own_key, 6)
    for position, shards_of in cuts:
        steps = jnp.exp(jax.random.uniform(jax.random.fold_in(own, position), (shards_of,), jnp.float32, smallest / len(cuts), high / len(cuts)))
        loudness = loudness * jnp.repeat(steps, shape[position] // shards_of).reshape([-1 if axis == position else 1 for axis in range(len(shape))])
    return loudness


def noise(own_key, extent, spread, reach, cuts=(), kind=jnp.bfloat16):
    drawn = spread * jax.random.normal(own_key, extent, jnp.float32)
    if cuts:
        drawn = drawn * steps_of(own_key, extent, cuts, -0.22, 0.18)
    return jnp.clip(drawn, -reach, reach).astype(kind)


def setup_inputs(seed: int = 0) -> dict:
    streams_of = jax.random.split(jax.random.key(seed), 10)
    tokens = noise(streams_of[0], (TOKENS, D), 1.0, 6.0, ((0, 32),), jnp.float32)
    gain = jnp.clip(1.0 + 0.15 * jax.random.normal(streams_of[1], (D,), jnp.float32), 0.25, 1.75)
    query_weight = draw_query_weight(jax.random.fold_in(streams_of[9], 71), 0)
    key_weight = noise(streams_of[3], (D, D), D ** -0.5, 0.25, (), jnp.float32)
    value_weight = noise(streams_of[4], (D, D), D ** -0.5, 0.25, (), jnp.float32)
    output_weight = noise(streams_of[5], (D, D), D ** -0.5, 0.25, (), jnp.float32)
    neighbour_list = draw_neighbour_list(jax.random.fold_in(streams_of[9], 71), 0)
    neighbour_count = draw_neighbour_count(jax.random.fold_in(streams_of[9], 71), 0)
    cotangent = noise(streams_of[8], (TOKENS, D), 1.0, 6.0, ((0, 32),), jnp.float32)
    return {"tokens": tokens, "gain": gain, "query_weight": query_weight, "key_weight": key_weight, "value_weight": value_weight, "output_weight": output_weight, "neighbour_list": neighbour_list, "neighbour_count": neighbour_count, "cotangent": cotangent}


def matmul(left, right):
    return jnp.dot(left, right, precision=lax.Precision.HIGHEST, preferred_element_type=jnp.float32)

def normalize(tokens, gain):
    row_mean = lax.optimization_barrier(jnp.mean(tokens, axis=1, keepdims=True))
    centred = tokens - row_mean
    variance = lax.optimization_barrier(jnp.mean(centred * centred, axis=1, keepdims=True))
    return centred * lax.rsqrt(variance + 1e-05) * gain[None, :]

def attention(query, key_win, value_win, block_index, live_mask):
    patch_count = block_index.shape[0]
    model_width = query.shape[1]
    head_dim = model_width // HEADS
    picked_keys = key_win.reshape(-1, PT, model_width)[block_index].reshape(patch_count, -1, HEADS, head_dim)
    picked_values = value_win.reshape(-1, PT, model_width)[block_index].reshape(patch_count, -1, HEADS, head_dim)
    query_blocks = query.reshape(patch_count, PT, HEADS, head_dim)
    scores = jnp.einsum('pqhd,pkhd->phqk', query_blocks, picked_keys, precision=lax.Precision.HIGHEST) * head_dim ** (-0.5)
    key_mask = jnp.repeat(live_mask, PT, axis=1)
    scores = jnp.where(key_mask[:, None, None, :], scores, -1e+30)
    row_max = lax.optimization_barrier(jnp.max(scores, axis=3, keepdims=True))
    weights = jnp.exp(scores - row_max)
    probability = weights / lax.optimization_barrier(jnp.sum(weights, axis=3, keepdims=True))
    mixed = jnp.einsum('phqk,pkhd->pqhd', probability, picked_values, precision=lax.Precision.HIGHEST)
    return mixed.reshape(patch_count * PT, model_width)

def reference(tokens, gain, query_weight, key_weight, value_weight, output_weight, neighbour_list, neighbour_count, cotangent):
    device_count = N_SPACE * N_SLAB
    own_blocks = P_DEV + jnp.arange(PATCHES, dtype=jnp.int32) % P_DEV
    block_index = jnp.concatenate([own_blocks[:, None], neighbour_list], axis=1).reshape(device_count, P_DEV, NB + 1)
    slot_ids = jnp.arange(NB, dtype=jnp.int32)
    live_mask = jnp.concatenate([jnp.ones((PATCHES, 1), dtype=bool), slot_ids[None, :] < neighbour_count[:, None]], axis=1)
    live_mask = live_mask.reshape(device_count, P_DEV, NB + 1)

    def windows(field):
        grid = field.reshape(N_SPACE, N_SLAB, P_DEV * PT, D)
        joined = jnp.concatenate([jnp.roll(grid, 1, axis=0), grid, jnp.roll(grid, -1, axis=0)], axis=2)
        return joined.reshape(device_count, 3 * P_DEV * PT, D)

    def one_device(pieces):
        return attention(pieces[0], pieces[1], pieces[2], pieces[3], pieces[4])

    def forward(tokens, gain, query_weight, key_weight, value_weight, output_weight):
        hidden = normalize(tokens, gain)
        query = matmul(hidden, query_weight)
        key_rows = matmul(hidden, key_weight)
        value_rows = matmul(hidden, value_weight)
        mixed = lax.map(jax.checkpoint(one_device), (query.reshape(device_count, P_DEV * PT, D), windows(key_rows), windows(value_rows), block_index, live_mask))
        return matmul(mixed.reshape(TOKENS, D), output_weight) + tokens
    result, pullback = jax.vjp(forward, tokens, gain, query_weight, key_weight, value_weight, output_weight)
    d_tokens, d_gain, d_query, d_key, d_value, d_output = pullback(cotangent)
    return (result, d_tokens, d_gain, d_query, d_key, d_value, d_output)
```

```python
import functools

import jax
import jax.numpy as jnp
from jax import lax
from jax.experimental import pallas as pl
from jax.experimental.pallas import tpu as pltpu
from jax.sharding import PartitionSpec as P

HEADS = 8
PT = 128
HD = 64
PAIRS = HEADS // 2
F32 = jnp.float32
BF16 = jnp.bfloat16
NN = (((1,), (0,)), ((), ()))
NT = (((1,), (1,)), ((), ()))
VMEM = pl.BlockSpec(memory_space=pltpu.VMEM)
SMEM = pl.BlockSpec(memory_space=pltpu.SMEM)


def pair_of(x):
    high = x.astype(BF16)
    return high, (x - high.astype(F32)).astype(BF16)


def dot(left, right, dims=NN):
    return lax.dot_general(left, right, dims, preferred_element_type=F32)


def dot3(left, right, dims=NN):
    return dot(left[0], right[0], dims) + (dot(left[0], right[1], dims) + dot(left[1], right[0], dims))


def load(refs, *index):
    return refs[0][index], refs[1][index]


def store(refs, pair, *index):
    refs[0][index] = pair[0]
    refs[1][index] = pair[1]


def unit_rows(tokens):
    centred = tokens - jnp.mean(tokens, axis=1, keepdims=True)
    variance = jnp.mean(centred * centred, axis=1, keepdims=True)
    rstd = lax.rsqrt(variance + 1e-05)
    return centred * rstd, rstd


def store_stacked(ref, row, rows):
    count = rows.shape[0]
    left_half = lax.broadcasted_iota(jnp.int32, (count, 2 * HD), 1) < HD
    for p in range(PAIRS):
        part = rows[:, p * 2 * HD : (p + 1) * 2 * HD]
        swapped = pltpu.roll(part, HD, 1)
        for a in range(2):
            both = jnp.where(left_half == (a == 0), part, swapped)
            high, low = pair_of(both)
            base = (2 * p + a) * 4 * HD
            ref[pl.ds(row, count), base : base + 2 * HD] = high
            ref[pl.ds(row, count), base + 2 * HD : base + 4 * HD] = low


def pre_kernel(
    tokens, gain, wq, wk, wv, wo, cot,
    xhat, ht_h, ht_l, q_h, q_l, q_stack, k_stack, v_stack, kt_h, kt_l, vt_h, vt_l, dot_out,
    wq_h, wq_l, wk_h, wk_l, wv_h, wv_l, wo_h, wo_l,
):
    for source, high, low in ((wq, wq_h, wq_l), (wk, wk_h, wk_l), (wv, wv_h, wv_l), (wo, wo_h, wo_l)):
        store((high, low), pair_of(source[...]), ...)
    normal, _ = unit_rows(tokens[...])
    xhat[...] = normal
    hidden = normal * gain[...]
    store((ht_h, ht_l), pair_of(hidden.T), ...)
    rows = pair_of(hidden)
    query = dot3(rows, load((wq_h, wq_l), ...)) * HD ** (-0.5)
    store((q_h, q_l), pair_of(query), ...)
    qt_h, qt_l = pair_of(query.T)
    for h in range(HEADS):
        high, low = qt_h[h * HD : (h + 1) * HD], qt_l[h * HD : (h + 1) * HD]
        for i, piece in enumerate((high, low, high, low)):
            q_stack[h * 4 * HD + i * HD : h * 4 * HD + (i + 1) * HD, :] = piece
    key = dot3(rows, load((wk_h, wk_l), ...))
    store_stacked(k_stack, 0, key)
    store((kt_h, kt_l), pair_of(key.T), ...)
    value = dot3(rows, load((wv_h, wv_l), ...))
    store_stacked(v_stack, 0, value)
    store((vt_h, vt_l), pair_of(value.T), ...)
    dot_out[...] = dot3(load((wo_h, wo_l), ...), pair_of(cot[...]), NT)


def main_kernel(
    listed, counts, before, after, gain, tokens, cot,
    xhat, ht_h, ht_l, q_h, q_l, q_stack, k_stack, v_stack, kt_h, kt_l, vt_h, vt_l, dot_out,
    wq_h, wq_l, wk_h, wk_l, wv_h, wv_l, wo_h, wo_l,
    result, dh_own, dh_before, dh_after, grads, d_gain,
    bias, xhat2, ht2_h, ht2_l, k_stack2, v_stack2, kt2_h, kt2_l, vt2_h, vt2_l,
    e_h, e_l, s_h, s_l, mixed_t, dq_t, dk_h, dk_l, dv_h, dv_l,
):
    own = tokens.shape[0]
    halo = 2 * own
    lane = lax.broadcasted_iota(jnp.int32, (1, own), 1)
    for place, w in enumerate((2, 3, 0, 1, 4, 5)):
        level = []
        for p in range(2):
            live = jnp.int32(1 if w == 2 + p else 0)
            for j in range(listed.shape[1]):
                hit = jnp.logical_and(j < counts[0, p], listed[p, j] == w)
                live = jnp.where(hit, 1, live)
            level.append(jnp.where(live == 1, 0.0, -1e30).astype(F32))
        bias[place : place + 1, :] = jnp.where(lane < PT, level[0], level[1])

    for i, rows_ref in enumerate((before, after)):
        normal, _ = unit_rows(rows_ref[...])
        at = slice(i * own, (i + 1) * own)
        xhat2[at, :] = normal
        hidden = normal * gain[...]
        store((ht2_h, ht2_l), pair_of(hidden.T), slice(None), at)
        rows = pair_of(hidden)
        key = dot3(rows, load((wk_h, wk_l), ...))
        store_stacked(k_stack2, i * own, key)
        store((kt2_h, kt2_l), pair_of(key.T), slice(None), at)
        value = dot3(rows, load((wv_h, wv_l), ...))
        store_stacked(v_stack2, i * own, value)
        store((vt2_h, vt2_l), pair_of(value.T), slice(None), at)

    def biased(scores, first):
        return jnp.concatenate(
            [scores[i * PT : (i + 1) * PT] + bias[first + i : first + i + 1, :] for i in range(scores.shape[0] // PT)],
            axis=0,
        )

    def joined(one, two, rows):
        return jnp.concatenate([one[rows, :], two[rows, :]], axis=1)

    left_half = lax.broadcasted_iota(jnp.int32, (own, 2 * HD), 1) < HD

    def masked(pair, a):
        keep = left_half == (a == 0)
        zero = jnp.zeros_like(pair[0])
        return jnp.where(keep, pair[0], zero), jnp.where(keep, pair[1], zero)

    def gathered(left_h, left_l, right):
        one, two = masked(right, 0), masked(right, 1)
        wide = dot(left_h[0], jnp.concatenate(one, axis=1)) + dot(left_h[1], jnp.concatenate(two, axis=1))
        narrow = dot(left_l[0], one[0]) + dot(left_l[1], two[0])
        return wide[:, : 2 * HD] + (wide[:, 2 * HD :] + narrow)

    def one_pair(p, carry):
        scaled = []
        for a in range(2):
            head = pl.ds(pl.multiple_of(p * 2 * HD + a * HD, HD), HD)
            stack = pl.ds(pl.multiple_of((2 * p + a) * 4 * HD, 4 * HD), 4 * HD)
            q_now = q_stack[stack, :]
            s_own = biased(dot(k_stack[:, stack], q_now), 0)
            s_halo = biased(dot(k_stack2[:, stack], q_now), 2)
            top = jnp.maximum(jnp.max(s_own, axis=0, keepdims=True), jnp.max(s_halo, axis=0, keepdims=True))
            e_own, e_halo = jnp.exp(s_own - top), jnp.exp(s_halo - top)
            total = jnp.sum(e_own, axis=0, keepdims=True) + jnp.sum(e_halo, axis=0, keepdims=True)
            e_all = jnp.concatenate([e_own, e_halo], axis=0)
            high, low = pair_of(e_all)
            e_h[a] = high
            e_l[a] = low
            v_high, v_low = joined(vt_h, vt2_h, head), joined(vt_l, vt2_l, head)
            both = dot(jnp.concatenate([v_high, v_low], axis=0), high)
            mixed = both[:HD] + (both[HD:] + dot(v_high, low))
            share = 1.0 / total
            mixed = mixed * share
            mixed_t[head, :] = mixed
            d_mixed = dot_out[head, :] * share
            scaled.append(d_mixed)
            delta = jnp.sum(d_mixed * mixed, axis=0, keepdims=True)
            d_high, d_low = pair_of(d_mixed)
            d_now = jnp.concatenate([d_high, d_low, d_high, d_low], axis=0)
            d_scores = jnp.concatenate([dot(v_stack[:, stack], d_now), dot(v_stack2[:, stack], d_now)], axis=0)
            d_scores = (d_scores - delta) * (e_h[a].astype(F32) + e_l[a].astype(F32))
            high, low = pair_of(d_scores)
            s_h[a] = high
            s_l[a] = low
            k_high, k_low = joined(kt_h, kt2_h, head), joined(kt_l, kt2_l, head)
            both = dot(jnp.concatenate([k_high, k_low], axis=0), high)
            dq_t[head, :] = (both[:HD] + (both[HD:] + dot(k_high, low))) * HD ** (-0.5)
        lanes = pl.ds(pl.multiple_of(p * 2 * HD, 2 * HD), 2 * HD)
        d_rows = pair_of(jnp.concatenate(scaled, axis=0).T)
        store((dv_h, dv_l), pair_of(gathered((e_h[0], e_h[1]), (e_l[0], e_l[1]), d_rows)), slice(None), lanes)
        q_rows = (q_h[:, lanes], q_l[:, lanes])
        store((dk_h, dk_l), pair_of(gathered((s_h[0], s_h[1]), (s_l[0], s_l[1]), q_rows)), slice(None), lanes)
        return carry

    lax.fori_loop(0, PAIRS, one_pair, 0)

    w_q, w_k, w_v, w_o = (load(w, ...) for w in ((wq_h, wq_l), (wk_h, wk_l), (wv_h, wv_l), (wo_h, wo_l)))
    width = tokens.shape[1]
    mixed = mixed_t[...]
    result[...] = dot3(pair_of(mixed.T), w_o) + tokens[...]
    grads[3 * width :, :] = dot3(pair_of(mixed), pair_of(cot[...]))
    d_query = pair_of(dq_t[...].T)
    ht, ht2 = load((ht_h, ht_l), ...), load((ht2_h, ht2_l), ...)
    grads[:width, :] = dot3(ht, d_query)
    first, rest = slice(0, own), slice(own, own + halo)
    for i, pair in ((1, (dk_h, dk_l)), (2, (dv_h, dv_l))):
        grads[i * width : (i + 1) * width, :] = dot3(ht, load(pair, first)) + dot3(ht2, load(pair, rest))
    d_own = (
        dot3(d_query, w_q, NT) + dot3(load((dk_h, dk_l), first), w_k, NT) + dot3(load((dv_h, dv_l), first), w_v, NT)
    )
    dh_own[...] = d_own
    gain_sum = jnp.sum(d_own * xhat[...], axis=0, keepdims=True)
    for i, out in enumerate((dh_before, dh_after)):
        at = slice(own + i * own, 2 * own + i * own)
        d_part = dot3(load((dk_h, dk_l), at), w_k, NT) + dot3(load((dv_h, dv_l), at), w_v, NT)
        out[...] = d_part
        gain_sum = gain_sum + jnp.sum(d_part * xhat2[i * own : (i + 1) * own, :], axis=0, keepdims=True)
    d_gain[...] = gain_sum


def post_kernel(tokens, gain, cot, d_own, d_one, d_two, out):
    normal, rstd = unit_rows(tokens[...])
    d_normal = (d_own[...] + (d_one[...] + d_two[...])) * gain[...]
    inner = jnp.mean(d_normal * normal, axis=1, keepdims=True)
    centre = jnp.mean(d_normal, axis=1, keepdims=True)
    out[...] = (d_normal - centre - normal * inner) * rstd + cot[...]


def shape(*dims, dtype=F32):
    return jax.ShapeDtypeStruct(dims, dtype)


def pairs(*dims):
    return [shape(*dims, dtype=BF16)] * 2


def call(kernel, inputs, outputs, scratch=(), scalars=0, limit=56):
    return pl.pallas_call(
        kernel,
        out_shape=outputs,
        in_specs=[SMEM] * scalars + [VMEM] * (len(inputs) - scalars),
        out_specs=[VMEM] * len(outputs),
        scratch_shapes=[pltpu.VMEM(s.shape, s.dtype) for s in scratch],
        compiler_params=pltpu.CompilerParams(vmem_limit_bytes=limit * 2**20),
    )(*inputs)


def shifted(value, axis, steps):
    count = lax.axis_size(axis)
    return lax.ppermute(value, axis, [(i, (i + steps) % count) for i in range(count)])


def swapped(value, axis, mask):
    return lax.ppermute(value, axis, [(i, i ^ mask) for i in range(lax.axis_size(axis))])


def side(axis, mask):
    return (lax.axis_index(axis) // mask) % 2


def half(value, index):
    rows = value.shape[0] // 2
    return lax.dynamic_slice_in_dim(value, index * rows, rows, 0)


def halved(value, dim):
    mine = side(*dim)
    return half(value, mine) + swapped(half(value, 1 - mine), *dim)


def doubled(value, dim):
    mine = side(*dim)
    other = swapped(value, *dim)
    return jnp.concatenate([jnp.where(mine == 0, value, other), jnp.where(mine == 0, other, value)], axis=0)


def bits(axis):
    return [(axis, 1 << k) for k in range((lax.axis_size(axis) - 1).bit_length())]


def summed(value):
    slab, space = bits("slab"), bits("space")
    first, rest = slab[0], slab[1:] + space
    cross, along, last = rest[0], rest[1], rest[2:]
    orders = [[along, cross, *last], [cross, last[0], along, *last[1:]], [last[0], along, cross, *last[1:]]]
    value = halved(value, first)
    rows = value.shape[0]
    step = 1 << len(rest)
    third = -(-rows // (3 * step)) * step
    parts = [value[:third], value[third : 2 * third], value[2 * third :]]
    for i in range(len(rest)):
        parts = [halved(part, order[i]) for part, order in zip(parts, orders)]
    for i in reversed(range(len(rest))):
        parts = [doubled(part, order[i]) for part, order in zip(parts, orders)]
    return doubled(jnp.concatenate(parts, axis=0), first)


def body(tokens, gain, wq, wk, wv, wo, neighbour_list, neighbour_count, cotangent):
    rows, width = tokens.shape
    before, after = shifted(tokens, "space", 1), shifted(tokens, "space", -1)
    gain_row = gain[None, :]
    mid = call(
        pre_kernel,
        (tokens, gain_row, wq, wk, wv, wo, cotangent),
        [
            shape(rows, width), *pairs(width, rows), *pairs(rows, width),
            shape(HEADS * 4 * HD, rows, dtype=BF16),
            shape(rows, HEADS * 4 * HD, dtype=BF16), shape(rows, HEADS * 4 * HD, dtype=BF16),
            *pairs(width, rows), *pairs(width, rows), shape(width, rows),
            *pairs(width, width), *pairs(width, width), *pairs(width, width), *pairs(width, width),
        ],
    )
    halo, window = 2 * rows, 3 * rows
    result, d_own, d_before, d_after, grads, d_gain = call(
        main_kernel,
        (neighbour_list, neighbour_count[None, :], before, after, gain_row, tokens, cotangent, *mid),
        [shape(rows, width)] * 4 + [shape(4 * width, width), shape(1, width)],
        [
            shape(8, rows), shape(halo, width), *pairs(width, halo),
            shape(halo, HEADS * 4 * HD, dtype=BF16), shape(halo, HEADS * 4 * HD, dtype=BF16),
            *pairs(width, halo), *pairs(width, halo),
            *pairs(2, window, rows), *pairs(2, window, rows),
            shape(width, rows), shape(width, rows), *pairs(window, width), *pairs(window, width),
        ],
        scalars=2,
    )
    from_after, from_before = shifted(d_before, "space", -1), shifted(d_after, "space", 1)
    (d_tokens,) = call(
        post_kernel, (tokens, gain_row, cotangent, d_own, from_after, from_before), [shape(rows, width)]
    )
    grads = summed(grads)
    d_gain = lax.psum(d_gain[0], ("space", "slab"))
    gq, gk, gv, go = (grads[i * width : (i + 1) * width] for i in range(4))
    return (result, d_tokens, d_gain, gq, gk, gv, go)


def solution(mesh):
    tokens = P(("space", "slab"), None)
    return jax.shard_map(
        body,
        mesh=mesh,
        in_specs=(tokens, P(), P(), P(), P(), P(), tokens, P(("space", "slab")), tokens),
        out_specs=(tokens, tokens, P(), P(), P(), P(), P()),
        check_vma=False,
    )
```

```python
import functools

import jax
import jax.numpy as jnp
from jax import lax
from jax.experimental import pallas as pl
from jax.experimental.pallas import tpu as pltpu
from jax.sharding import PartitionSpec as P

HEADS = 8
PT = 128
HD = 64
PAIRS = HEADS // 2
F32 = jnp.float32
BF16 = jnp.bfloat16
NN = (((1,), (0,)), ((), ()))
NT = (((1,), (1,)), ((), ()))
VMEM = pl.BlockSpec(memory_space=pltpu.VMEM)
SMEM = pl.BlockSpec(memory_space=pltpu.SMEM)


def pair_of(x):
    high = x.astype(BF16)
    return high, (x - high.astype(F32)).astype(BF16)


def dot(left, right, dims=NN):
    return lax.dot_general(left, right, dims, preferred_element_type=F32)


def dot3(left, right, dims=NN):
    return dot(left[0], right[0], dims) + (dot(left[0], right[1], dims) + dot(left[1], right[0], dims))


def load(refs, *index):
    return refs[0][index], refs[1][index]


def store(refs, pair, *index):
    refs[0][index] = pair[0]
    refs[1][index] = pair[1]


def unit_rows(tokens):
    centred = tokens - jnp.mean(tokens, axis=1, keepdims=True)
    variance = jnp.mean(centred * centred, axis=1, keepdims=True)
    rstd = lax.rsqrt(variance + 1e-05)
    return centred * rstd, rstd


def store_stacked(ref, row, rows):
    count = rows.shape[0]
    left_half = lax.broadcasted_iota(jnp.int32, (count, 2 * HD), 1) < HD
    for p in range(PAIRS):
        part = rows[:, p * 2 * HD : (p + 1) * 2 * HD]
        swapped = pltpu.roll(part, HD, 1)
        for a in range(2):
            both = jnp.where(left_half == (a == 0), part, swapped)
            high, low = pair_of(both)
            base = (2 * p + a) * 4 * HD
            ref[pl.ds(row, count), base : base + 2 * HD] = high
            ref[pl.ds(row, count), base + 2 * HD : base + 4 * HD] = low


def store_interleaved(ref, columns):
    high, low = pair_of(columns)
    for h in range(HEADS):
        for i, piece in enumerate((high, low, high, low)):
            at = h * 4 * HD + i * HD
            ref[at : at + HD, :] = piece[h * HD : (h + 1) * HD]


def sums_of(left, right, dims=NN):
    return sum(dot3(a, b, dims) for a, b in zip(left[1:], right[1:], strict=True)) + dot3(left[0], right[0], dims)


def weight_kernel(_me, _parity, wq, wk, wv, wo, wq_h, wq_l, wk_h, wk_l, wv_h, wv_l, wo_h, wo_l):
    for source, high, low in ((wq, wq_h, wq_l), (wk, wk_h, wk_l), (wv, wv_h, wv_l), (wo, wo_h, wo_l)):
        store((high, low), pair_of(source[...]), ...)


def own_kernel(
    _, tokens, gain, cot, wq_h, wq_l, wk_h, wk_l, wv_h, wv_l, wo_h, wo_l,
    xhat, ht_h, ht_l, q_t, q_stack, k_stack, v_stack, kt_h, kt_l, vt_h, vt_l, d_mixed_t, d_stack,
):
    normal, _ = unit_rows(tokens[...])
    xhat[...] = normal
    hidden = normal * gain[...]
    store((ht_h, ht_l), pair_of(hidden.T), ...)
    rows = pair_of(hidden)
    query = dot3(rows, load((wq_h, wq_l), ...)) * HD ** (-0.5)
    q_t[...] = query.T
    store_interleaved(q_stack, q_t[...])
    key = dot3(rows, load((wk_h, wk_l), ...))
    store_stacked(k_stack, 0, key)
    store((kt_h, kt_l), pair_of(key.T), ...)
    value = dot3(rows, load((wv_h, wv_l), ...))
    store_stacked(v_stack, 0, value)
    store((vt_h, vt_l), pair_of(value.T), ...)
    d_mixed = dot3(load((wo_h, wo_l), ...), pair_of(cot[...]), NT)
    d_mixed_t[...] = d_mixed
    store_interleaved(d_stack, d_mixed)


def store_bias(bias, listed, counts, parity, patches):
    queries = bias.shape[1]
    lane = lax.broadcasted_iota(jnp.int32, (1, queries), 1)
    near = jnp.where(parity[0] == 0, 4, 0)
    windows = (2, 3, near, near + 1, 4 - near, 5 - near)
    for place in patches:
        level = []
        for p in range(2):
            live = jnp.int32(1 if place == p else 0)
            for j in range(listed.shape[1]):
                hit = jnp.logical_and(j < counts[0, p], listed[p, j] == windows[place])
                live = jnp.where(hit, 1, live)
            level.append(jnp.where(live == 1, 0.0, -1e30).astype(F32))
        bias[place : place + 1, :] = jnp.where(lane < PT, level[0], level[1])


def biased(scores, bias, first):
    count = scores.shape[0] // PT
    return jnp.concatenate(
        [scores[i * PT : (i + 1) * PT] + bias[first + i : first + i + 1, :] for i in range(count)], axis=0
    )


def key_side(patches, gain, wk, wv, xhat, ht, k_stack, kt, v_stack, vt):
    for i, tokens in enumerate(patches):
        normal, _ = unit_rows(tokens[...])
        at = slice(i * PT, (i + 1) * PT)
        xhat[at, :] = normal
        hidden = normal * gain[...]
        store(ht, pair_of(hidden.T), slice(None), at)
    hidden = pair_of(xhat[...] * gain[...])
    key = dot3(hidden, load(wk, ...))
    store_stacked(k_stack, 0, key)
    store(kt, pair_of(key.T), ...)
    value = dot3(hidden, load(wv, ...))
    store_stacked(v_stack, 0, value)
    store(vt, pair_of(value.T), ...)


def head_rows(h):
    return pl.ds(pl.multiple_of(h * HD, HD), HD)


def head_stack(h):
    return pl.ds(pl.multiple_of(h * 4 * HD, 4 * HD), 4 * HD)


def weighed(highs, lows, rows, right):
    high = jnp.concatenate([r[rows, :] for r in highs], axis=1)
    low = jnp.concatenate([r[rows, :] for r in lows], axis=1)
    both = dot(jnp.concatenate([high, low], axis=0), right[0])
    return both[:HD] + (both[HD:] + dot(high, right[1]))


def near_kernel(
    parity, listed, counts, patch_0, patch_1, gain, q_stack, k_stack, v_stack, vt_h, vt_l, d_stack,
    wk_h, wk_l, wv_h, wv_l,
    xhat, ht_h, ht_l, kt_h, kt_l, e_h, e_l, d_scores, mixed, tops, totals,
    bias, k_near, v_near, vt2_h, vt2_l,
):
    store_bias(bias, listed, counts, parity, range(4))
    key_side(
        (patch_0, patch_1), gain, (wk_h, wk_l), (wv_h, wv_l), xhat, (ht_h, ht_l), k_near, (kt_h, kt_l), v_near,
        (vt2_h, vt2_l),
    )

    def one_head(h, carry):
        stack, rows = head_stack(h), head_rows(h)
        q_now, d_now = q_stack[stack, :], d_stack[stack, :]
        scores = jnp.concatenate(
            [biased(dot(k_stack[:, stack], q_now), bias, 0), biased(dot(k_near[:, stack], q_now), bias, 2)], axis=0
        )
        top = jnp.max(scores, axis=0, keepdims=True)
        weights = jnp.exp(scores - top)
        tops[pl.ds(h, 1), :] = top
        totals[pl.ds(h, 1), :] = jnp.sum(weights, axis=0, keepdims=True)
        pair = pair_of(weights)
        e_h[h] = pair[0]
        e_l[h] = pair[1]
        mixed[rows, :] = weighed((vt_h, vt2_h), (vt_l, vt2_l), rows, pair)
        d_scores[h] = jnp.concatenate([dot(v_stack[:, stack], d_now), dot(v_near[:, stack], d_now)], axis=0)
        return carry

    lax.fori_loop(0, HEADS, one_head, 0, unroll=UNROLL)


def gathered(left_h, left_l, right):
    left_half = lax.broadcasted_iota(jnp.int32, right[0].shape, 1) < HD
    zero = jnp.zeros_like(right[0])
    one = [jnp.where(left_half, x, zero) for x in right]
    two = [jnp.where(left_half, zero, x) for x in right]
    wide = dot(left_h[0], jnp.concatenate(one, axis=1)) + dot(left_h[1], jnp.concatenate(two, axis=1))
    narrow = dot(left_l[0], one[0]) + dot(left_l[1], two[0])
    return wide[:, : 2 * HD] + (wide[:, 2 * HD :] + narrow)


def pair_lanes(p):
    return pl.ds(pl.multiple_of(p * 2 * HD, 2 * HD), 2 * HD)


def kept_and_sent(me, pair, keep, send):
    rows = pair[0].shape[0]

    @pl.when(me[0] % 2 == 0)
    def _():
        keep[:rows, :] = pair[0][...]
        send[:rows, :] = pair[1][...]

    @pl.when(me[0] % 2 == 1)
    def _():
        keep[:rows, :] = pair[1][...]
        send[:rows, :] = pair[0][...]


def far_kernel(
    parity, listed, counts, patch_0, patch_1, gain, q_t, q_stack, d_mixed_t, d_stack, mixed_1, tops, totals,
    wk_h, wk_l, wv_h, wv_l,
    xhat, ht_h, ht_l, kt_h, kt_l, u_h, u_l, mixed_t, deltas, shares, shares_1, dk_h, dk_l, dv_h, dv_l, d_far,
    bias, k_far, v_far, vt_h, vt_l, e_h, e_l,
):
    store_bias(bias, listed, counts, parity, range(4, 6))
    key_side(
        (patch_0, patch_1), gain, (wk_h, wk_l), (wv_h, wv_l), xhat, (ht_h, ht_l), k_far, (kt_h, kt_l), v_far,
        (vt_h, vt_l),
    )

    def one_pair(p, carry):
        d_scaled, q_scaled = [], []
        for a in range(2):
            h = 2 * p + a
            stack, rows, row = head_stack(h), head_rows(h), pl.ds(h, 1)
            scores = biased(dot(k_far[:, stack], q_stack[stack, :]), bias, 4)
            top_1 = tops[row, :]
            top = jnp.maximum(top_1, jnp.max(scores, axis=0, keepdims=True))
            weights = jnp.exp(scores - top)
            shrink = jnp.exp(top_1 - top)
            share = 1.0 / (shrink * totals[row, :] + jnp.sum(weights, axis=0, keepdims=True))
            share_1 = shrink * share
            pair = pair_of(weights)
            e_h[a] = pair[0]
            e_l[a] = pair[1]
            mixed = share_1 * mixed_1[rows, :] + share * weighed((vt_h,), (vt_l,), rows, pair)
            mixed_t[rows, :] = mixed
            d_mixed = d_mixed_t[rows, :]
            delta = jnp.sum(d_mixed * mixed, axis=0, keepdims=True)
            deltas[row, :] = delta
            shares[row, :] = share
            shares_1[row, :] = share_1
            pair = pair_of(weights * (dot(v_far[:, stack], d_stack[stack, :]) - delta))
            u_h[h] = pair[0]
            u_l[h] = pair[1]
            d_scaled.append(d_mixed * share)
            q_scaled.append(q_t[rows, :] * share)
        lanes = pair_lanes(p)
        right = pair_of(jnp.concatenate(d_scaled, axis=0).T)
        d_value = gathered((e_h[0], e_h[1]), (e_l[0], e_l[1]), right)
        store((dv_h, dv_l), pair_of(d_value), slice(None), lanes)
        right = pair_of(jnp.concatenate(q_scaled, axis=0).T)
        d_key = gathered((u_h[2 * p], u_h[2 * p + 1]), (u_l[2 * p], u_l[2 * p + 1]), right)
        store((dk_h, dk_l), pair_of(d_key), slice(None), lanes)
        return carry

    lax.fori_loop(0, PAIRS, one_pair, 0, unroll=UNROLL)
    d_far[...] = sums_of(
        [load((dk_h, dk_l), ...), load((dv_h, dv_l), ...)], [load((wk_h, wk_l), ...), load((wv_h, wv_l), ...)], NT
    )


def mix_kernel(
    me, mixed_t, e_h, e_l, d_mixed_t, shares_1, ht_h, ht_l, ht2_h, ht2_l, ht3_h, ht3_l, dv3_h, dv3_l, tokens, cot,
    wo_h, wo_l,
    result, keep, send, dv_h, dv_l,
    grad_o, grad_v,
):
    own = tokens.shape[0]

    def one_pair(p, carry):
        d_scaled = [
            d_mixed_t[head_rows(2 * p + a), :] * shares_1[pl.ds(2 * p + a, 1), :] for a in range(2)
        ]
        right = pair_of(jnp.concatenate(d_scaled, axis=0).T)
        d_value = gathered((e_h[2 * p], e_h[2 * p + 1]), (e_l[2 * p], e_l[2 * p + 1]), right)
        store((dv_h, dv_l), pair_of(d_value), slice(None), pair_lanes(p))
        return carry

    lax.fori_loop(0, PAIRS, one_pair, 0, unroll=UNROLL)
    mixed = mixed_t[...]
    grad_o[...] = dot3(pair_of(mixed), pair_of(cot[...]))
    turned = [load(t, ...) for t in ((ht_h, ht_l), (ht2_h, ht2_l), (ht3_h, ht3_l))]
    d_values = [load((dv_h, dv_l), slice(0, own)), load((dv_h, dv_l), slice(own, 2 * own)), load((dv3_h, dv3_l), ...)]
    grad_v[...] = sums_of(turned, d_values)
    kept_and_sent(me, (grad_o, grad_v), keep, send)
    result[...] = dot3(pair_of(mixed.T), load((wo_h, wo_l), ...)) + tokens[...]


def back_kernel(
    d_back, q_t, kt_h, kt_l, kt2_h, kt2_l, kt3_h, kt3_l, e_h, e_l, d_scores, u_h, u_l, deltas, shares, shares_1,
    dv_h, dv_l, wk_h, wk_l, wv_h, wv_l,
    d_near, dq_t, dk_h, dk_l,
    s_h, s_l,
):
    own = d_near.shape[0]

    def one_pair(p, carry):
        q_scaled = []
        for a in range(2):
            h = 2 * p + a
            rows, row = head_rows(h), pl.ds(h, 1)
            weights = e_h[h].astype(F32) + e_l[h].astype(F32)
            pair = pair_of(weights * (d_scores[h] - deltas[row, :]))
            s_h[a] = pair[0]
            s_l[a] = pair[1]
            share_1 = shares_1[row, :]
            one = weighed((kt_h, kt2_h), (kt_l, kt2_l), rows, pair)
            two = weighed((kt3_h,), (kt3_l,), rows, (u_h[h], u_l[h]))
            dq_t[rows, :] = (share_1 * one + shares[row, :] * two) * HD ** (-0.5)
            q_scaled.append(q_t[rows, :] * share_1)
        right = pair_of(jnp.concatenate(q_scaled, axis=0).T)
        d_key = gathered((s_h[0], s_h[1]), (s_l[0], s_l[1]), right)
        store((dk_h, dk_l), pair_of(d_key), slice(None), pair_lanes(p))
        return carry

    lax.fori_loop(0, PAIRS, one_pair, 0, unroll=UNROLL)
    near = slice(own, 2 * own)
    d_near[...] = d_back[...] + sums_of(
        [load((dk_h, dk_l), near), load((dv_h, dv_l), near)], [load((wk_h, wk_l), ...), load((wv_h, wv_l), ...)], NT
    )


def grad_kernel(
    me, d_back, ht_h, ht_l, ht2_h, ht2_l, ht3_h, ht3_l, xhat, xhat2, xhat3, dq_t, dk_h, dk_l, dk3_h, dk3_l, dv_h, dv_l,
    d_near, d_far, wq_h, wq_l, wk_h, wk_l, wv_h, wv_l,
    keep, send, d_own,
    grad_q, grad_k,
):
    own, width = d_own.shape
    first, second = slice(0, own), slice(own, 2 * own)
    d_query = pair_of(dq_t[...].T)
    turned = [load(t, ...) for t in ((ht_h, ht_l), (ht2_h, ht2_l), (ht3_h, ht3_l))]
    d_keys = [load((dk_h, dk_l), first), load((dk_h, dk_l), second), load((dk3_h, dk3_l), ...)]
    grad_q[...] = dot3(turned[0], d_query)
    grad_k[...] = sums_of(turned, d_keys)
    w_q, w_k, w_v = load((wq_h, wq_l), ...), load((wk_h, wk_l), ...), load((wv_h, wv_l), ...)
    d_own[...] = sums_of([d_query, d_keys[0], load((dv_h, dv_l), first)], [w_q, w_k, w_v], NT)
    d_gain = jnp.sum(
        d_own[...] * xhat[...] + (d_near[...] - d_back[...]) * xhat2[...] + d_far[...] * xhat3[...],
        axis=0, keepdims=True,
    )
    top = lax.broadcasted_iota(jnp.int32, (TAIL, width), 0) == 0
    for out in (keep, send):
        out[width:, :] = jnp.where(top, d_gain, 0.0)
    kept_and_sent(me, (grad_q, grad_k), keep, send)


TAIL = 8


def half_of(me, mask, mine, rows):
    index = (me[0] // mask) % 2
    return pl.ds(pl.multiple_of((index if mine else 1 - index) * rows, 8), rows)


def add_kernel(a, b, out):
    out[...] = a[...] + b[...]


def last_kernel(a, b, out, tail):
    rows = out.shape[0]
    out[...] = a[:rows, :] + b[:rows, :]
    tail[...] = a[rows : rows + 1, :] + b[rows : rows + 1, :]


def cut_kernel(masks, me, keep_1, other_1, keep_2, other_2, *outs):
    count = keep_1.shape[0]
    sums = outs[-1]
    sums[:count, :] = keep_1[...] + other_1[...]
    sums[count:, :] = keep_2[...] + other_2[...]
    tail = sums[2 * count :, :]
    at = 0
    for i, mask in enumerate(masks):
        keep, send = outs[2 * i], outs[2 * i + 1]
        rows = keep.shape[0] - (TAIL if i == 0 else 0)
        for out, mine in ((keep, True), (send, False)):
            index = (me[0] // mask) % 2
            start = at + (index if mine else 1 - index) * rows
            out[:rows, :] = sums[pl.ds(pl.multiple_of(start, 8), rows), :]
            if i == 0:
                out[rows:, :] = tail
        at += 2 * rows


def halve_kernel(mask, tail, me, keep, other, next_keep, next_send):
    rows = next_keep.shape[0] - tail
    for out, mine in ((next_keep, True), (next_send, False)):
        at = half_of(me, mask, mine, rows)
        out[:rows, :] = keep[at, :] + other[at, :]
        if tail:
            out[rows:, :] = keep[2 * rows :, :] + other[2 * rows :, :]


def join_kernel(mask, me, *refs):
    *ins, keep, send, d_tokens, sums = refs
    at = 0
    for i in range(3):
        rows = ins[2 * i].shape[0] - (TAIL if i == 0 else 0)
        sums[at : at + rows, :] = ins[2 * i][:rows, :] + ins[2 * i + 1][:rows, :]
        at += rows
    tail = ins[0][rows_of(ins[0]) :, :] + ins[1][rows_of(ins[0]) :, :]
    for out, mine in ((keep, True), (send, False)):
        out[: at // 2, :] = sums[half_of(me, mask, mine, at // 2), :]
        out[at // 2 :, :] = tail
    tokens_kernel(*ins[6:], d_tokens)


def rows_of(ref):
    return ref.shape[0] - TAIL


def part_kernel(mask, me, mine, other, *outs):
    *parts, whole = outs
    rows = mine.shape[0]
    whole[half_of(me, mask, True, rows), :] = mine[...]
    whole[half_of(me, mask, False, rows), :] = other[...]
    at = 0
    for out in parts:
        out[...] = whole[at : at + out.shape[0], :]
        at += out.shape[0]


def double_kernel(mask, me, mine, other, out):
    rows = mine.shape[0]
    out[half_of(me, mask, True, rows), :] = mine[...]
    out[half_of(me, mask, False, rows), :] = other[...]


def split_kernel(ranges, me, *refs):
    *ins, one, two = refs
    count = len(ins) // 2
    for bit in range(2):

        @pl.when(me[0] % 2 == bit)
        def _():
            for out, pieces in ((one, ins[:count] if bit == 0 else ins[count:]), (two, ins[count:] if bit == 0 else ins[:count])):
                at = 0
                for piece, (start, stop) in zip(pieces, ranges):
                    out[at : at + stop - start, :] = piece[start:stop, :]
                    at += stop - start


def tokens_kernel(tokens, gain, cot, d_own, d_other, out):
    normal, rstd = unit_rows(tokens[...])
    d_normal = (d_own[...] + d_other[...]) * gain[...]
    inner = jnp.mean(d_normal * normal, axis=1, keepdims=True)
    centre = jnp.mean(d_normal, axis=1, keepdims=True)
    out[...] = (d_normal - centre - normal * inner) * rstd + cot[...]


def shape(*dims, dtype=F32):
    return jax.ShapeDtypeStruct(dims, dtype)


def pairs(*dims):
    return [shape(*dims, dtype=BF16)] * 2


def call(kernel, inputs, outputs, scratch=(), scalars=0, limit=4, us=1):
    return pl.pallas_call(
        kernel,
        out_shape=outputs,
        in_specs=[SMEM] * scalars + [VMEM] * (len(inputs) - scalars),
        out_specs=[VMEM] * len(outputs),
        scratch_shapes=[pltpu.VMEM(s.shape, s.dtype) for s in scratch],
        compiler_params=pltpu.CompilerParams(vmem_limit_bytes=limit * 2**20),
        cost_estimate=pl.CostEstimate(flops=us * 10**9, bytes_accessed=0, transcendentals=0),
    )(*inputs)


def along_space(value, target):
    count = lax.axis_size("space")
    return lax.ppermute(value, "space", [(i, target(i) % count) for i in range(count)])


def across(value):
    return along_space(value, lambda i: i ^ 1)


def onward(value):
    return along_space(value, lambda i: i + 2 - 4 * (i % 2))


def homeward(value):
    return along_space(value, lambda i: i - 2 + 4 * (i % 2))


def devices():
    return lax.axis_size("space") * lax.axis_size("slab")


def swapped(value, mask):
    return lax.ppermute(value, ("space", "slab"), [(i, i ^ mask) for i in range(devices())])


ORDERS = ((4, 2, 8), (2, 8, 4), (8, 4, 2))
LAST = 16


def summed(me, keep_1, other_1, keep_2, send_2, token_side):
    count, width = keep_1.shape
    total = 2 * count
    unit = 8 * 8
    sizes = [total // unit // 3 * unit] * 2
    sizes.append(total - sum(sizes))
    tails = (TAIL, 0, 0)
    halves = [size // 2 for size in sizes]
    parts = call(
        functools.partial(cut_kernel, [order[0] for order in ORDERS]),
        (me, keep_1, other_1, keep_2, swapped(send_2, 1)),
        [shape(half + tail, width) for half, tail in zip(halves, tails) for _ in range(2)],
        [shape(total + TAIL, width)],
        scalars=1, limit=8,
    )
    parts = [[parts[2 * i], swapped(parts[2 * i + 1], ORDERS[i][0])] for i in range(3)]
    for step in (1, 2):
        for i in range(3):
            rows, mask = sizes[i] >> (step + 1), ORDERS[i][step]
            keep, send = call(
                functools.partial(halve_kernel, mask, tails[i]), (me, *parts[i]), [shape(rows + tails[i], width)] * 2,
                scalars=1,
            )
            parts[i] = [keep, swapped(send, mask)]
    joined = total // 8
    keep, send, *d_tokens = call(
        functools.partial(join_kernel, LAST), (me, *parts[0], *parts[1], *parts[2], *token_side),
        [shape(joined // 2 + TAIL, width)] * 2 + [token_side[0]], [shape(joined, width)], scalars=1, limit=8,
    )
    other = swapped(send, LAST)
    mask = 2 * LAST
    while mask < devices():
        (keep,) = call(add_kernel, (keep, other), [keep])
        other = swapped(keep, mask)
        mask *= 2
    mine, d_gain = call(last_kernel, (keep, other), [shape(joined // 2, width), shape(1, width)])
    parts = list(call(
        functools.partial(part_kernel, LAST), (me, mine, swapped(mine, LAST)),
        [shape(size // 8, width) for size in sizes], [shape(joined, width)], scalars=1,
    ))
    for step in (2, 1, 0):
        for i in range(3):
            mask = ORDERS[i][step]
            (parts[i],) = call(
                functools.partial(double_kernel, mask), (me, parts[i], swapped(parts[i], mask)),
                [shape(2 * parts[i].shape[0], width)], scalars=1,
            )
    others = [swapped(part, 1) for part in parts]
    split = count - sizes[0]
    first = call(
        functools.partial(split_kernel, [(0, sizes[0]), (0, split)]), (me, *parts[:2], *others[:2]),
        [shape(count, width)] * 2, scalars=1, limit=8,
    )
    second = call(
        functools.partial(split_kernel, [(split, sizes[1]), (0, sizes[2])]), (me, *parts[1:], *others[1:]),
        [shape(count, width)] * 2, scalars=1, limit=8,
    )
    return first, second, d_gain.reshape(width), d_tokens


def body(tokens, gain, wq, wk, wv, wo, neighbour_list, neighbour_count, cotangent):
    rows, width = tokens.shape
    me = (lax.axis_index("space") * lax.axis_size("slab") + lax.axis_index("slab")).astype(jnp.int32)[None]
    parity = (lax.axis_index("space") % 2).astype(jnp.int32)[None]
    counts = neighbour_count[None, :]
    near = [across(tokens[i * PT : (i + 1) * PT]) for i in range(2)]
    far = [onward(part) for part in near]
    gain_row = gain[None, :]
    stack_rows, stack_columns = shape(HEADS * 4 * HD, rows, dtype=BF16), shape(rows, HEADS * 4 * HD, dtype=BF16)
    turned, square, pair = pairs(width, rows), pairs(width, width), pairs(rows, width)
    whole, whole_t, scalars = shape(rows, width), shape(width, rows), shape(HEADS, rows)
    weights = call(weight_kernel, (me, parity, wq, wk, wv, wo), square * 4, scalars=2, limit=20, us=2)
    wq_h, wq_l, wk_h, wk_l, wv_h, wv_l, wo_h, wo_l = weights
    (
        xhat, ht_h, ht_l, q_t, q_stack, k_stack, v_stack, kt_h, kt_l, vt_h, vt_l, d_mixed_t, d_stack,
    ) = call(
        own_kernel,
        (near[0], tokens, gain_row, cotangent, *weights),
        [whole, *turned, whole_t, stack_rows, stack_columns, stack_columns, *turned, *turned, whole_t, stack_rows],
        limit=LIMITS[0], us=3,
    )
    w_k, w_v = (wk_h, wk_l), (wv_h, wv_l)
    xhat2, ht2_h, ht2_l, kt2_h, kt2_l, e_h, e_l, d_scores, mixed, tops, totals = call(
        near_kernel,
        (
            parity, neighbour_list, counts, *near, gain_row, q_stack, k_stack, v_stack, vt_h, vt_l, d_stack,
            *w_k, *w_v,
        ),
        [
            whole, *turned, *turned, *pairs(HEADS, 2 * rows, rows), shape(HEADS, 2 * rows, rows), whole_t, scalars,
            scalars,
        ],
        [shape(8, rows), stack_columns, stack_columns, *turned],
        scalars=3, limit=LIMITS[1], us=6,
    )
    (
        xhat3, ht3_h, ht3_l, kt3_h, kt3_l, u_h, u_l, mixed_t, deltas, shares, shares_1, dk3_h, dk3_l, dv3_h, dv3_l,
        d_far,
    ) = call(
        far_kernel,
        (
            parity, neighbour_list, counts, *far, gain_row, q_t, q_stack, d_mixed_t, d_stack, mixed, tops, totals,
            *w_k, *w_v,
        ),
        [
            whole, *turned, *turned, *pairs(HEADS, rows, rows), whole_t, scalars, scalars, scalars, *pair, *pair,
            whole,
        ],
        [shape(8, rows), stack_columns, stack_columns, *turned, *pairs(2, rows, rows)],
        scalars=3, limit=LIMITS[2], us=6,
    )
    d_back = homeward(d_far)
    result, keep_1, send_1, dv_h, dv_l = call(
        mix_kernel,
        (
            me, mixed_t, e_h, e_l, d_mixed_t, shares_1, ht_h, ht_l, ht2_h, ht2_l, ht3_h, ht3_l, dv3_h, dv3_l, tokens,
            cotangent, wo_h, wo_l,
        ),
        [whole, shape(width, width), shape(width, width), *pairs(2 * rows, width)],
        [shape(width, width), shape(width, width)],
        scalars=1, limit=LIMITS[3], us=5,
    )
    other_1 = swapped(send_1, 1)
    d_near, dq_t, dk_h, dk_l = call(
        back_kernel,
        (
            d_back, q_t, kt_h, kt_l, kt2_h, kt2_l, kt3_h, kt3_l, e_h, e_l, d_scores, u_h, u_l, deltas, shares, shares_1,
            dv_h, dv_l, *w_k, *w_v,
        ),
        [whole, whole_t, *pairs(2 * rows, width)],
        [*pairs(2, 2 * rows, rows)],
        limit=LIMITS[4], us=5,
    )
    d_other = across(d_near)
    tall = shape(width + TAIL, width)
    keep_2, send_2, d_own = call(
        grad_kernel,
        (
            me, d_back, ht_h, ht_l, ht2_h, ht2_l, ht3_h, ht3_l, xhat, xhat2, xhat3, dq_t, dk_h, dk_l, dk3_h, dk3_l,
            dv_h, dv_l, d_near, d_far, wq_h, wq_l, *w_k, *w_v,
        ),
        [tall, tall, whole],
        [shape(width, width), shape(width, width)],
        scalars=1, limit=LIMITS[5], us=4,
    )
    (grad_o, grad_v), (grad_q, grad_k), d_gain, (d_tokens,) = summed(
        me, keep_1, other_1, keep_2, send_2, (tokens, gain_row, cotangent, d_own, d_other)
    )
    return (result, d_tokens, d_gain, grad_q, grad_k, grad_v, grad_o)


UNROLL = False
LIMITS = (8, 8, 8, 8, 8, 8)


def solution(mesh):
    tokens = P(("space", "slab"), None)
    return jax.shard_map(
        body,
        mesh=mesh,
        in_specs=(tokens, P(), P(), P(), P(), P(), tokens, P(("space", "slab")), tokens),
        out_specs=(tokens, tokens, P(), P(), P(), P(), P()),
        check_vma=False,
    )
```

```python
import functools

import jax
import jax.numpy as jnp
from jax import lax
from jax.experimental import pallas as pl
from jax.experimental.pallas import tpu as pltpu
from jax.sharding import PartitionSpec as P

HEADS = 8
PT = 128
HD = 64
PAIRS = HEADS // 2
F32 = jnp.float32
BF16 = jnp.bfloat16
NN = (((1,), (0,)), ((), ()))
NT = (((1,), (1,)), ((), ()))
VMEM = pl.BlockSpec(memory_space=pltpu.VMEM)
SMEM = pl.BlockSpec(memory_space=pltpu.SMEM)


def pair_of(x):
    high = x.astype(BF16)
    return high, (x - high.astype(F32)).astype(BF16)


def dot(left, right, dims=NN):
    return lax.dot_general(left, right, dims, preferred_element_type=F32)


def dot3(left, right, dims=NN):
    return dot(left[0], right[0], dims) + (dot(left[0], right[1], dims) + dot(left[1], right[0], dims))


def load(refs, *index):
    return refs[0][index], refs[1][index]


def store(refs, pair, *index):
    refs[0][index] = pair[0]
    refs[1][index] = pair[1]


def unit_rows(tokens):
    centred = tokens - jnp.mean(tokens, axis=1, keepdims=True)
    variance = jnp.mean(centred * centred, axis=1, keepdims=True)
    rstd = lax.rsqrt(variance + 1e-05)
    return centred * rstd, rstd


def store_stacked(ref, row, rows):
    count = rows.shape[0]
    left_half = lax.broadcasted_iota(jnp.int32, (count, 2 * HD), 1) < HD
    for p in range(PAIRS):
        part = rows[:, p * 2 * HD : (p + 1) * 2 * HD]
        swapped = pltpu.roll(part, HD, 1)
        for a in range(2):
            both = jnp.where(left_half == (a == 0), part, swapped)
            high, low = pair_of(both)
            base = (2 * p + a) * 4 * HD
            ref[pl.ds(row, count), base : base + 2 * HD] = high
            ref[pl.ds(row, count), base + 2 * HD : base + 4 * HD] = low


def store_interleaved(ref, columns):
    high, low = pair_of(columns)
    for h in range(HEADS):
        for i, piece in enumerate((high, low, high, low)):
            at = h * 4 * HD + i * HD
            ref[at : at + HD, :] = piece[h * HD : (h + 1) * HD]


def sums_of(left, right, dims=NN):
    return sum(dot3(a, b, dims) for a, b in zip(left[1:], right[1:], strict=True)) + dot3(left[0], right[0], dims)


def weight_kernel(_me, _parity, wq, wk, wv, wo, wq_h, wq_l, wk_h, wk_l, wv_h, wv_l, wo_h, wo_l):
    for source, high, low in ((wq, wq_h, wq_l), (wk, wk_h, wk_l), (wv, wv_h, wv_l), (wo, wo_h, wo_l)):
        store((high, low), pair_of(source[...]), ...)


def own_kernel(
    _, tokens, gain, cot, wq_h, wq_l, wk_h, wk_l, wv_h, wv_l, wo_h, wo_l,
    xhat, ht_h, ht_l, q_t, q_stack, k_stack, v_stack, kt_h, kt_l, vt_h, vt_l, d_mixed_t, d_stack,
):
    normal, _ = unit_rows(tokens[...])
    xhat[...] = normal
    hidden = normal * gain[...]
    store((ht_h, ht_l), pair_of(hidden.T), ...)
    rows = pair_of(hidden)
    query = dot3(rows, load((wq_h, wq_l), ...)) * HD ** (-0.5)
    q_t[...] = query.T
    store_interleaved(q_stack, q_t[...])
    key = dot3(rows, load((wk_h, wk_l), ...))
    store_stacked(k_stack, 0, key)
    store((kt_h, kt_l), pair_of(key.T), ...)
    value = dot3(rows, load((wv_h, wv_l), ...))
    store_stacked(v_stack, 0, value)
    store((vt_h, vt_l), pair_of(value.T), ...)
    d_mixed = dot3(load((wo_h, wo_l), ...), pair_of(cot[...]), NT)
    d_mixed_t[...] = d_mixed
    store_interleaved(d_stack, d_mixed)


def store_bias(bias, listed, counts, parity, patches):
    queries = bias.shape[1]
    lane = lax.broadcasted_iota(jnp.int32, (1, queries), 1)
    near = jnp.where(parity[0] == 0, 4, 0)
    windows = (2, 3, near, near + 1, 4 - near, 5 - near)
    for place in patches:
        level = []
        for p in range(2):
            live = jnp.int32(1 if place == p else 0)
            for j in range(listed.shape[1]):
                hit = jnp.logical_and(j < counts[0, p], listed[p, j] == windows[place])
                live = jnp.where(hit, 1, live)
            level.append(jnp.where(live == 1, 0.0, -1e30).astype(F32))
        bias[place : place + 1, :] = jnp.where(lane < PT, level[0], level[1])


def biased(scores, bias, first):
    count = scores.shape[0] // PT
    return jnp.concatenate(
        [scores[i * PT : (i + 1) * PT] + bias[first + i : first + i + 1, :] for i in range(count)], axis=0
    )


def key_side(patches, gain, wk, wv, xhat, ht, k_stack, kt, v_stack, vt):
    for i, tokens in enumerate(patches):
        normal, _ = unit_rows(tokens[...])
        at = slice(i * PT, (i + 1) * PT)
        xhat[at, :] = normal
        hidden = normal * gain[...]
        store(ht, pair_of(hidden.T), slice(None), at)
    hidden = pair_of(xhat[...] * gain[...])
    key = dot3(hidden, load(wk, ...))
    store_stacked(k_stack, 0, key)
    store(kt, pair_of(key.T), ...)
    value = dot3(hidden, load(wv, ...))
    store_stacked(v_stack, 0, value)
    store(vt, pair_of(value.T), ...)


def head_rows(h):
    return pl.ds(pl.multiple_of(h * HD, HD), HD)


def head_stack(h):
    return pl.ds(pl.multiple_of(h * 4 * HD, 4 * HD), 4 * HD)


def weighed(highs, lows, rows, right):
    high = jnp.concatenate([r[rows, :] for r in highs], axis=1)
    low = jnp.concatenate([r[rows, :] for r in lows], axis=1)
    both = dot(jnp.concatenate([high, low], axis=0), right[0])
    return both[:HD] + (both[HD:] + dot(high, right[1]))


def near_side_kernel(
    patch_0, patch_1, gain, wk_h, wk_l, wv_h, wv_l,
    xhat, ht_h, ht_l, kt_h, kt_l, k_stack, v_stack, vt_h, vt_l,
):
    key_side(
        (patch_0, patch_1), gain, (wk_h, wk_l), (wv_h, wv_l), xhat, (ht_h, ht_l), k_stack, (kt_h, kt_l), v_stack,
        (vt_h, vt_l),
    )


def near_kernel(
    parity, listed, counts, _, q_stack, k_stack, v_stack, vt_h, vt_l, d_stack, k_near, v_near, vt2_h, vt2_l,
    e_h, e_l, d_scores, mixed, tops, totals,
    bias,
):
    store_bias(bias, listed, counts, parity, range(4))

    def one_head(h, carry):
        stack, rows = head_stack(h), head_rows(h)
        q_now, d_now = q_stack[stack, :], d_stack[stack, :]
        scores = jnp.concatenate(
            [biased(dot(k_stack[:, stack], q_now), bias, 0), biased(dot(k_near[:, stack], q_now), bias, 2)], axis=0
        )
        top = jnp.max(scores, axis=0, keepdims=True)
        weights = jnp.exp(scores - top)
        tops[pl.ds(h, 1), :] = top
        totals[pl.ds(h, 1), :] = jnp.sum(weights, axis=0, keepdims=True)
        pair = pair_of(weights)
        e_h[h] = pair[0]
        e_l[h] = pair[1]
        mixed[rows, :] = weighed((vt_h, vt2_h), (vt_l, vt2_l), rows, pair)
        d_scores[h] = jnp.concatenate([dot(v_stack[:, stack], d_now), dot(v_near[:, stack], d_now)], axis=0)
        return carry

    lax.fori_loop(0, HEADS, one_head, 0, unroll=UNROLL)


def gathered(left_h, left_l, right):
    left_half = lax.broadcasted_iota(jnp.int32, right[0].shape, 1) < HD
    zero = jnp.zeros_like(right[0])
    one = [jnp.where(left_half, x, zero) for x in right]
    two = [jnp.where(left_half, zero, x) for x in right]
    wide = dot(left_h[0], jnp.concatenate(one, axis=1)) + dot(left_h[1], jnp.concatenate(two, axis=1))
    narrow = dot(left_l[0], one[0]) + dot(left_l[1], two[0])
    return wide[:, : 2 * HD] + (wide[:, 2 * HD :] + narrow)


def pair_lanes(p):
    return pl.ds(pl.multiple_of(p * 2 * HD, 2 * HD), 2 * HD)


def kept_and_sent(me, pair, keep, send):
    rows = pair[0].shape[0]

    @pl.when(me[0] % 2 == 0)
    def _():
        keep[:rows, :] = pair[0][...]
        send[:rows, :] = pair[1][...]

    @pl.when(me[0] % 2 == 1)
    def _():
        keep[:rows, :] = pair[1][...]
        send[:rows, :] = pair[0][...]


def far_kernel(
    parity, listed, counts, patch_0, patch_1, gain, q_t, q_stack, d_mixed_t, d_stack, mixed_1, tops, totals,
    wk_h, wk_l, wv_h, wv_l,
    xhat, ht_h, ht_l, kt_h, kt_l, u_h, u_l, mixed_t, deltas, shares, shares_1, dk_h, dk_l, dv_h, dv_l, d_far,
    bias, k_far, v_far, vt_h, vt_l, e_h, e_l,
):
    store_bias(bias, listed, counts, parity, range(4, 6))
    key_side(
        (patch_0, patch_1), gain, (wk_h, wk_l), (wv_h, wv_l), xhat, (ht_h, ht_l), k_far, (kt_h, kt_l), v_far,
        (vt_h, vt_l),
    )

    def one_pair(p, carry):
        d_scaled, q_scaled = [], []
        for a in range(2):
            h = 2 * p + a
            stack, rows, row = head_stack(h), head_rows(h), pl.ds(h, 1)
            scores = biased(dot(k_far[:, stack], q_stack[stack, :]), bias, 4)
            top_1 = tops[row, :]
            top = jnp.maximum(top_1, jnp.max(scores, axis=0, keepdims=True))
            weights = jnp.exp(scores - top)
            shrink = jnp.exp(top_1 - top)
            share = 1.0 / (shrink * totals[row, :] + jnp.sum(weights, axis=0, keepdims=True))
            share_1 = shrink * share
            pair = pair_of(weights)
            e_h[a] = pair[0]
            e_l[a] = pair[1]
            mixed = share_1 * mixed_1[rows, :] + share * weighed((vt_h,), (vt_l,), rows, pair)
            mixed_t[rows, :] = mixed
            d_mixed = d_mixed_t[rows, :]
            delta = jnp.sum(d_mixed * mixed, axis=0, keepdims=True)
            deltas[row, :] = delta
            shares[row, :] = share
            shares_1[row, :] = share_1
            pair = pair_of(weights * (dot(v_far[:, stack], d_stack[stack, :]) - delta))
            u_h[h] = pair[0]
            u_l[h] = pair[1]
            d_scaled.append(d_mixed * share)
            q_scaled.append(q_t[rows, :] * share)
        lanes = pair_lanes(p)
        right = pair_of(jnp.concatenate(d_scaled, axis=0).T)
        d_value = gathered((e_h[0], e_h[1]), (e_l[0], e_l[1]), right)
        store((dv_h, dv_l), pair_of(d_value), slice(None), lanes)
        right = pair_of(jnp.concatenate(q_scaled, axis=0).T)
        d_key = gathered((u_h[2 * p], u_h[2 * p + 1]), (u_l[2 * p], u_l[2 * p + 1]), right)
        store((dk_h, dk_l), pair_of(d_key), slice(None), lanes)
        return carry

    lax.fori_loop(0, PAIRS, one_pair, 0, unroll=UNROLL)
    d_far[...] = sums_of(
        [load((dk_h, dk_l), ...), load((dv_h, dv_l), ...)], [load((wk_h, wk_l), ...), load((wv_h, wv_l), ...)], NT
    )


def back_kernel(
    q_t, d_mixed_t, kt_h, kt_l, kt2_h, kt2_l, kt3_h, kt3_l, e_h, e_l, d_scores, u_h, u_l, deltas, shares, shares_1,
    wk_h, wk_l, wv_h, wv_l,
    d_near, dq_t, dk_h, dk_l, dv_h, dv_l,
    s_h, s_l,
):
    own = d_near.shape[0]

    def one_pair(p, carry):
        q_scaled, d_scaled = [], []
        for a in range(2):
            h = 2 * p + a
            rows, row = head_rows(h), pl.ds(h, 1)
            weights = e_h[h].astype(F32) + e_l[h].astype(F32)
            pair = pair_of(weights * (d_scores[h] - deltas[row, :]))
            s_h[a] = pair[0]
            s_l[a] = pair[1]
            share_1 = shares_1[row, :]
            one = weighed((kt_h, kt2_h), (kt_l, kt2_l), rows, pair)
            two = weighed((kt3_h,), (kt3_l,), rows, (u_h[h], u_l[h]))
            dq_t[rows, :] = (share_1 * one + shares[row, :] * two) * HD ** (-0.5)
            q_scaled.append(q_t[rows, :] * share_1)
            d_scaled.append(d_mixed_t[rows, :] * share_1)
        lanes = pair_lanes(p)
        right = pair_of(jnp.concatenate(q_scaled, axis=0).T)
        d_key = gathered((s_h[0], s_h[1]), (s_l[0], s_l[1]), right)
        store((dk_h, dk_l), pair_of(d_key), slice(None), lanes)
        right = pair_of(jnp.concatenate(d_scaled, axis=0).T)
        d_value = gathered((e_h[2 * p], e_h[2 * p + 1]), (e_l[2 * p], e_l[2 * p + 1]), right)
        store((dv_h, dv_l), pair_of(d_value), slice(None), lanes)
        return carry

    lax.fori_loop(0, PAIRS, one_pair, 0, unroll=UNROLL)
    near = slice(own, 2 * own)
    d_near[...] = sums_of(
        [load((dk_h, dk_l), near), load((dv_h, dv_l), near)], [load((wk_h, wk_l), ...), load((wv_h, wv_l), ...)], NT
    )


def mix_kernel(
    me, mixed_t, ht_h, ht_l, ht2_h, ht2_l, ht3_h, ht3_l, dv_h, dv_l, dv3_h, dv3_l, cot,
    keep, send,
    grad_o, grad_v,
):
    own = cot.shape[0]
    grad_o[...] = dot3(pair_of(mixed_t[...]), pair_of(cot[...]))
    turned = [load(t, ...) for t in ((ht_h, ht_l), (ht2_h, ht2_l), (ht3_h, ht3_l))]
    d_values = [load((dv_h, dv_l), slice(0, own)), load((dv_h, dv_l), slice(own, 2 * own)), load((dv3_h, dv3_l), ...)]
    grad_v[...] = sums_of(turned, d_values)
    kept_and_sent(me, (grad_o, grad_v), keep, send)


def result_kernel(_, mixed_t, tokens, wo_h, wo_l, result, mark):
    mark[...] = jnp.zeros_like(mark)
    result[...] = dot3(pair_of(mixed_t[...].T), load((wo_h, wo_l), ...)) + tokens[...]


def grad_kernel(
    ht_h, ht_l, ht2_h, ht2_l, ht3_h, ht3_l, xhat, xhat2, xhat3, dq_t, dk_h, dk_l, dk3_h, dk3_l, dv_h, dv_l,
    d_near, d_far, wq_h, wq_l, wk_h, wk_l, wv_h, wv_l,
    grad_q, grad_k, d_own, gain_sum,
):
    own, width = d_own.shape
    first, second = slice(0, own), slice(own, 2 * own)
    d_query = pair_of(dq_t[...].T)
    turned = [load(t, ...) for t in ((ht_h, ht_l), (ht2_h, ht2_l), (ht3_h, ht3_l))]
    d_keys = [load((dk_h, dk_l), first), load((dk_h, dk_l), second), load((dk3_h, dk3_l), ...)]
    grad_q[...] = dot3(turned[0], d_query)
    grad_k[...] = sums_of(turned, d_keys)
    w_q, w_k, w_v = load((wq_h, wq_l), ...), load((wk_h, wk_l), ...), load((wv_h, wv_l), ...)
    d_own[...] = sums_of([d_query, d_keys[0], load((dv_h, dv_l), first)], [w_q, w_k, w_v], NT)
    gain_sum[...] = jnp.sum(
        d_own[...] * xhat[...] + d_near[...] * xhat2[...] + d_far[...] * xhat3[...], axis=0, keepdims=True
    )


def core_kernel(me, grad_q, grad_k, gain_sum, d_near, d_back, _, keep, send, d_given):
    d_given[...] = d_near[...] + d_back[...]
    width = grad_q.shape[1]
    top = lax.broadcasted_iota(jnp.int32, (TAIL, width), 0) == 0
    for out in (keep, send):
        out[width:, :] = jnp.where(top, gain_sum[...], 0.0)
    kept_and_sent(me, (grad_q, grad_k), keep, send)


TAIL = 8


def half_of(me, mask, mine, rows):
    index = (me[0] // mask) % 2
    return pl.ds(pl.multiple_of((index if mine else 1 - index) * rows, 8), rows)


def add_kernel(a, b, out):
    out[...] = a[...] + b[...]


def cut_kernel(masks, me, keep_1, other_1, keep_2, other_2, *outs):
    count = keep_1.shape[0]
    *outs, sums = outs
    sums[:count, :] = keep_1[...] + other_1[...]
    sums[count:, :] = keep_2[...] + other_2[...]
    tail = sums[2 * count :, :]
    at = 0
    for i, mask in enumerate(masks):
        keep, send = outs[2 * i], outs[2 * i + 1]
        rows = keep.shape[0] - (TAIL if i == 0 else 0)
        for out, mine in ((keep, True), (send, False)):
            index = (me[0] // mask) % 2
            start = at + (index if mine else 1 - index) * rows
            out[:rows, :] = sums[pl.ds(pl.multiple_of(start, 8), rows), :]
            if i == 0:
                out[rows:, :] = tail
        at += 2 * rows


def halve_kernel(mask, tail, me, keep, other, next_keep, next_send):
    rows = next_keep.shape[0] - tail
    for out, mine in ((next_keep, True), (next_send, False)):
        at = half_of(me, mask, mine, rows)
        out[:rows, :] = keep[at, :] + other[at, :]
        if tail:
            out[rows:, :] = keep[2 * rows :, :] + other[2 * rows :, :]


def join_kernel(*refs):
    *ins, d_given, sums, d_going = refs
    at = 0
    for i in range(3):
        rows = ins[2 * i].shape[0] - (TAIL if i == 0 else 0)
        sums[at : at + rows, :] = ins[2 * i][:rows, :] + ins[2 * i + 1][:rows, :]
        at += rows
    sums[at:, :] = ins[0][rows_of(ins[0]) :, :] + ins[1][rows_of(ins[0]) :, :]
    d_going[...] = d_given[...]


def rows_of(ref):
    return ref.shape[0] - TAIL


def part_kernel(a, b, _mark, _other, *outs):
    at = 0
    for out in outs:
        rows = out.shape[0]
        out[...] = a[at : at + rows, :] + b[at : at + rows, :]
        at += rows


def double_kernel(mask, me, mine, other, *rest):
    out = rest[-1]
    rows = mine.shape[0]
    out[half_of(me, mask, True, rows), :] = mine[...]
    out[half_of(me, mask, False, rows), :] = other[...]


def split_kernel(ranges, me, *refs):
    count = len(refs) - 5
    ins, outs, sent = refs[:count], refs[count:-1], refs[-1]
    for bit in range(2):

        @pl.when(me[0] % 2 == bit)
        def _():
            copies = []
            for core in range(2):
                for part, first, rows, exchange, to in ranges:
                    source = ins[part + core * (count // 2)].at[pl.ds(first, rows)]
                    target = outs[2 * exchange + (bit + core) % 2].at[pl.ds(to, rows)]
                    copies.append(pltpu.make_async_copy(source, target, sent.at[len(copies)]))
            for copy in copies:
                copy.start()
            for copy in copies:
                copy.wait()


def tokens_kernel(_, tokens, gain, cot, d_own, d_other, out, mark):
    mark[...] = jnp.zeros_like(mark)
    normal, rstd = unit_rows(tokens[...])
    d_normal = (d_own[...] + d_other[...]) * gain[...]
    inner = jnp.mean(d_normal * normal, axis=1, keepdims=True)
    centre = jnp.mean(d_normal, axis=1, keepdims=True)
    out[...] = (d_normal - centre - normal * inner) * rstd + cot[...]


def shape(*dims, dtype=F32):
    return jax.ShapeDtypeStruct(dims, dtype)


def pairs(*dims):
    return [shape(*dims, dtype=BF16)] * 2


def call(kernel, inputs, outputs, scratch=(), scalars=0, limit=4, us=1):
    return pl.pallas_call(
        kernel,
        out_shape=outputs,
        in_specs=[SMEM] * scalars + [VMEM] * (len(inputs) - scalars),
        out_specs=[VMEM] * len(outputs),
        scratch_shapes=[pltpu.VMEM(s.shape, s.dtype) for s in scratch],
        compiler_params=pltpu.CompilerParams(vmem_limit_bytes=limit * 2**20),
        cost_estimate=pl.CostEstimate(flops=us * 10**9, bytes_accessed=0, transcendentals=0),
    )(*inputs)


MARK = shape(8, 128)


def along_space(value, target):
    count = lax.axis_size("space")
    return lax.ppermute(value, "space", [(i, target(i) % count) for i in range(count)])


def across(value):
    return along_space(value, lambda i: i ^ 1)


def onward(value):
    return along_space(value, lambda i: i + 2 - 4 * (i % 2))


def homeward(value):
    return along_space(value, lambda i: i - 2 + 4 * (i % 2))


def devices():
    return lax.axis_size("space") * lax.axis_size("slab")


def swapped(value, mask):
    return lax.ppermute(value, ("space", "slab"), [(i, i ^ mask) for i in range(devices())])


ORDERS = ((4, 2, 8), (2, 8, 4), (8, 4, 2))
LAST = 16


def summed(me, keep_1, other_1, keep_2, send_2, d_given, token_side, result_of):
    count, width = keep_1.shape
    total = 2 * count
    unit = 8 * 8
    sizes = [total // unit // 3 * unit] * 2
    sizes.append(total - sum(sizes))
    tails = (TAIL, 0, 0)
    halves = [size // 2 for size in sizes]
    parts = call(
        functools.partial(cut_kernel, [order[0] for order in ORDERS]),
        (me, keep_1, other_1, keep_2, swapped(send_2, 1)),
        [shape(half + tail, width) for half, tail in zip(halves, tails) for _ in range(2)],
        [shape(total + TAIL, width)],
        scalars=1, limit=8,
    )
    parts = [[parts[2 * i], swapped(parts[2 * i + 1], ORDERS[i][0])] for i in range(3)]
    for step in (1, 2):
        for i in range(3):
            rows, mask = sizes[i] >> (step + 1), ORDERS[i][step]
            keep, send = call(
                functools.partial(halve_kernel, mask, tails[i]), (me, *parts[i]), [shape(rows + tails[i], width)] * 2,
                scalars=1,
            )
            parts[i] = [keep, swapped(send, mask)]
    joined = total // 8
    sums, d_going = call(
        join_kernel, (*parts[0], *parts[1], *parts[2], d_given), [shape(joined + TAIL, width), d_given],
        limit=8,
    )
    other = swapped(sums, LAST)
    result, mark = result_of(sums)
    d_other = across(d_going)
    mask = 2 * LAST
    while mask < devices():
        (sums,) = call(add_kernel, (sums, other), [sums])
        other = swapped(sums, mask)
        mask *= 2
    *parts, d_gain = call(
        part_kernel, (sums, other, mark, d_other), [shape(size // 8, width) for size in sizes] + [shape(1, width)],
    )
    for step in (2, 1, 0):
        for i in range(3):
            mask = ORDERS[i][step]
            place = (mark,) if step == 0 and i == 2 else ()
            (parts[i],) = call(
                functools.partial(double_kernel, mask), (me, parts[i], swapped(parts[i], mask), *place),
                [shape(2 * parts[i].shape[0], width)], scalars=1,
            )
        if step == 1:
            d_tokens, mark = call(tokens_kernel, (parts[0], *token_side, d_other), [d_given, MARK])
    others = [swapped(part, 1) for part in parts]
    ranges, at = [], 0
    for i, size in enumerate(sizes):
        for exchange in range(2):
            start, stop = max(at, exchange * count), min(at + size, (exchange + 1) * count)
            if start < stop:
                ranges.append((i, start - at, stop - start, exchange, start - exchange * count))
        at += size
    outputs = pl.pallas_call(
        functools.partial(split_kernel, ranges),
        out_shape=[shape(count, width)] * 4,
        in_specs=[SMEM] + [VMEM] * 6,
        out_specs=[pl.BlockSpec(memory_space=pl.ANY)] * 4,
        scratch_shapes=[pltpu.SemaphoreType.DMA((2 * len(ranges),))],
        compiler_params=pltpu.CompilerParams(vmem_limit_bytes=2**23),
    )(me, *parts, *others)
    first, second = outputs[:2], outputs[2:]
    return first, second, d_gain.reshape(width), d_tokens, result


def body(tokens, gain, wq, wk, wv, wo, neighbour_list, neighbour_count, cotangent):
    rows, width = tokens.shape
    me = (lax.axis_index("space") * lax.axis_size("slab") + lax.axis_index("slab")).astype(jnp.int32)[None]
    parity = (lax.axis_index("space") % 2).astype(jnp.int32)[None]
    counts = neighbour_count[None, :]
    near = [across(tokens[i * PT : (i + 1) * PT]) for i in range(2)]
    far = [onward(near[0])]
    gain_row = gain[None, :]
    stack_rows, stack_columns = shape(HEADS * 4 * HD, rows, dtype=BF16), shape(rows, HEADS * 4 * HD, dtype=BF16)
    turned, square, pair = pairs(width, rows), pairs(width, width), pairs(rows, width)
    whole, whole_t, scalars = shape(rows, width), shape(width, rows), shape(HEADS, rows)
    weights = call(weight_kernel, (me, parity, wq, wk, wv, wo), square * 4, scalars=2, limit=20)
    wq_h, wq_l, wk_h, wk_l, wv_h, wv_l, wo_h, wo_l = weights
    (
        xhat, ht_h, ht_l, q_t, q_stack, k_stack, v_stack, kt_h, kt_l, vt_h, vt_l, d_mixed_t, d_stack,
    ) = call(
        own_kernel,
        (near[0], tokens, gain_row, cotangent, *weights),
        [whole, *turned, whole_t, stack_rows, stack_columns, stack_columns, *turned, *turned, whole_t, stack_rows],
        limit=LIMITS[0], us=1,
    )
    near[1], q_stack = lax.optimization_barrier((near[1], q_stack))
    far.append(onward(near[1]))
    w_k, w_v = (wk_h, wk_l), (wv_h, wv_l)
    xhat2, ht2_h, ht2_l, kt2_h, kt2_l, k_near, v_near, vt2_h, vt2_l = call(
        near_side_kernel,
        (*near, gain_row, *w_k, *w_v),
        [whole, *turned, *turned, stack_columns, stack_columns, *turned],
        limit=LIMITS[1], us=1,
    )
    e_h, e_l, d_scores, mixed, tops, totals = call(
        near_kernel,
        (
            parity, neighbour_list, counts, far[0], q_stack, k_stack, v_stack, vt_h, vt_l, d_stack, k_near, v_near,
            vt2_h, vt2_l,
        ),
        [*pairs(HEADS, 2 * rows, rows), shape(HEADS, 2 * rows, rows), whole_t, scalars, scalars],
        [shape(8, rows)],
        scalars=3, limit=LIMITS[1], us=1,
    )
    (
        xhat3, ht3_h, ht3_l, kt3_h, kt3_l, u_h, u_l, mixed_t, deltas, shares, shares_1, dk3_h, dk3_l, dv3_h, dv3_l,
        d_far,
    ) = call(
        far_kernel,
        (
            parity, neighbour_list, counts, *far, gain_row, q_t, q_stack, d_mixed_t, d_stack, mixed, tops, totals,
            *w_k, *w_v,
        ),
        [
            whole, *turned, *turned, *pairs(HEADS, rows, rows), whole_t, scalars, scalars, scalars, *pair, *pair,
            whole,
        ],
        [shape(8, rows), stack_columns, stack_columns, *turned, *pairs(2, rows, rows)],
        scalars=3, limit=LIMITS[2], us=1,
    )
    d_back = homeward(d_far)
    d_near, dq_t, dk_h, dk_l, dv_h, dv_l = call(
        back_kernel,
        (
            q_t, d_mixed_t, kt_h, kt_l, kt2_h, kt2_l, kt3_h, kt3_l, e_h, e_l, d_scores, u_h, u_l, deltas, shares,
            shares_1, *w_k, *w_v,
        ),
        [whole, whole_t, *pairs(2 * rows, width), *pairs(2 * rows, width)],
        [*pairs(2, 2 * rows, rows)],
        limit=LIMITS[4], us=1,
    )
    keep_1, send_1 = call(
        mix_kernel,
        (me, mixed_t, ht_h, ht_l, ht2_h, ht2_l, ht3_h, ht3_l, dv_h, dv_l, dv3_h, dv3_l, cotangent),
        [shape(width, width), shape(width, width)],
        [shape(width, width), shape(width, width)],
        scalars=1, limit=LIMITS[3], us=1,
    )
    other_1 = swapped(send_1, 1)
    tall = shape(width + TAIL, width)
    grad_q, grad_k, d_own, gain_sum = call(
        grad_kernel,
        (
            ht_h, ht_l, ht2_h, ht2_l, ht3_h, ht3_l, xhat, xhat2, xhat3, dq_t, dk_h, dk_l, dk3_h, dk3_l,
            dv_h, dv_l, d_near, d_far, wq_h, wq_l, *w_k, *w_v,
        ),
        [shape(width, width), shape(width, width), whole, shape(1, width)],
        limit=LIMITS[5], us=1,
    )
    keep_2, send_2, d_given = call(
        core_kernel, (me, grad_q, grad_k, gain_sum, d_near, d_back, keep_1), [tall, tall, whole], scalars=1, limit=8
    )

    def result_of(place):
        return call(result_kernel, (place, mixed_t, tokens, wo_h, wo_l), [whole, MARK], limit=LIMITS[3], us=1)

    (grad_o, grad_v), (grad_q, grad_k), d_gain, d_tokens, result = summed(
        me, keep_1, other_1, keep_2, send_2, d_given, (tokens, gain_row, cotangent, d_own), result_of
    )
    return (result, d_tokens, d_gain, grad_q, grad_k, grad_v, grad_o)


UNROLL = True
LIMITS = (8, 8, 8, 8, 8, 8)


def solution(mesh):
    tokens = P(("space", "slab"), None)
    return jax.shard_map(
        body,
        mesh=mesh,
        in_specs=(tokens, P(), P(), P(), P(), P(), tokens, P(("space", "slab")), tokens),
        out_specs=(tokens, tokens, P(), P(), P(), P(), P()),
        check_vma=False,
    )
```

```python
import functools

import jax
import jax.numpy as jnp
from jax import lax
from jax.experimental import pallas as pl
from jax.experimental.pallas import tpu as pltpu
from jax.sharding import PartitionSpec as P

HEADS = 8
PT = 128
HD = 64
PAIRS = HEADS // 2
F32 = jnp.float32
BF16 = jnp.bfloat16
NN = (((1,), (0,)), ((), ()))
NT = (((1,), (1,)), ((), ()))
VMEM = pl.BlockSpec(memory_space=pltpu.VMEM)
SMEM = pl.BlockSpec(memory_space=pltpu.SMEM)


def pair_of(x):
    high = x.astype(BF16)
    return high, (x - high.astype(F32)).astype(BF16)


def dot(left, right, dims=NN):
    return lax.dot_general(left, right, dims, preferred_element_type=F32)


def dot3(left, right, dims=NN):
    return dot(left[0], right[0], dims) + (dot(left[0], right[1], dims) + dot(left[1], right[0], dims))


def load(refs, *index):
    return refs[0][index], refs[1][index]


def store(refs, pair, *index):
    refs[0][index] = pair[0]
    refs[1][index] = pair[1]


def unit_rows(tokens):
    centred = tokens - jnp.mean(tokens, axis=1, keepdims=True)
    variance = jnp.mean(centred * centred, axis=1, keepdims=True)
    rstd = lax.rsqrt(variance + 1e-05)
    return centred * rstd, rstd


def store_stacked(ref, row, rows):
    count = rows.shape[0]
    left_half = lax.broadcasted_iota(jnp.int32, (count, 2 * HD), 1) < HD
    for p in range(PAIRS):
        part = rows[:, p * 2 * HD : (p + 1) * 2 * HD]
        swapped = pltpu.roll(part, HD, 1)
        for a in range(2):
            both = jnp.where(left_half == (a == 0), part, swapped)
            high, low = pair_of(both)
            base = (2 * p + a) * 4 * HD
            ref[pl.ds(row, count), base : base + 2 * HD] = high
            ref[pl.ds(row, count), base + 2 * HD : base + 4 * HD] = low


def store_interleaved(ref, columns):
    high, low = pair_of(columns)
    for h in range(HEADS):
        for i, piece in enumerate((high, low, high, low)):
            at = h * 4 * HD + i * HD
            ref[at : at + HD, :] = piece[h * HD : (h + 1) * HD]


def sums_of(left, right, dims=NN):
    return sum(dot3(a, b, dims) for a, b in zip(left[1:], right[1:], strict=True)) + dot3(left[0], right[0], dims)


def weight_kernel(_me, _parity, wq, wk, wv, wo, wq_h, wq_l, wk_h, wk_l, wv_h, wv_l, wo_h, wo_l):
    for source, high, low in ((wq, wq_h, wq_l), (wk, wk_h, wk_l), (wv, wv_h, wv_l), (wo, wo_h, wo_l)):
        store((high, low), pair_of(source[...]), ...)


def own_kernel(
    _, tokens, gain, cot, wq_h, wq_l, wk_h, wk_l, wv_h, wv_l, wo_h, wo_l,
    xhat, ht_h, ht_l, q_t, q_stack, k_stack, v_stack, kt_h, kt_l, vt_h, vt_l, d_mixed_t, d_stack,
):
    normal, _ = unit_rows(tokens[...])
    xhat[...] = normal
    hidden = normal * gain[...]
    store((ht_h, ht_l), pair_of(hidden.T), ...)
    rows = pair_of(hidden)
    query = dot3(rows, load((wq_h, wq_l), ...)) * HD ** (-0.5)
    q_t[...] = query.T
    store_interleaved(q_stack, q_t[...])
    key = dot3(rows, load((wk_h, wk_l), ...))
    store_stacked(k_stack, 0, key)
    store((kt_h, kt_l), pair_of(key.T), ...)
    value = dot3(rows, load((wv_h, wv_l), ...))
    store_stacked(v_stack, 0, value)
    store((vt_h, vt_l), pair_of(value.T), ...)
    d_mixed = dot3(load((wo_h, wo_l), ...), pair_of(cot[...]), NT)
    d_mixed_t[...] = d_mixed
    store_interleaved(d_stack, d_mixed)


def store_bias(bias, listed, counts, parity, patches):
    queries = bias.shape[1]
    lane = lax.broadcasted_iota(jnp.int32, (1, queries), 1)
    near = jnp.where(parity[0] == 0, 4, 0)
    windows = (2, 3, near, near + 1, 4 - near, 5 - near)
    for place in patches:
        level = []
        for p in range(2):
            live = jnp.int32(1 if place == p else 0)
            for j in range(listed.shape[1]):
                hit = jnp.logical_and(j < counts[0, p], listed[p, j] == windows[place])
                live = jnp.where(hit, 1, live)
            level.append(jnp.where(live == 1, 0.0, -1e30).astype(F32))
        bias[place : place + 1, :] = jnp.where(lane < PT, level[0], level[1])


def biased(scores, bias, first):
    count = scores.shape[0] // PT
    return jnp.concatenate(
        [scores[i * PT : (i + 1) * PT] + bias[first + i : first + i + 1, :] for i in range(count)], axis=0
    )


def key_side(patches, gain, wk, wv, xhat, ht, k_stack, kt, v_stack, vt):
    for i, tokens in enumerate(patches):
        normal, _ = unit_rows(tokens[...])
        at = slice(i * PT, (i + 1) * PT)
        xhat[at, :] = normal
        hidden = normal * gain[...]
        store(ht, pair_of(hidden.T), slice(None), at)
    hidden = pair_of(xhat[...] * gain[...])
    key = dot3(hidden, load(wk, ...))
    store_stacked(k_stack, 0, key)
    store(kt, pair_of(key.T), ...)
    value = dot3(hidden, load(wv, ...))
    store_stacked(v_stack, 0, value)
    store(vt, pair_of(value.T), ...)


def head_rows(h):
    return pl.ds(pl.multiple_of(h * HD, HD), HD)


def head_stack(h):
    return pl.ds(pl.multiple_of(h * 4 * HD, 4 * HD), 4 * HD)


def weighed(highs, lows, rows, right):
    high = jnp.concatenate([r[rows, :] for r in highs], axis=1)
    low = jnp.concatenate([r[rows, :] for r in lows], axis=1)
    both = dot(jnp.concatenate([high, low], axis=0), right[0])
    return both[:HD] + (both[HD:] + dot(high, right[1]))


def near_side_kernel(
    patch_0, patch_1, gain, wk_h, wk_l, wv_h, wv_l,
    xhat, ht_h, ht_l, kt_h, kt_l, k_stack, v_stack, vt_h, vt_l,
):
    key_side(
        (patch_0, patch_1), gain, (wk_h, wk_l), (wv_h, wv_l), xhat, (ht_h, ht_l), k_stack, (kt_h, kt_l), v_stack,
        (vt_h, vt_l),
    )


def near_kernel(
    parity, listed, counts, _, q_stack, k_stack, v_stack, vt_h, vt_l, d_stack, k_near, v_near, vt2_h, vt2_l,
    e_h, e_l, d_scores, mixed, tops, totals,
    bias,
):
    store_bias(bias, listed, counts, parity, range(4))

    def one_head(h, carry):
        stack, rows = head_stack(h), head_rows(h)
        q_now, d_now = q_stack[stack, :], d_stack[stack, :]
        scores = jnp.concatenate(
            [biased(dot(k_stack[:, stack], q_now), bias, 0), biased(dot(k_near[:, stack], q_now), bias, 2)], axis=0
        )
        top = jnp.max(scores, axis=0, keepdims=True)
        weights = jnp.exp(scores - top)
        tops[pl.ds(h, 1), :] = top
        totals[pl.ds(h, 1), :] = jnp.sum(weights, axis=0, keepdims=True)
        pair = pair_of(weights)
        e_h[h] = pair[0]
        e_l[h] = pair[1]
        mixed[rows, :] = weighed((vt_h, vt2_h), (vt_l, vt2_l), rows, pair)
        d_scores[h] = jnp.concatenate([dot(v_stack[:, stack], d_now), dot(v_near[:, stack], d_now)], axis=0)
        return carry

    lax.fori_loop(0, HEADS, one_head, 0, unroll=UNROLL)


def gathered(left_h, left_l, right):
    left_half = lax.broadcasted_iota(jnp.int32, right[0].shape, 1) < HD
    zero = jnp.zeros_like(right[0])
    one = [jnp.where(left_half, x, zero) for x in right]
    two = [jnp.where(left_half, zero, x) for x in right]
    wide = dot(left_h[0], jnp.concatenate(one, axis=1)) + dot(left_h[1], jnp.concatenate(two, axis=1))
    narrow = dot(left_l[0], one[0]) + dot(left_l[1], two[0])
    return wide[:, : 2 * HD] + (wide[:, 2 * HD :] + narrow)


def pair_lanes(p):
    return pl.ds(pl.multiple_of(p * 2 * HD, 2 * HD), 2 * HD)


def kept_and_sent(me, pair, keep, send):
    rows = pair[0].shape[0]

    @pl.when(me[0] % 2 == 0)
    def _():
        keep[:rows, :] = pair[0][...]
        send[:rows, :] = pair[1][...]

    @pl.when(me[0] % 2 == 1)
    def _():
        keep[:rows, :] = pair[1][...]
        send[:rows, :] = pair[0][...]


def far_kernel(
    parity, listed, counts, patch_0, patch_1, gain, q_t, q_stack, d_mixed_t, d_stack, mixed_1, tops, totals,
    wk_h, wk_l, wv_h, wv_l,
    xhat, ht_h, ht_l, kt_h, kt_l, u_h, u_l, mixed_t, deltas, shares, shares_1, dk_h, dk_l, dv_h, dv_l, d_far,
    bias, k_far, v_far, vt_h, vt_l, e_h, e_l,
):
    store_bias(bias, listed, counts, parity, range(4, 6))
    key_side(
        (patch_0, patch_1), gain, (wk_h, wk_l), (wv_h, wv_l), xhat, (ht_h, ht_l), k_far, (kt_h, kt_l), v_far,
        (vt_h, vt_l),
    )

    def one_pair(p, carry):
        d_scaled, q_scaled = [], []
        for a in range(2):
            h = 2 * p + a
            stack, rows, row = head_stack(h), head_rows(h), pl.ds(h, 1)
            scores = biased(dot(k_far[:, stack], q_stack[stack, :]), bias, 4)
            top_1 = tops[row, :]
            top = jnp.maximum(top_1, jnp.max(scores, axis=0, keepdims=True))
            weights = jnp.exp(scores - top)
            shrink = jnp.exp(top_1 - top)
            share = 1.0 / (shrink * totals[row, :] + jnp.sum(weights, axis=0, keepdims=True))
            share_1 = shrink * share
            pair = pair_of(weights)
            e_h[a] = pair[0]
            e_l[a] = pair[1]
            mixed = share_1 * mixed_1[rows, :] + share * weighed((vt_h,), (vt_l,), rows, pair)
            mixed_t[rows, :] = mixed
            d_mixed = d_mixed_t[rows, :]
            delta = jnp.sum(d_mixed * mixed, axis=0, keepdims=True)
            deltas[row, :] = delta
            shares[row, :] = share
            shares_1[row, :] = share_1
            pair = pair_of(weights * (dot(v_far[:, stack], d_stack[stack, :]) - delta))
            u_h[h] = pair[0]
            u_l[h] = pair[1]
            d_scaled.append(d_mixed * share)
            q_scaled.append(q_t[rows, :] * share)
        lanes = pair_lanes(p)
        right = pair_of(jnp.concatenate(d_scaled, axis=0).T)
        d_value = gathered((e_h[0], e_h[1]), (e_l[0], e_l[1]), right)
        store((dv_h, dv_l), pair_of(d_value), slice(None), lanes)
        right = pair_of(jnp.concatenate(q_scaled, axis=0).T)
        d_key = gathered((u_h[2 * p], u_h[2 * p + 1]), (u_l[2 * p], u_l[2 * p + 1]), right)
        store((dk_h, dk_l), pair_of(d_key), slice(None), lanes)
        return carry

    lax.fori_loop(0, PAIRS, one_pair, 0, unroll=UNROLL)
    d_far[...] = sums_of(
        [load((dk_h, dk_l), ...), load((dv_h, dv_l), ...)], [load((wk_h, wk_l), ...), load((wv_h, wv_l), ...)], NT
    )


def back_kernel(
    q_t, d_mixed_t, kt_h, kt_l, kt2_h, kt2_l, kt3_h, kt3_l, e_h, e_l, d_scores, u_h, u_l, deltas, shares, shares_1,
    dq_t, dk_h, dk_l, dv_h, dv_l,
    s_h, s_l,
):
    def one_pair(p, carry):
        q_scaled, d_scaled = [], []
        for a in range(2):
            h = 2 * p + a
            rows, row = head_rows(h), pl.ds(h, 1)
            weights = e_h[h].astype(F32) + e_l[h].astype(F32)
            pair = pair_of(weights * (d_scores[h] - deltas[row, :]))
            s_h[a] = pair[0]
            s_l[a] = pair[1]
            share_1 = shares_1[row, :]
            one = weighed((kt_h, kt2_h), (kt_l, kt2_l), rows, pair)
            two = weighed((kt3_h,), (kt3_l,), rows, (u_h[h], u_l[h]))
            dq_t[rows, :] = (share_1 * one + shares[row, :] * two) * HD ** (-0.5)
            q_scaled.append(q_t[rows, :] * share_1)
            d_scaled.append(d_mixed_t[rows, :] * share_1)
        lanes = pair_lanes(p)
        right = pair_of(jnp.concatenate(q_scaled, axis=0).T)
        d_key = gathered((s_h[0], s_h[1]), (s_l[0], s_l[1]), right)
        store((dk_h, dk_l), pair_of(d_key), slice(None), lanes)
        right = pair_of(jnp.concatenate(d_scaled, axis=0).T)
        d_value = gathered((e_h[2 * p], e_h[2 * p + 1]), (e_l[2 * p], e_l[2 * p + 1]), right)
        store((dv_h, dv_l), pair_of(d_value), slice(None), lanes)
        return carry

    lax.fori_loop(0, PAIRS, one_pair, 0, unroll=UNROLL)


def mix_kernel(
    me, mixed_t, ht_h, ht_l, ht2_h, ht2_l, ht3_h, ht3_l, dv_h, dv_l, dv3_h, dv3_l, cot,
    keep, send,
    grad_o, grad_v,
):
    own = cot.shape[0]
    grad_o[...] = dot3(pair_of(mixed_t[...]), pair_of(cot[...]))
    turned = [load(t, ...) for t in ((ht_h, ht_l), (ht2_h, ht2_l), (ht3_h, ht3_l))]
    d_values = [load((dv_h, dv_l), slice(0, own)), load((dv_h, dv_l), slice(own, 2 * own)), load((dv3_h, dv3_l), ...)]
    grad_v[...] = sums_of(turned, d_values)
    kept_and_sent(me, (grad_o, grad_v), keep, send)


def result_kernel(_, mixed_t, tokens, wo_h, wo_l, result, mark):
    mark[...] = jnp.zeros_like(mark)
    result[...] = dot3(pair_of(mixed_t[...].T), load((wo_h, wo_l), ...)) + tokens[...]


def grad_kernel(
    ht_h, ht_l, ht2_h, ht2_l, ht3_h, ht3_l, dq_t, dk_h, dk_l, dk3_h, dk3_l,
    grad_q, grad_k, dq_h, dq_l,
):
    own = dq_h.shape[0]
    d_query = pair_of(dq_t[...].T)
    store((dq_h, dq_l), d_query, ...)
    turned = [load(t, ...) for t in ((ht_h, ht_l), (ht2_h, ht2_l), (ht3_h, ht3_l))]
    d_keys = [load((dk_h, dk_l), slice(0, own)), load((dk_h, dk_l), slice(own, 2 * own)), load((dk3_h, dk3_l), ...)]
    grad_q[...] = dot3(turned[0], d_query)
    grad_k[...] = sums_of(turned, d_keys)


def core_kernel(me, grad_q, grad_k, _back, _keep, keep, send):
    kept_and_sent(me, (grad_q, grad_k), keep, send)


def side_kernel(
    _, d_back, dq_h, dq_l, dk_h, dk_l, dv_h, dv_l, wq_h, wq_l, wk_h, wk_l, wv_h, wv_l,
    d_given, d_own, mark,
):
    mark[...] = jnp.zeros_like(mark)
    own = d_own.shape[0]
    first, near = slice(0, own), slice(own, 2 * own)
    w_q, w_k, w_v = load((wq_h, wq_l), ...), load((wk_h, wk_l), ...), load((wv_h, wv_l), ...)
    d_given[...] = d_back[...] + sums_of(
        [load((dk_h, dk_l), near), load((dv_h, dv_l), near)], [w_k, w_v], NT
    )
    d_own[...] = sums_of(
        [load((dq_h, dq_l), ...), load((dk_h, dk_l), first), load((dv_h, dv_l), first)], [w_q, w_k, w_v], NT
    )


def half_of(me, mask, mine, rows):
    index = (me[0] // mask) % 2
    return pl.ds(pl.multiple_of((index if mine else 1 - index) * rows, 8), rows)


def add_kernel(a, b, out, *_):
    out[...] = a[...] + b[...]


def cut_kernel(masks, me, keep_1, other_1, keep_2, other_2, *outs):
    count = keep_1.shape[0]
    *outs, sums = outs
    sums[:count, :] = keep_1[...] + other_1[...]
    sums[count:, :] = keep_2[...] + other_2[...]
    at = 0
    for i, mask in enumerate(masks):
        rows = outs[2 * i].shape[0]
        for out, mine in ((outs[2 * i], True), (outs[2 * i + 1], False)):
            index = (me[0] // mask) % 2
            start = at + (index if mine else 1 - index) * rows
            out[...] = sums[pl.ds(pl.multiple_of(start, 8), rows), :]
        at += 2 * rows


def halve_kernel(mask, me, keep, other, *rest):
    next_keep, next_send = rest[-2:]
    rows = next_keep.shape[0]
    for out, mine in ((next_keep, True), (next_send, False)):
        at = half_of(me, mask, mine, rows)
        out[...] = keep[at, :] + other[at, :]


def first_kernel(a, b, d_given, out, d_going):
    out[...] = a[...] + b[...]
    d_going[...] = d_given[...]


def last_kernel(a, b, *rest):
    rest[-1][...] = a[...] + b[...]


def double_kernel(mask, me, mine, other, *rest):
    out = rest[-1]
    rows = mine.shape[0]
    out[half_of(me, mask, True, rows), :] = mine[...]
    out[half_of(me, mask, False, rows), :] = other[...]


def write_kernel(ranges, me, gain, wv_h, wv_l, wq_h, wq_l, wk_h, wk_l, *refs):
    mine, other, outs, d_gain, (partial, sent) = refs[:3], refs[3:6], refs[6:10], refs[10], refs[11:]
    weights = (None, (wv_h, wv_l), (wq_h, wq_l), (wk_h, wk_l))
    lanes = partial.shape[1]
    partial[...] = jnp.zeros_like(partial)
    for bit in range(2):

        @pl.when(me[0] % 2 == bit)
        def _():
            pieces = [
                (parts[i].at[pl.ds(first, rows)], 2 * exchange + (bit + core) % 2, to, rows)
                for core, parts in enumerate((mine, other))
                for i, first, rows, exchange, to in ranges
            ]
            copies = [
                pltpu.make_async_copy(piece, outs[matrix].at[pl.ds(to, rows)], sent.at[n])
                for n, (piece, matrix, to, rows) in enumerate(pieces)
            ]
            for copy in copies:
                copy.start()
            for piece, matrix, to, rows in pieces:
                if matrix:
                    high, low = weights[matrix]
                    for lane in range(0, piece.shape[1], lanes):
                        at = (slice(to, to + rows), slice(lane, lane + lanes))
                        weight = high[at].astype(F32) + low[at].astype(F32)
                        partial[to : to + rows, :] += weight * piece[:, lane : lane + lanes]
            for copy in copies:
                copy.wait()

    d_gain[...] = jnp.sum(partial[...].T, axis=0, keepdims=True) / gain[...]


def tokens_kernel(_, tokens, gain, cot, d_own, d_other, out, mark):
    mark[...] = jnp.zeros_like(mark)
    normal, rstd = unit_rows(tokens[...])
    d_normal = (d_own[...] + d_other[...]) * gain[...]
    inner = jnp.mean(d_normal * normal, axis=1, keepdims=True)
    centre = jnp.mean(d_normal, axis=1, keepdims=True)
    out[...] = (d_normal - centre - normal * inner) * rstd + cot[...]


def shape(*dims, dtype=F32):
    return jax.ShapeDtypeStruct(dims, dtype)


def pairs(*dims):
    return [shape(*dims, dtype=BF16)] * 2


def call(kernel, inputs, outputs, scratch=(), scalars=0, limit=4, us=1):
    return pl.pallas_call(
        kernel,
        out_shape=outputs,
        in_specs=[SMEM] * scalars + [VMEM] * (len(inputs) - scalars),
        out_specs=[VMEM] * len(outputs),
        scratch_shapes=[pltpu.VMEM(s.shape, s.dtype) for s in scratch],
        compiler_params=pltpu.CompilerParams(vmem_limit_bytes=limit * 2**20),
        cost_estimate=pl.CostEstimate(flops=us * 10**9, bytes_accessed=0, transcendentals=0),
    )(*inputs)


MARK = shape(8, 128)


def along_space(value, target):
    count = lax.axis_size("space")
    return lax.ppermute(value, "space", [(i, target(i) % count) for i in range(count)])


def across(value):
    return along_space(value, lambda i: i ^ 1)


def onward(value):
    return along_space(value, lambda i: i + 2 - 4 * (i % 2))


def homeward(value):
    return along_space(value, lambda i: i - 2 + 4 * (i % 2))


def devices():
    return lax.axis_size("space") * lax.axis_size("slab")


def swapped(value, mask):
    return lax.ppermute(value, ("space", "slab"), [(i, i ^ mask) for i in range(devices())])


ORDERS = ((4, 2, 8), (2, 8, 4), (8, 4, 2))
LAST = 16


def summed(me, keep_1, other_1, keep_2, send_2, weights, gain, result_of, side_of, tokens_of):
    count, width = keep_1.shape
    total = 2 * count
    unit = 8 * 8
    sizes = [total // unit // 3 * unit] * 2
    sizes.append(total - sum(sizes))
    parts = call(
        functools.partial(cut_kernel, [order[0] for order in ORDERS]),
        (me, keep_1, other_1, keep_2, swapped(send_2, 1)),
        [shape(size // 2, width) for size in sizes for _ in range(2)],
        [shape(total, width)],
        scalars=1, limit=8,
    )
    d_given, d_own, mark = side_of(parts[0])
    parts = [[parts[2 * i], swapped(parts[2 * i + 1], ORDERS[i][0])] for i in range(3)]
    for step in (1, 2):
        for i in range(3):
            half, mask = shape(sizes[i] >> (step + 1), width), ORDERS[i][step]
            place = (mark,) if step == 1 and i == 0 else ()
            keep, send = call(
                functools.partial(halve_kernel, mask), (me, *parts[i], *place), [half, half], scalars=1
            )
            parts[i] = [keep, swapped(send, mask)]
    for i in (0, 2, 1):
        if i == 0:
            part, d_going = call(first_kernel, (*parts[i], d_given), [parts[i][0], d_given])
            d_other = across(d_going)
            result, mark = result_of(part)
        else:
            (part,) = call(add_kernel, parts[i], [parts[i][0]])
        mask, other = LAST, swapped(part, LAST)
        while 2 * mask < devices():
            (part,) = call(add_kernel, (part, other), [part])
            mask *= 2
            other = swapped(part, mask)
        place = (d_other, mark) if i == 1 else ()
        (parts[i],) = call(last_kernel, (part, other, *place), [part])
    for step in (2, 1, 0):
        for i in range(3):
            mask = ORDERS[i][step]
            place = (mark,) if step == 0 and i == 2 else ()
            (parts[i],) = call(
                functools.partial(double_kernel, mask), (me, parts[i], swapped(parts[i], mask), *place),
                [shape(2 * parts[i].shape[0], width)], scalars=1,
            )
        if step == 1:
            d_tokens, mark = tokens_of(parts[0], d_own, d_other)
    others = [swapped(part, 1) for part in parts]
    ranges, at = [], 0
    for i, size in enumerate(sizes):
        for exchange in range(2):
            start, stop = max(at, exchange * count), min(at + size, (exchange + 1) * count)
            if start < stop:
                ranges.append((i, start - at, stop - start, exchange, start - exchange * count))
        at += size
    *gradients, d_gain = pl.pallas_call(
        functools.partial(write_kernel, ranges),
        out_shape=[shape(count, width)] * 4 + [shape(1, width)],
        in_specs=[SMEM] + [VMEM] * 13,
        out_specs=[pl.BlockSpec(memory_space=pl.ANY)] * 4 + [VMEM],
        scratch_shapes=[pltpu.VMEM((count, 128), F32), pltpu.SemaphoreType.DMA((2 * len(ranges),))],
        compiler_params=pltpu.CompilerParams(vmem_limit_bytes=2**23),
    )(me, gain, *weights, *parts, *others)
    return gradients, d_gain.reshape(width), d_tokens, result


def body(tokens, gain, wq, wk, wv, wo, neighbour_list, neighbour_count, cotangent):
    rows, width = tokens.shape
    me = (lax.axis_index("space") * lax.axis_size("slab") + lax.axis_index("slab")).astype(jnp.int32)[None]
    parity = (lax.axis_index("space") % 2).astype(jnp.int32)[None]
    counts = neighbour_count[None, :]
    near = [across(tokens[i * PT : (i + 1) * PT]) for i in range(2)]
    far = [onward(near[0])]
    gain_row = gain[None, :]
    stack_rows, stack_columns = shape(HEADS * 4 * HD, rows, dtype=BF16), shape(rows, HEADS * 4 * HD, dtype=BF16)
    turned, square, pair = pairs(width, rows), pairs(width, width), pairs(rows, width)
    whole, whole_t, scalars = shape(rows, width), shape(width, rows), shape(HEADS, rows)
    weights = call(weight_kernel, (me, parity, wq, wk, wv, wo), square * 4, scalars=2, limit=20)
    wq_h, wq_l, wk_h, wk_l, wv_h, wv_l, wo_h, wo_l = weights
    (
        xhat, ht_h, ht_l, q_t, q_stack, k_stack, v_stack, kt_h, kt_l, vt_h, vt_l, d_mixed_t, d_stack,
    ) = call(
        own_kernel,
        (near[0], tokens, gain_row, cotangent, *weights),
        [whole, *turned, whole_t, stack_rows, stack_columns, stack_columns, *turned, *turned, whole_t, stack_rows],
        limit=LIMITS[0], us=1,
    )
    near[1], q_stack = lax.optimization_barrier((near[1], q_stack))
    far.append(onward(near[1]))
    w_k, w_v = (wk_h, wk_l), (wv_h, wv_l)
    xhat2, ht2_h, ht2_l, kt2_h, kt2_l, k_near, v_near, vt2_h, vt2_l = call(
        near_side_kernel,
        (*near, gain_row, *w_k, *w_v),
        [whole, *turned, *turned, stack_columns, stack_columns, *turned],
        limit=LIMITS[1], us=1,
    )
    e_h, e_l, d_scores, mixed, tops, totals = call(
        near_kernel,
        (
            parity, neighbour_list, counts, far[0], q_stack, k_stack, v_stack, vt_h, vt_l, d_stack, k_near, v_near,
            vt2_h, vt2_l,
        ),
        [*pairs(HEADS, 2 * rows, rows), shape(HEADS, 2 * rows, rows), whole_t, scalars, scalars],
        [shape(8, rows)],
        scalars=3, limit=LIMITS[1], us=1,
    )
    (
        xhat3, ht3_h, ht3_l, kt3_h, kt3_l, u_h, u_l, mixed_t, deltas, shares, shares_1, dk3_h, dk3_l, dv3_h, dv3_l,
        d_far,
    ) = call(
        far_kernel,
        (
            parity, neighbour_list, counts, *far, gain_row, q_t, q_stack, d_mixed_t, d_stack, mixed, tops, totals,
            *w_k, *w_v,
        ),
        [
            whole, *turned, *turned, *pairs(HEADS, rows, rows), whole_t, scalars, scalars, scalars, *pair, *pair,
            whole,
        ],
        [shape(8, rows), stack_columns, stack_columns, *turned, *pairs(2, rows, rows)],
        scalars=3, limit=LIMITS[2], us=1,
    )
    d_back = homeward(d_far)
    dq_t, dk_h, dk_l, dv_h, dv_l = call(
        back_kernel,
        (
            q_t, d_mixed_t, kt_h, kt_l, kt2_h, kt2_l, kt3_h, kt3_l, e_h, e_l, d_scores, u_h, u_l, deltas, shares,
            shares_1,
        ),
        [whole_t, *pairs(2 * rows, width), *pairs(2 * rows, width)],
        [*pairs(2, 2 * rows, rows)],
        limit=LIMITS[4], us=1,
    )
    keep_1, send_1 = call(
        mix_kernel,
        (me, mixed_t, ht_h, ht_l, ht2_h, ht2_l, ht3_h, ht3_l, dv_h, dv_l, dv3_h, dv3_l, cotangent),
        [shape(width, width), shape(width, width)],
        [shape(width, width), shape(width, width)],
        scalars=1, limit=LIMITS[3], us=1,
    )
    other_1 = swapped(send_1, 1)
    grad_q, grad_k, dq_h, dq_l = call(
        grad_kernel,
        (ht_h, ht_l, ht2_h, ht2_l, ht3_h, ht3_l, dq_t, dk_h, dk_l, dk3_h, dk3_l),
        [shape(width, width), shape(width, width), *pair],
        limit=LIMITS[5], us=1,
    )
    keep_2, send_2 = call(
        core_kernel, (me, grad_q, grad_k, d_back, keep_1), [shape(width, width)] * 2, scalars=1, limit=8
    )

    def result_of(place):
        return call(result_kernel, (place, mixed_t, tokens, wo_h, wo_l), [whole, MARK], limit=LIMITS[3], us=1)

    def side_of(place):
        inputs = (place, d_back, dq_h, dq_l, dk_h, dk_l, dv_h, dv_l, wq_h, wq_l, *w_k, *w_v)
        return call(side_kernel, inputs, [whole, whole, MARK], limit=LIMITS[3], us=1)

    def tokens_of(place, d_own, d_other):
        inputs = (place, tokens, gain_row, cotangent, d_own, d_other)
        return call(tokens_kernel, inputs, [whole, MARK], limit=8)

    (grad_o, grad_v, grad_q, grad_k), d_gain, d_tokens, result = summed(
        me, keep_1, other_1, keep_2, send_2, (wv_h, wv_l, wq_h, wq_l, *w_k), gain_row, result_of, side_of, tokens_of
    )
    return (result, d_tokens, d_gain, grad_q, grad_k, grad_v, grad_o)


UNROLL = True
LIMITS = (8, 8, 8, 8, 8, 8)


def solution(mesh):
    tokens = P(("space", "slab"), None)
    return jax.shard_map(
        body,
        mesh=mesh,
        in_specs=(tokens, P(), P(), P(), P(), P(), tokens, P(("space", "slab")), tokens),
        out_specs=(tokens, tokens, P(), P(), P(), P(), P()),
        check_vma=False,
    )
```

```python
import functools

import jax
import jax.numpy as jnp
from jax import lax
from jax.experimental import pallas as pl
from jax.experimental.pallas import tpu as pltpu
from jax.sharding import PartitionSpec as P

HEADS = 8
PT = 128
HD = 64
PAIRS = HEADS // 2
F32 = jnp.float32
BF16 = jnp.bfloat16
NN = (((1,), (0,)), ((), ()))
NT = (((1,), (1,)), ((), ()))
VMEM = pl.BlockSpec(memory_space=pltpu.VMEM)
SMEM = pl.BlockSpec(memory_space=pltpu.SMEM)


def pair_of(x):
    high = x.astype(BF16)
    return high, (x - high.astype(F32)).astype(BF16)


def dot(left, right, dims=NN):
    return lax.dot_general(left, right, dims, preferred_element_type=F32)


def dot3(left, right, dims=NN):
    return dot(left[0], right[0], dims) + (dot(left[0], right[1], dims) + dot(left[1], right[0], dims))


def load(refs, *index):
    return refs[0][index], refs[1][index]


def store(refs, pair, *index):
    refs[0][index] = pair[0]
    refs[1][index] = pair[1]


def unit_rows(tokens):
    centred = tokens - jnp.mean(tokens, axis=1, keepdims=True)
    variance = jnp.mean(centred * centred, axis=1, keepdims=True)
    rstd = lax.rsqrt(variance + 1e-05)
    return centred * rstd, rstd


def store_stacked(ref, row, rows):
    count = rows.shape[0]
    left_half = lax.broadcasted_iota(jnp.int32, (count, 2 * HD), 1) < HD
    for p in range(PAIRS):
        part = rows[:, p * 2 * HD : (p + 1) * 2 * HD]
        swapped = pltpu.roll(part, HD, 1)
        for a in range(2):
            both = jnp.where(left_half == (a == 0), part, swapped)
            high, low = pair_of(both)
            base = (2 * p + a) * 4 * HD
            ref[pl.ds(row, count), base : base + 2 * HD] = high
            ref[pl.ds(row, count), base + 2 * HD : base + 4 * HD] = low


def store_interleaved(ref, columns):
    high, low = pair_of(columns)
    for h in range(HEADS):
        for i, piece in enumerate((high, low, high, low)):
            at = h * 4 * HD + i * HD
            ref[at : at + HD, :] = piece[h * HD : (h + 1) * HD]


def sums_of(left, right, dims=NN):
    return sum(dot3(a, b, dims) for a, b in zip(left[1:], right[1:], strict=True)) + dot3(left[0], right[0], dims)


def weight_kernel(_me, _parity, wq, wk, wv, wo, wq_h, wq_l, wk_h, wk_l, wv_h, wv_l, wo_h, wo_l):
    for source, high, low in ((wq, wq_h, wq_l), (wk, wk_h, wk_l), (wv, wv_h, wv_l), (wo, wo_h, wo_l)):
        store((high, low), pair_of(source[...]), ...)


def own_kernel(
    _, tokens, gain, cot, wq_h, wq_l, wk_h, wk_l, wv_h, wv_l, wo_h, wo_l,
    ht_h, ht_l, q_t, q_stack, k_stack, v_stack, kt_h, kt_l, vt_h, vt_l, d_mixed_t, d_stack,
):
    hidden = unit_rows(tokens[...])[0] * gain[...]
    store((ht_h, ht_l), pair_of(hidden.T), ...)
    rows = pair_of(hidden)
    query = dot3(rows, load((wq_h, wq_l), ...)) * HD ** (-0.5)
    q_t[...] = query.T
    store_interleaved(q_stack, q_t[...])
    key = dot3(rows, load((wk_h, wk_l), ...))
    store_stacked(k_stack, 0, key)
    store((kt_h, kt_l), pair_of(key.T), ...)
    value = dot3(rows, load((wv_h, wv_l), ...))
    store_stacked(v_stack, 0, value)
    store((vt_h, vt_l), pair_of(value.T), ...)
    d_mixed = dot3(load((wo_h, wo_l), ...), pair_of(cot[...]), NT)
    d_mixed_t[...] = d_mixed
    store_interleaved(d_stack, d_mixed)


def store_bias(bias, listed, counts, parity, patches):
    queries = bias.shape[1]
    lane = lax.broadcasted_iota(jnp.int32, (1, queries), 1)
    near = jnp.where(parity[0] == 0, 4, 0)
    windows = (2, 3, near, near + 1, 4 - near, 5 - near)
    for place in patches:
        level = []
        for p in range(2):
            live = jnp.int32(1 if place == p else 0)
            for j in range(listed.shape[1]):
                hit = jnp.logical_and(j < counts[0, p], listed[p, j] == windows[place])
                live = jnp.where(hit, 1, live)
            level.append(jnp.where(live == 1, 0.0, -1e30).astype(F32))
        bias[place : place + 1, :] = jnp.where(lane < PT, level[0], level[1])


def biased(scores, bias, first):
    count = scores.shape[0] // PT
    return jnp.concatenate(
        [scores[i * PT : (i + 1) * PT] + bias[first + i : first + i + 1, :] for i in range(count)], axis=0
    )


def key_side(patches, gain, wk, wv, k_stack, v_stack, vt):
    hidden = jnp.concatenate([unit_rows(tokens[...])[0] * gain[...] for tokens in patches], axis=0)
    rows = pair_of(hidden)
    key = dot3(rows, load(wk, ...))
    store_stacked(k_stack, 0, key)
    value = dot3(rows, load(wv, ...))
    store_stacked(v_stack, 0, value)
    store(vt, pair_of(value.T), ...)
    return hidden, key


def head_rows(h):
    return pl.ds(pl.multiple_of(h * HD, HD), HD)


def head_stack(h):
    return pl.ds(pl.multiple_of(h * 4 * HD, 4 * HD), 4 * HD)


def weighed(highs, lows, rows, right):
    high = jnp.concatenate([r[rows, :] for r in highs], axis=1)
    low = jnp.concatenate([r[rows, :] for r in lows], axis=1)
    left = jnp.concatenate([high, low], axis=0)
    both = dot(left, right[0]) + dot(left, right[1])
    return both[:HD] + both[HD:]


def near_side_kernel(
    patch_0, patch_1, gain, wk_h, wk_l, wv_h, wv_l,
    ht_h, ht_l, kt_h, kt_l, k_stack, v_stack, vt_h, vt_l,
):
    hidden, key = key_side((patch_0, patch_1), gain, (wk_h, wk_l), (wv_h, wv_l), k_stack, v_stack, (vt_h, vt_l))
    store((ht_h, ht_l), pair_of(hidden.T), ...)
    store((kt_h, kt_l), pair_of(key.T), ...)


def near_kernel(
    parity, listed, counts, _, q_stack, k_stack, v_stack, vt_h, vt_l, d_stack, k_near, v_near, vt2_h, vt2_l,
    e_h, e_l, d_scores, mixed, tops, totals,
    bias,
):
    store_bias(bias, listed, counts, parity, range(4))

    def one_head(h, carry):
        stack, rows = head_stack(h), head_rows(h)
        q_now, d_now = q_stack[stack, :], d_stack[stack, :]
        scores = jnp.concatenate(
            [biased(dot(k_stack[:, stack], q_now), bias, 0), biased(dot(k_near[:, stack], q_now), bias, 2)], axis=0
        )
        top = jnp.max(scores, axis=0, keepdims=True)
        weights = jnp.exp(scores - top)
        tops[pl.ds(h, 1), :] = top
        totals[pl.ds(h, 1), :] = jnp.sum(weights, axis=0, keepdims=True)
        pair = pair_of(weights)
        e_h[h] = pair[0]
        e_l[h] = pair[1]
        mixed[rows, :] = weighed((vt_h, vt2_h), (vt_l, vt2_l), rows, pair)
        d_scores[h] = jnp.concatenate([dot(v_stack[:, stack], d_now), dot(v_near[:, stack], d_now)], axis=0)
        return carry

    lax.fori_loop(0, HEADS, one_head, 0, unroll=UNROLL)


def gathered(left_h, left_l, right):
    left_half = lax.broadcasted_iota(jnp.int32, right[0].shape, 1) < HD
    zero = jnp.zeros_like(right[0])
    one = [jnp.where(left_half, x, zero) for x in right]
    two = [jnp.where(left_half, zero, x) for x in right]
    one, two = jnp.concatenate(one, axis=1), jnp.concatenate(two, axis=1)
    wide = (dot(left_h[0], one) + dot(left_h[1], two)) + (dot(left_l[0], one) + dot(left_l[1], two))
    return wide[:, : 2 * HD] + wide[:, 2 * HD :]


def pair_lanes(p):
    return pl.ds(pl.multiple_of(p * 2 * HD, 2 * HD), 2 * HD)


def kept_and_sent(me, pair, keep, sends):
    rows = sends[0].shape[0]
    for bit in range(2):

        @pl.when(me[0] % 2 == bit)
        def _():
            keep[...] = pair[bit][...]
            for i, send in enumerate(sends):
                send[...] = pair[1 - bit][i * rows : (i + 1) * rows, :]


def far_kernel(
    parity, listed, counts, patch_0, patch_1, gain, q_t, q_stack, d_mixed_t, d_stack, mixed_1, tops, totals,
    wk_h, wk_l, wv_h, wv_l,
    hidden, key, u_h, u_l, mixed_t, deltas, shares, shares_1, dk_h, dk_l, dv_h, dv_l, d_far,
    bias, k_far, v_far, vt_h, vt_l, e_h, e_l,
):
    store_bias(bias, listed, counts, parity, range(4, 6))
    hidden[...], key[...] = key_side(
        (patch_0, patch_1), gain, (wk_h, wk_l), (wv_h, wv_l), k_far, v_far, (vt_h, vt_l)
    )

    def one_pair(p, carry):
        d_scaled, q_scaled = [], []
        for a in range(2):
            h = 2 * p + a
            stack, rows, row = head_stack(h), head_rows(h), pl.ds(h, 1)
            scores = biased(dot(k_far[:, stack], q_stack[stack, :]), bias, 4)
            top_1 = tops[row, :]
            top = jnp.maximum(top_1, jnp.max(scores, axis=0, keepdims=True))
            weights = jnp.exp(scores - top)
            shrink = jnp.exp(top_1 - top)
            share = 1.0 / (shrink * totals[row, :] + jnp.sum(weights, axis=0, keepdims=True))
            share_1 = shrink * share
            pair = pair_of(weights)
            e_h[a] = pair[0]
            e_l[a] = pair[1]
            mixed = share_1 * mixed_1[rows, :] + share * weighed((vt_h,), (vt_l,), rows, pair)
            mixed_t[rows, :] = mixed
            d_mixed = d_mixed_t[rows, :]
            delta = jnp.sum(d_mixed * mixed, axis=0, keepdims=True)
            deltas[row, :] = delta
            shares[row, :] = share
            shares_1[row, :] = share_1
            pair = pair_of(weights * (dot(v_far[:, stack], d_stack[stack, :]) - delta))
            u_h[h] = pair[0]
            u_l[h] = pair[1]
            d_scaled.append(d_mixed * share)
            q_scaled.append(q_t[rows, :] * share)
        lanes = pair_lanes(p)
        right = pair_of(jnp.concatenate(d_scaled, axis=0).T)
        d_value = gathered((e_h[0], e_h[1]), (e_l[0], e_l[1]), right)
        store((dv_h, dv_l), pair_of(d_value), slice(None), lanes)
        right = pair_of(jnp.concatenate(q_scaled, axis=0).T)
        d_key = gathered((u_h[2 * p], u_h[2 * p + 1]), (u_l[2 * p], u_l[2 * p + 1]), right)
        store((dk_h, dk_l), pair_of(d_key), slice(None), lanes)
        return carry

    lax.fori_loop(0, PAIRS, one_pair, 0, unroll=UNROLL)
    d_far[...] = sums_of(
        [load((dk_h, dk_l), ...), load((dv_h, dv_l), ...)], [load((wk_h, wk_l), ...), load((wv_h, wv_l), ...)], NT
    )


def back_kernel(
    q_t, d_mixed_t, kt_h, kt_l, kt2_h, kt2_l, key3, e_h, e_l, d_scores, u_h, u_l, deltas, shares, shares_1,
    dq_t, dk_h, dk_l, dv_h, dv_l,
    s_h, s_l, kt3_h, kt3_l,
):
    store((kt3_h, kt3_l), pair_of(key3[...].T), ...)

    def one_pair(p, carry):
        q_scaled, d_scaled = [], []
        for a in range(2):
            h = 2 * p + a
            rows, row = head_rows(h), pl.ds(h, 1)
            weights = e_h[h].astype(F32) + e_l[h].astype(F32)
            pair = pair_of(weights * (d_scores[h] - deltas[row, :]))
            s_h[a] = pair[0]
            s_l[a] = pair[1]
            share_1 = shares_1[row, :]
            one = weighed((kt_h, kt2_h), (kt_l, kt2_l), rows, pair)
            two = weighed((kt3_h,), (kt3_l,), rows, (u_h[h], u_l[h]))
            dq_t[rows, :] = (share_1 * one + shares[row, :] * two) * HD ** (-0.5)
            q_scaled.append(q_t[rows, :] * share_1)
            d_scaled.append(d_mixed_t[rows, :] * share_1)
        lanes = pair_lanes(p)
        right = pair_of(jnp.concatenate(q_scaled, axis=0).T)
        d_key = gathered((s_h[0], s_h[1]), (s_l[0], s_l[1]), right)
        store((dk_h, dk_l), pair_of(d_key), slice(None), lanes)
        right = pair_of(jnp.concatenate(d_scaled, axis=0).T)
        d_value = gathered((e_h[2 * p], e_h[2 * p + 1]), (e_l[2 * p], e_l[2 * p + 1]), right)
        store((dv_h, dv_l), pair_of(d_value), slice(None), lanes)
        return carry

    lax.fori_loop(0, PAIRS, one_pair, 0, unroll=UNROLL)


def mix_kernel(
    me, mixed_t, ht_h, ht_l, ht2_h, ht2_l, hidden3, dv_h, dv_l, dv3_h, dv3_l, cot, ht3_h, ht3_l, keep, *refs
):
    *sends, grad_o, grad_v = refs
    own = cot.shape[0]
    store((ht3_h, ht3_l), pair_of(hidden3[...].T), ...)
    grad_o[...] = dot3(pair_of(mixed_t[...]), pair_of(cot[...]))
    turned = [load(t, ...) for t in ((ht_h, ht_l), (ht2_h, ht2_l), (ht3_h, ht3_l))]
    d_values = [load((dv_h, dv_l), slice(0, own)), load((dv_h, dv_l), slice(own, 2 * own)), load((dv3_h, dv3_l), ...)]
    grad_v[...] = sums_of(turned, d_values)
    kept_and_sent(me, (grad_o, grad_v), keep, sends)


def result_kernel(_, mixed_t, tokens, wo_h, wo_l, result, mark):
    mark[...] = jnp.zeros_like(mark)
    result[...] = dot3(pair_of(mixed_t[...].T), load((wo_h, wo_l), ...)) + tokens[...]


def grad_kernel(
    ht_h, ht_l, ht2_h, ht2_l, ht3_h, ht3_l, dq_t, dk_h, dk_l, dk3_h, dk3_l,
    grad_q, grad_k, dq_h, dq_l,
):
    own = dq_h.shape[0]
    d_query = pair_of(dq_t[...].T)
    store((dq_h, dq_l), d_query, ...)
    turned = [load(t, ...) for t in ((ht_h, ht_l), (ht2_h, ht2_l), (ht3_h, ht3_l))]
    d_keys = [load((dk_h, dk_l), slice(0, own)), load((dk_h, dk_l), slice(own, 2 * own)), load((dk3_h, dk3_l), ...)]
    grad_q[...] = dot3(turned[0], d_query)
    grad_k[...] = sums_of(turned, d_keys)


def core_kernel(me, grad_q, grad_k, _keep, _back, keep, *sends):
    kept_and_sent(me, (grad_q, grad_k), keep, sends)


def side_kernel(
    _, d_back, dq_h, dq_l, dk_h, dk_l, dv_h, dv_l, wq_h, wq_l, wk_h, wk_l, wv_h, wv_l,
    d_given, d_own, mark,
):
    mark[...] = jnp.zeros_like(mark)
    own = d_own.shape[0]
    first, near = slice(0, own), slice(own, 2 * own)
    w_q, w_k, w_v = load((wq_h, wq_l), ...), load((wk_h, wk_l), ...), load((wv_h, wv_l), ...)
    d_given[...] = d_back[...] + sums_of(
        [load((dk_h, dk_l), near), load((dv_h, dv_l), near)], [w_k, w_v], NT
    )
    d_own[...] = sums_of(
        [load((dq_h, dq_l), ...), load((dk_h, dk_l), first), load((dv_h, dv_l), first)], [w_q, w_k, w_v], NT
    )


def half_of(me, mask, mine, rows):
    index = (me[0] // mask) % 2
    return pl.ds(pl.multiple_of((index if mine else 1 - index) * rows, 8), rows)


def add_kernel(a, b, out, *_):
    out[...] = a[...] + b[...]


def cut_kernel(masks, me, keep_1, keep_2, *refs):
    others, outs, sums = refs[: 2 * PIECES], refs[2 * PIECES : -1], refs[-1]
    rows = others[0].shape[0]
    for i, other in enumerate(others):
        keep = (keep_1, keep_2)[i // PIECES]
        first = i % PIECES * rows
        sums[i * rows : (i + 1) * rows, :] = keep[first : first + rows, :] + other[...]
    at = 0
    for i, mask in enumerate(masks):
        rows = outs[2 * i].shape[0]
        for out, mine in ((outs[2 * i], True), (outs[2 * i + 1], False)):
            index = (me[0] // mask) % 2
            start = at + (index if mine else 1 - index) * rows
            out[...] = sums[pl.ds(pl.multiple_of(start, 8), rows), :]
        at += 2 * rows


def halve_kernel(mask, me, keep, other, *rest):
    next_keep, next_send = rest[-2:]
    rows = next_keep.shape[0]
    for out, mine in ((next_keep, True), (next_send, False)):
        at = half_of(me, mask, mine, rows)
        out[...] = keep[at, :] + other[at, :]


def first_kernel(a, b, d_given, out, d_going):
    out[...] = a[...] + b[...]
    d_going[...] = d_given[...]


def last_kernel(a, b, *rest):
    rest[-1][...] = a[...] + b[...]


def double_kernel(mask, me, mine, other, *rest):
    out = rest[-1]
    rows = mine.shape[0]
    out[half_of(me, mask, True, rows), :] = mine[...]
    out[half_of(me, mask, False, rows), :] = other[...]


def write_kernel(ranges, core, me, gain, wv_h, wv_l, wq_h, wq_l, wk_h, wk_l, *refs):
    parts, refs = refs[:3], refs[3:]
    before = refs[4] if core else None
    refs = refs[5 * core :]
    outs, last, (partial, total, sent) = refs[:4], refs[4], refs[5:] if core else (refs[4], None, refs[5])
    weights = (None, (wv_h, wv_l), (wq_h, wq_l), (wk_h, wk_l))
    lanes = partial.shape[1]
    partial[...] = before[...] if core else jnp.zeros_like(partial)
    for bit in range(2):

        @pl.when(me[0] % 2 == bit)
        def _():
            pieces = [
                (parts[i].at[pl.ds(first, rows)], 2 * exchange + (bit + core) % 2, to, rows)
                for i, first, rows, exchange, to in ranges
            ]
            copies = [
                pltpu.make_async_copy(piece, outs[matrix].at[pl.ds(to, rows)], sent.at[n])
                for n, (piece, matrix, to, rows) in enumerate(pieces)
            ]
            for copy in copies:
                copy.start()
            for piece, matrix, to, rows in pieces:
                if matrix:
                    high, low = weights[matrix]
                    for lane in range(0, piece.shape[1], lanes):
                        at = (slice(to, to + rows), slice(lane, lane + lanes))
                        weight = high[at].astype(F32) + low[at].astype(F32)
                        partial[to : to + rows, :] += weight * piece[:, lane : lane + lanes]
            if core:
                total[...] = jnp.sum(partial[...].T, axis=0, keepdims=True) / gain[...]
                copies.append(pltpu.make_async_copy(total, last, sent.at[len(copies)]))
                copies[-1].start()
            for copy in copies:
                copy.wait()


def written(me, gain, weights, parts, ranges, count, core, held=()):
    width = parts[0].shape[1]
    anywhere = pl.BlockSpec(memory_space=pl.ANY)
    partial = shape(count, 128)
    semaphores = pltpu.SemaphoreType.DMA((len(ranges) + core,))
    return pl.pallas_call(
        functools.partial(write_kernel, ranges, core),
        out_shape=[shape(count, width)] * 4 + [shape(1, width) if core else partial],
        in_specs=[SMEM] + [VMEM] * 10 + ([anywhere] * 4 + [VMEM] if core else []),
        out_specs=[anywhere] * 4 + [anywhere if core else VMEM],
        scratch_shapes=([pltpu.VMEM(partial.shape, F32), pltpu.VMEM((1, width), F32)] if core else []) + [semaphores],
        input_output_aliases={11 + i: i for i in range(4)} if core else {},
        compiler_params=pltpu.CompilerParams(vmem_limit_bytes=2**23),
        cost_estimate=pl.CostEstimate(flops=10**9, bytes_accessed=0, transcendentals=0),
    )(me, gain, *weights, *parts, *held)


def tokens_kernel(_, tokens, gain, cot, d_own, d_other, out, mark):
    mark[...] = jnp.zeros_like(mark)
    normal, rstd = unit_rows(tokens[...])
    d_normal = (d_own[...] + d_other[...]) * gain[...]
    inner = jnp.mean(d_normal * normal, axis=1, keepdims=True)
    centre = jnp.mean(d_normal, axis=1, keepdims=True)
    out[...] = (d_normal - centre - normal * inner) * rstd + cot[...]


def shape(*dims, dtype=F32):
    return jax.ShapeDtypeStruct(dims, dtype)


def pairs(*dims):
    return [shape(*dims, dtype=BF16)] * 2


def call(kernel, inputs, outputs, scratch=(), scalars=0, limit=4, us=1):
    return pl.pallas_call(
        kernel,
        out_shape=outputs,
        in_specs=[SMEM] * scalars + [VMEM] * (len(inputs) - scalars),
        out_specs=[VMEM] * len(outputs),
        scratch_shapes=[pltpu.VMEM(s.shape, s.dtype) for s in scratch],
        compiler_params=pltpu.CompilerParams(vmem_limit_bytes=limit * 2**20),
        cost_estimate=pl.CostEstimate(flops=int(us * 10**9), bytes_accessed=0, transcendentals=0),
    )(*inputs)


MARK = shape(8, 128)


def along_space(value, target):
    count = lax.axis_size("space")
    return lax.ppermute(value, "space", [(i, target(i) % count) for i in range(count)])


def across(value):
    return along_space(value, lambda i: i ^ 1)


def onward(value):
    return along_space(value, lambda i: i + 2 - 4 * (i % 2))


def homeward(value):
    return along_space(value, lambda i: i - 2 + 4 * (i % 2))


def devices():
    return lax.axis_size("space") * lax.axis_size("slab")


def swapped(value, mask):
    return lax.ppermute(value, ("space", "slab"), [(i, i ^ mask) for i in range(devices())])


ORDERS = ((4, 2, 8), (2, 8, 4), (8, 4, 2))
LAST = 16


def summed(me, keep_1, others_1, keep_2, others_2, weights, gain, result_of, side_of, tokens_of):
    count, width = keep_1.shape
    total = 2 * count
    unit = 8 * 8
    sizes = [total // unit // 3 * unit] * 2
    sizes.append(total - sum(sizes))
    parts = call(
        functools.partial(cut_kernel, [order[0] for order in ORDERS]),
        (me, keep_1, keep_2, *others_1, *others_2),
        [shape(size // 2, width) for size in sizes for _ in range(2)],
        [shape(total, width)],
        scalars=1, limit=8,
    )
    d_given, d_own, mark = side_of(parts[0])
    parts = [[parts[2 * i], swapped(parts[2 * i + 1], ORDERS[i][0])] for i in range(3)]
    for step in (1, 2):
        for i in range(3):
            half, mask = shape(sizes[i] >> (step + 1), width), ORDERS[i][step]
            place = (mark,) if step == 1 else ()
            keep, send = call(
                functools.partial(halve_kernel, mask), (me, *parts[i], *place), [half, half], scalars=1
            )
            parts[i] = [keep, swapped(send, mask)]
    for i in (0, 2, 1):
        if i == 1:
            part, d_going = call(first_kernel, (*parts[i], d_given), [parts[i][0], d_given])
            d_other = across(d_going)
        else:
            (part,) = call(add_kernel, parts[i], [parts[i][0]])
        if i == 0:
            result, mark = result_of(part)
        mask, other = LAST, swapped(part, LAST)
        while 2 * mask < devices():
            (part,) = call(add_kernel, (part, other), [part])
            mask *= 2
            other = swapped(part, mask)
        place = (mark,) if i == 1 else ()
        (parts[i],) = call(last_kernel, (part, other, *place), [part])
    for step in (2, 1, 0):
        for i in range(3):
            mask = ORDERS[i][step]
            place = {(2, 1): (d_other,), (0, 2): (mark,)}.get((step, i), ())
            (parts[i],) = call(
                functools.partial(double_kernel, mask), (me, parts[i], swapped(parts[i], mask), *place),
                [shape(2 * parts[i].shape[0], width)], scalars=1,
            )
        if step == 1:
            d_tokens, mark = tokens_of(parts[0], d_own, d_other)
    others = [swapped(part, 1) for part in parts]
    ranges, at = [], 0
    for i, size in enumerate(sizes):
        for exchange in range(2):
            start, stop = max(at, exchange * count), min(at + size, (exchange + 1) * count)
            if start < stop:
                ranges.append((i, start - at, stop - start, exchange, start - exchange * count))
        at += size
    held = written(me, gain, weights, parts, ranges, count, 0)
    *gradients, d_gain = written(me, gain, weights, others, ranges, count, 1, held)
    return gradients, d_gain.reshape(width), d_tokens, result


def body(tokens, gain, wq, wk, wv, wo, neighbour_list, neighbour_count, cotangent):
    rows, width = tokens.shape
    me = (lax.axis_index("space") * lax.axis_size("slab") + lax.axis_index("slab")).astype(jnp.int32)[None]
    parity = (lax.axis_index("space") % 2).astype(jnp.int32)[None]
    counts = neighbour_count[None, :]
    near = [across(tokens[i * PT : (i + 1) * PT]) for i in range(2)]
    far = [onward(near[0])]
    gain_row = gain[None, :]
    stack_rows, stack_columns = shape(HEADS * 4 * HD, rows, dtype=BF16), shape(rows, HEADS * 4 * HD, dtype=BF16)
    turned, square, pair = pairs(width, rows), pairs(width, width), pairs(rows, width)
    whole, whole_t, scalars = shape(rows, width), shape(width, rows), shape(HEADS, rows)
    weights = call(weight_kernel, (me, parity, wq, wk, wv, wo), square * 4, scalars=2, limit=20)
    wq_h, wq_l, wk_h, wk_l, wv_h, wv_l, wo_h, wo_l = weights
    (
        ht_h, ht_l, q_t, q_stack, k_stack, v_stack, kt_h, kt_l, vt_h, vt_l, d_mixed_t, d_stack,
    ) = call(
        own_kernel,
        (near[0], tokens, gain_row, cotangent, *weights),
        [*turned, whole_t, stack_rows, stack_columns, stack_columns, *turned, *turned, whole_t, stack_rows],
        limit=LIMITS[0], us=1,
    )
    near[1], q_stack = lax.optimization_barrier((near[1], q_stack))
    far.append(onward(near[1]))
    w_k, w_v = (wk_h, wk_l), (wv_h, wv_l)
    ht2_h, ht2_l, kt2_h, kt2_l, k_near, v_near, vt2_h, vt2_l = call(
        near_side_kernel,
        (*near, gain_row, *w_k, *w_v),
        [*turned, *turned, stack_columns, stack_columns, *turned],
        limit=LIMITS[1], us=1,
    )
    e_h, e_l, d_scores, mixed, tops, totals = call(
        near_kernel,
        (
            parity, neighbour_list, counts, far[0], q_stack, k_stack, v_stack, vt_h, vt_l, d_stack, k_near, v_near,
            vt2_h, vt2_l,
        ),
        [*pairs(HEADS, 2 * rows, rows), shape(HEADS, 2 * rows, rows), whole_t, scalars, scalars],
        [shape(8, rows)],
        scalars=3, limit=LIMITS[1], us=1,
    )
    (
        hidden3, key3, u_h, u_l, mixed_t, deltas, shares, shares_1, dk3_h, dk3_l, dv3_h, dv3_l,
        d_far,
    ) = call(
        far_kernel,
        (
            parity, neighbour_list, counts, *far, gain_row, q_t, q_stack, d_mixed_t, d_stack, mixed, tops, totals,
            *w_k, *w_v,
        ),
        [
            whole, whole, *pairs(HEADS, rows, rows), whole_t, scalars, scalars, scalars, *pair, *pair,
            whole,
        ],
        [shape(8, rows), stack_columns, stack_columns, *turned, *pairs(2, rows, rows)],
        scalars=3, limit=LIMITS[2], us=1,
    )
    d_back = homeward(d_far)
    dq_t, dk_h, dk_l, dv_h, dv_l = call(
        back_kernel,
        (
            q_t, d_mixed_t, kt_h, kt_l, kt2_h, kt2_l, key3, e_h, e_l, d_scores, u_h, u_l, deltas, shares,
            shares_1,
        ),
        [whole_t, *pairs(2 * rows, width), *pairs(2 * rows, width)],
        [*pairs(2, 2 * rows, rows), *turned],
        limit=LIMITS[4], us=1,
    )
    pieces = [shape(width // PIECES, width)] * PIECES
    ht3_h, ht3_l, keep_1, *sends_1 = call(
        mix_kernel,
        (me, mixed_t, ht_h, ht_l, ht2_h, ht2_l, hidden3, dv_h, dv_l, dv3_h, dv3_l, cotangent),
        [*turned, shape(width, width), *pieces],
        [shape(width, width), shape(width, width)],
        scalars=1, limit=LIMITS[3], us=1,
    )
    others_1 = [swapped(send, 1) for send in sends_1]
    grad_q, grad_k, dq_h, dq_l = call(
        grad_kernel,
        (ht_h, ht_l, ht2_h, ht2_l, ht3_h, ht3_l, dq_t, dk_h, dk_l, dk3_h, dk3_l),
        [shape(width, width), shape(width, width), *pair],
        limit=LIMITS[5], us=1,
    )
    keep_2, *sends_2 = call(
        core_kernel, (me, grad_q, grad_k, keep_1, d_back), [shape(width, width), *pieces], scalars=1, limit=8, us=1
    )
    others_2 = [swapped(send, 1) for send in sends_2]

    def result_of(place):
        return call(result_kernel, (place, mixed_t, tokens, wo_h, wo_l), [whole, MARK], limit=LIMITS[3], us=1)

    def side_of(place):
        inputs = (place, d_back, dq_h, dq_l, dk_h, dk_l, dv_h, dv_l, wq_h, wq_l, *w_k, *w_v)
        return call(side_kernel, inputs, [whole, whole, MARK], limit=LIMITS[3], us=1)

    def tokens_of(place, d_own, d_other):
        inputs = (place, tokens, gain_row, cotangent, d_own, d_other)
        return call(tokens_kernel, inputs, [whole, MARK], limit=8)

    (grad_o, grad_v, grad_q, grad_k), d_gain, d_tokens, result = summed(
        me, keep_1, others_1, keep_2, others_2, (wv_h, wv_l, wq_h, wq_l, *w_k), gain_row, result_of, side_of, tokens_of
    )
    return (result, d_tokens, d_gain, grad_q, grad_k, grad_v, grad_o)


UNROLL = True
PIECES = 1
LIMITS = (8, 8, 8, 8, 8, 8)


def solution(mesh):
    tokens = P(("space", "slab"), None)
    return jax.shard_map(
        body,
        mesh=mesh,
        in_specs=(tokens, P(), P(), P(), P(), P(), tokens, P(("space", "slab")), tokens),
        out_specs=(tokens, tokens, P(), P(), P(), P(), P()),
        check_vma=False,
    )
```

```python
import functools

import jax
import jax.numpy as jnp
from jax import lax
from jax.experimental import pallas as pl
from jax.experimental.pallas import tpu as pltpu
from jax.sharding import PartitionSpec as P

HEADS = 8
PT = 128
HD = 64
PAIRS = HEADS // 2
F32 = jnp.float32
BF16 = jnp.bfloat16
NN = (((1,), (0,)), ((), ()))
NT = (((1,), (1,)), ((), ()))
VMEM = pl.BlockSpec(memory_space=pltpu.VMEM)
SMEM = pl.BlockSpec(memory_space=pltpu.SMEM)


def pair_of(x):
    high = x.astype(BF16)
    return high, (x - high.astype(F32)).astype(BF16)


def dot(left, right, dims=NN):
    return lax.dot_general(left, right, dims, preferred_element_type=F32)


def dot3(left, right, dims=NN):
    return dot(left[0], right[0], dims) + (dot(left[0], right[1], dims) + dot(left[1], right[0], dims))


def load(refs, *index):
    return refs[0][index], refs[1][index]


def store(refs, pair, *index):
    refs[0][index] = pair[0]
    refs[1][index] = pair[1]


def unit_rows(tokens):
    centred = tokens - jnp.mean(tokens, axis=1, keepdims=True)
    variance = jnp.mean(centred * centred, axis=1, keepdims=True)
    rstd = lax.rsqrt(variance + 1e-05)
    return centred * rstd, rstd


def store_stacked(ref, row, rows):
    count = rows.shape[0]
    left_half = lax.broadcasted_iota(jnp.int32, (count, 2 * HD), 1) < HD
    for p in range(PAIRS):
        part = rows[:, p * 2 * HD : (p + 1) * 2 * HD]
        swapped = pltpu.roll(part, HD, 1)
        for a in range(2):
            both = jnp.where(left_half == (a == 0), part, swapped)
            high, low = pair_of(both)
            base = (2 * p + a) * 4 * HD
            ref[pl.ds(row, count), base : base + 2 * HD] = high
            ref[pl.ds(row, count), base + 2 * HD : base + 4 * HD] = low


def store_interleaved(ref, columns):
    high, low = pair_of(columns)
    for h in range(HEADS):
        for i, piece in enumerate((high, low, high, low)):
            at = h * 4 * HD + i * HD
            ref[at : at + HD, :] = piece[h * HD : (h + 1) * HD]


def sums_of(left, right, dims=NN):
    return sum(dot3(a, b, dims) for a, b in zip(left[1:], right[1:], strict=True)) + dot3(left[0], right[0], dims)


def weight_kernel(_me, _parity, wq, wk, wv, wo, wq_h, wq_l, wk_h, wk_l, wv_h, wv_l, wo_h, wo_l):
    for source, high, low in ((wq, wq_h, wq_l), (wk, wk_h, wk_l), (wv, wv_h, wv_l), (wo, wo_h, wo_l)):
        store((high, low), pair_of(source[...]), ...)


def own_kernel(
    _, tokens, gain, cot, wq_h, wq_l, wk_h, wk_l, wv_h, wv_l, wo_h, wo_l,
    ht_h, ht_l, q_t, q_stack, k_stack, v_stack, kt_h, kt_l, vt_h, vt_l, d_mixed_t, d_stack,
):
    hidden = unit_rows(tokens[...])[0] * gain[...]
    store((ht_h, ht_l), pair_of(hidden.T), ...)
    rows = pair_of(hidden)
    query = dot3(rows, load((wq_h, wq_l), ...)) * HD ** (-0.5)
    q_t[...] = query.T
    store_interleaved(q_stack, q_t[...])
    key = dot3(rows, load((wk_h, wk_l), ...))
    store_stacked(k_stack, 0, key)
    store((kt_h, kt_l), pair_of(key.T), ...)
    value = dot3(rows, load((wv_h, wv_l), ...))
    store_stacked(v_stack, 0, value)
    store((vt_h, vt_l), pair_of(value.T), ...)
    d_mixed = dot3(load((wo_h, wo_l), ...), pair_of(cot[...]), NT)
    d_mixed_t[...] = d_mixed
    store_interleaved(d_stack, d_mixed)


def store_bias(bias, listed, counts, parity, patches):
    queries = bias.shape[1]
    lane = lax.broadcasted_iota(jnp.int32, (1, queries), 1)
    near = jnp.where(parity[0] == 0, 4, 0)
    windows = (2, 3, near, near + 1, 4 - near, 5 - near)
    for place in patches:
        level = []
        for p in range(2):
            live = jnp.int32(1 if place == p else 0)
            for j in range(listed.shape[1]):
                hit = jnp.logical_and(j < counts[0, p], listed[p, j] == windows[place])
                live = jnp.where(hit, 1, live)
            level.append(jnp.where(live == 1, 0.0, -1e30).astype(F32))
        bias[place : place + 1, :] = jnp.where(lane < PT, level[0], level[1])


def biased(scores, bias, first):
    count = scores.shape[0] // PT
    return jnp.concatenate(
        [scores[i * PT : (i + 1) * PT] + bias[first + i : first + i + 1, :] for i in range(count)], axis=0
    )


def key_side(patches, gain, wk, wv, k_stack, v_stack, vt):
    hidden = jnp.concatenate([unit_rows(tokens[...])[0] * gain[...] for tokens in patches], axis=0)
    rows = pair_of(hidden)
    key = dot3(rows, load(wk, ...))
    store_stacked(k_stack, 0, key)
    value = dot3(rows, load(wv, ...))
    store_stacked(v_stack, 0, value)
    store(vt, pair_of(value.T), ...)
    return hidden, key


def head_rows(h):
    return pl.ds(pl.multiple_of(h * HD, HD), HD)


def head_stack(h):
    return pl.ds(pl.multiple_of(h * 4 * HD, 4 * HD), 4 * HD)


def weighed(highs, lows, rows, right):
    high = jnp.concatenate([r[rows, :] for r in highs], axis=1)
    low = jnp.concatenate([r[rows, :] for r in lows], axis=1)
    left = jnp.concatenate([high, low], axis=0)
    both = dot(left, right[0]) + dot(left, right[1])
    return both[:HD] + both[HD:]


def near_side_kernel(
    patch_0, patch_1, gain, wk_h, wk_l, wv_h, wv_l,
    ht_h, ht_l, kt_h, kt_l, k_stack, v_stack, vt_h, vt_l,
):
    hidden, key = key_side((patch_0, patch_1), gain, (wk_h, wk_l), (wv_h, wv_l), k_stack, v_stack, (vt_h, vt_l))
    store((ht_h, ht_l), pair_of(hidden.T), ...)
    store((kt_h, kt_l), pair_of(key.T), ...)


def near_kernel(
    parity, listed, counts, _, q_stack, k_stack, v_stack, vt_h, vt_l, d_stack, k_near, v_near, vt2_h, vt2_l,
    e_h, e_l, d_scores, mixed, tops, totals,
    bias,
):
    store_bias(bias, listed, counts, parity, range(4))

    def one_head(h, carry):
        stack, rows = head_stack(h), head_rows(h)
        q_now, d_now = q_stack[stack, :], d_stack[stack, :]
        scores = jnp.concatenate(
            [biased(dot(k_stack[:, stack], q_now), bias, 0), biased(dot(k_near[:, stack], q_now), bias, 2)], axis=0
        )
        top = jnp.max(scores, axis=0, keepdims=True)
        weights = jnp.exp(scores - top)
        tops[pl.ds(h, 1), :] = top
        totals[pl.ds(h, 1), :] = jnp.sum(weights, axis=0, keepdims=True)
        pair = pair_of(weights)
        e_h[h] = pair[0]
        e_l[h] = pair[1]
        mixed[rows, :] = weighed((vt_h, vt2_h), (vt_l, vt2_l), rows, pair)
        d_scores[h] = jnp.concatenate([dot(v_stack[:, stack], d_now), dot(v_near[:, stack], d_now)], axis=0)
        return carry

    lax.fori_loop(0, HEADS, one_head, 0, unroll=UNROLL)


def gathered(left_h, left_l, right):
    left_half = lax.broadcasted_iota(jnp.int32, right[0].shape, 1) < HD
    zero = jnp.zeros_like(right[0])
    one = [jnp.where(left_half, x, zero) for x in right]
    two = [jnp.where(left_half, zero, x) for x in right]
    one, two = jnp.concatenate(one, axis=1), jnp.concatenate(two, axis=1)
    wide = (dot(left_h[0], one) + dot(left_h[1], two)) + (dot(left_l[0], one) + dot(left_l[1], two))
    return wide[:, : 2 * HD] + wide[:, 2 * HD :]


def pair_lanes(p):
    return pl.ds(pl.multiple_of(p * 2 * HD, 2 * HD), 2 * HD)


def kept_and_sent(me, pair, keep, sends):
    rows = sends[0].shape[0]
    for bit in range(2):

        @pl.when(me[0] % 2 == bit)
        def _():
            keep[...] = pair[bit][...]
            for i, send in enumerate(sends):
                send[...] = pair[1 - bit][i * rows : (i + 1) * rows, :]


def far_kernel(
    parity, listed, counts, patch_0, patch_1, gain, q_t, q_stack, d_mixed_t, d_stack, mixed_1, tops, totals,
    wk_h, wk_l, wv_h, wv_l,
    hidden, key, u_h, u_l, mixed_t, deltas, shares, shares_1, dk_h, dk_l, dv_h, dv_l, d_far,
    bias, k_far, v_far, vt_h, vt_l, e_h, e_l,
):
    store_bias(bias, listed, counts, parity, range(4, 6))
    hidden[...], key[...] = key_side(
        (patch_0, patch_1), gain, (wk_h, wk_l), (wv_h, wv_l), k_far, v_far, (vt_h, vt_l)
    )

    def one_pair(p, carry):
        d_scaled, q_scaled = [], []
        for a in range(2):
            h = 2 * p + a
            stack, rows, row = head_stack(h), head_rows(h), pl.ds(h, 1)
            scores = biased(dot(k_far[:, stack], q_stack[stack, :]), bias, 4)
            top_1 = tops[row, :]
            top = jnp.maximum(top_1, jnp.max(scores, axis=0, keepdims=True))
            weights = jnp.exp(scores - top)
            shrink = jnp.exp(top_1 - top)
            share = 1.0 / (shrink * totals[row, :] + jnp.sum(weights, axis=0, keepdims=True))
            share_1 = shrink * share
            pair = pair_of(weights)
            e_h[a] = pair[0]
            e_l[a] = pair[1]
            mixed = share_1 * mixed_1[rows, :] + share * weighed((vt_h,), (vt_l,), rows, pair)
            mixed_t[rows, :] = mixed
            d_mixed = d_mixed_t[rows, :]
            delta = jnp.sum(d_mixed * mixed, axis=0, keepdims=True)
            deltas[row, :] = delta
            shares[row, :] = share
            shares_1[row, :] = share_1
            pair = pair_of(weights * (dot(v_far[:, stack], d_stack[stack, :]) - delta))
            u_h[h] = pair[0]
            u_l[h] = pair[1]
            d_scaled.append(d_mixed * share)
            q_scaled.append(q_t[rows, :] * share)
        lanes = pair_lanes(p)
        right = pair_of(jnp.concatenate(d_scaled, axis=0).T)
        d_value = gathered((e_h[0], e_h[1]), (e_l[0], e_l[1]), right)
        store((dv_h, dv_l), pair_of(d_value), slice(None), lanes)
        right = pair_of(jnp.concatenate(q_scaled, axis=0).T)
        d_key = gathered((u_h[2 * p], u_h[2 * p + 1]), (u_l[2 * p], u_l[2 * p + 1]), right)
        store((dk_h, dk_l), pair_of(d_key), slice(None), lanes)
        return carry

    lax.fori_loop(0, PAIRS, one_pair, 0, unroll=UNROLL)
    d_far[...] = sums_of(
        [load((dk_h, dk_l), ...), load((dv_h, dv_l), ...)], [load((wk_h, wk_l), ...), load((wv_h, wv_l), ...)], NT
    )


def back_kernel(
    q_t, d_mixed_t, kt_h, kt_l, kt2_h, kt2_l, key3, e_h, e_l, d_scores, u_h, u_l, deltas, shares, shares_1,
    dq_t, dk_h, dk_l, dv_h, dv_l,
    s_h, s_l, kt3_h, kt3_l,
):
    store((kt3_h, kt3_l), pair_of(key3[...].T), ...)

    def one_pair(p, carry):
        q_scaled, d_scaled = [], []
        for a in range(2):
            h = 2 * p + a
            rows, row = head_rows(h), pl.ds(h, 1)
            weights = e_h[h].astype(F32) + e_l[h].astype(F32)
            pair = pair_of(weights * (d_scores[h] - deltas[row, :]))
            s_h[a] = pair[0]
            s_l[a] = pair[1]
            share_1 = shares_1[row, :]
            one = weighed((kt_h, kt2_h), (kt_l, kt2_l), rows, pair)
            two = weighed((kt3_h,), (kt3_l,), rows, (u_h[h], u_l[h]))
            dq_t[rows, :] = (share_1 * one + shares[row, :] * two) * HD ** (-0.5)
            q_scaled.append(q_t[rows, :] * share_1)
            d_scaled.append(d_mixed_t[rows, :] * share_1)
        lanes = pair_lanes(p)
        right = pair_of(jnp.concatenate(q_scaled, axis=0).T)
        d_key = gathered((s_h[0], s_h[1]), (s_l[0], s_l[1]), right)
        store((dk_h, dk_l), pair_of(d_key), slice(None), lanes)
        right = pair_of(jnp.concatenate(d_scaled, axis=0).T)
        d_value = gathered((e_h[2 * p], e_h[2 * p + 1]), (e_l[2 * p], e_l[2 * p + 1]), right)
        store((dv_h, dv_l), pair_of(d_value), slice(None), lanes)
        return carry

    lax.fori_loop(0, PAIRS, one_pair, 0, unroll=UNROLL)


def mix_kernel(
    me, mixed_t, ht_h, ht_l, ht2_h, ht2_l, hidden3, dv_h, dv_l, dv3_h, dv3_l, cot, ht3_h, ht3_l, keep, *refs
):
    *sends, grad_o, grad_v = refs
    own = cot.shape[0]
    store((ht3_h, ht3_l), pair_of(hidden3[...].T), ...)
    grad_o[...] = dot3(pair_of(mixed_t[...]), pair_of(cot[...]))
    turned = [load(t, ...) for t in ((ht_h, ht_l), (ht2_h, ht2_l), (ht3_h, ht3_l))]
    d_values = [load((dv_h, dv_l), slice(0, own)), load((dv_h, dv_l), slice(own, 2 * own)), load((dv3_h, dv3_l), ...)]
    grad_v[...] = sums_of(turned, d_values)
    kept_and_sent(me, (grad_o, grad_v), keep, sends)


def result_kernel(_, mixed_t, tokens, wo_h, wo_l, result, mark):
    mark[...] = jnp.zeros_like(mark)
    result[...] = dot3(pair_of(mixed_t[...].T), load((wo_h, wo_l), ...)) + tokens[...]


def grad_kernel(
    ht_h, ht_l, ht2_h, ht2_l, ht3_h, ht3_l, dq_t, dk_h, dk_l, dk3_h, dk3_l,
    grad_q, grad_k, dq_h, dq_l,
):
    own = dq_h.shape[0]
    d_query = pair_of(dq_t[...].T)
    store((dq_h, dq_l), d_query, ...)
    turned = [load(t, ...) for t in ((ht_h, ht_l), (ht2_h, ht2_l), (ht3_h, ht3_l))]
    d_keys = [load((dk_h, dk_l), slice(0, own)), load((dk_h, dk_l), slice(own, 2 * own)), load((dk3_h, dk3_l), ...)]
    grad_q[...] = dot3(turned[0], d_query)
    grad_k[...] = sums_of(turned, d_keys)


def core_kernel(me, grad_q, grad_k, _keep, keep, *sends):
    kept_and_sent(me, (grad_q, grad_k), keep, sends)


def arrive_kernel(a, out, mark):
    mark[...] = jnp.zeros_like(mark)
    out[...] = a[...]


def side_kernel(
    _, d_back, dq_h, dq_l, dk_h, dk_l, dv_h, dv_l, wq_h, wq_l, wk_h, wk_l, wv_h, wv_l,
    d_given, d_own, mark,
):
    mark[...] = jnp.zeros_like(mark)
    own = d_own.shape[0]
    first, near = slice(0, own), slice(own, 2 * own)
    w_q, w_k, w_v = load((wq_h, wq_l), ...), load((wk_h, wk_l), ...), load((wv_h, wv_l), ...)
    d_given[...] = d_back[...] + sums_of(
        [load((dk_h, dk_l), near), load((dv_h, dv_l), near)], [w_k, w_v], NT
    )
    d_own[...] = sums_of(
        [load((dq_h, dq_l), ...), load((dk_h, dk_l), first), load((dv_h, dv_l), first)], [w_q, w_k, w_v], NT
    )


def half_of(me, mask, mine, rows):
    index = (me[0] // mask) % 2
    return pl.ds(pl.multiple_of((index if mine else 1 - index) * rows, 8), rows)


def add_kernel(a, b, out, *_):
    out[...] = a[...] + b[...]


def cut_kernel(masks, me, keep_1, keep_2, _, *refs):
    others, outs, sums = refs[: 2 * PIECES], refs[2 * PIECES : -1], refs[-1]
    rows = others[0].shape[0]
    for i, other in enumerate(others):
        keep = (keep_1, keep_2)[i // PIECES]
        first = i % PIECES * rows
        sums[i * rows : (i + 1) * rows, :] = keep[first : first + rows, :] + other[...]
    at = 0
    for i, mask in enumerate(masks):
        rows = outs[2 * i].shape[0]
        for out, mine in ((outs[2 * i], True), (outs[2 * i + 1], False)):
            index = (me[0] // mask) % 2
            start = at + (index if mine else 1 - index) * rows
            out[...] = sums[pl.ds(pl.multiple_of(start, 8), rows), :]
        at += 2 * rows


def halve_kernel(mask, me, keep, other, *rest):
    next_keep, next_send = rest[-2:]
    rows = next_keep.shape[0]
    for out, mine in ((next_keep, True), (next_send, False)):
        at = half_of(me, mask, mine, rows)
        out[...] = keep[at, :] + other[at, :]


def first_kernel(a, b, d_given, out, d_going):
    out[...] = a[...] + b[...]
    d_going[...] = d_given[...]


def last_kernel(a, b, *rest):
    rest[-1][...] = a[...] + b[...]


def double_kernel(mask, me, mine, other, *rest):
    out = rest[-1]
    rows = mine.shape[0]
    out[half_of(me, mask, True, rows), :] = mine[...]
    out[half_of(me, mask, False, rows), :] = other[...]


def write_kernel(ranges, core, me, gain, wv_h, wv_l, wq_h, wq_l, wk_h, wk_l, *refs):
    parts, refs = refs[:3], refs[3:]
    before = refs[4] if core else None
    refs = refs[5 * core :]
    outs, last, (partial, total, sent) = refs[:4], refs[4], refs[5:] if core else (refs[4], None, refs[5])
    weights = (None, (wv_h, wv_l), (wq_h, wq_l), (wk_h, wk_l))
    lanes = partial.shape[1]
    partial[...] = before[...] if core else jnp.zeros_like(partial)
    for bit in range(2):

        @pl.when(me[0] % 2 == bit)
        def _():
            pieces = [
                (parts[i].at[pl.ds(first, rows)], 2 * exchange + (bit + core) % 2, to, rows)
                for i, first, rows, exchange, to in ranges
            ]
            copies = [
                pltpu.make_async_copy(piece, outs[matrix].at[pl.ds(to, rows)], sent.at[n])
                for n, (piece, matrix, to, rows) in enumerate(pieces)
            ]
            for copy in copies:
                copy.start()
            for piece, matrix, to, rows in pieces:
                if matrix:
                    high, low = weights[matrix]
                    for lane in range(0, piece.shape[1], lanes):
                        at = (slice(to, to + rows), slice(lane, lane + lanes))
                        weight = high[at].astype(F32) + low[at].astype(F32)
                        partial[to : to + rows, :] += weight * piece[:, lane : lane + lanes]
            if core:
                total[...] = jnp.sum(partial[...].T, axis=0, keepdims=True) / gain[...]
                copies.append(pltpu.make_async_copy(total, last, sent.at[len(copies)]))
                copies[-1].start()
            for copy in copies:
                copy.wait()


def written(me, gain, weights, parts, ranges, count, core, held=()):
    width = parts[0].shape[1]
    anywhere = pl.BlockSpec(memory_space=pl.ANY)
    partial = shape(count, 128)
    semaphores = pltpu.SemaphoreType.DMA((len(ranges) + core,))
    return pl.pallas_call(
        functools.partial(write_kernel, ranges, core),
        out_shape=[shape(count, width)] * 4 + [shape(1, width) if core else partial],
        in_specs=[SMEM] + [VMEM] * 10 + ([anywhere] * 4 + [VMEM] if core else []),
        out_specs=[anywhere] * 4 + [anywhere if core else VMEM],
        scratch_shapes=([pltpu.VMEM(partial.shape, F32), pltpu.VMEM((1, width), F32)] if core else []) + [semaphores],
        input_output_aliases={11 + i: i for i in range(4)} if core else {},
        compiler_params=pltpu.CompilerParams(vmem_limit_bytes=2**23),
        cost_estimate=pl.CostEstimate(flops=10**9, bytes_accessed=0, transcendentals=0),
    )(me, gain, *weights, *parts, *held)


def tokens_kernel(_, tokens, gain, cot, d_own, d_other, out, mark):
    mark[...] = jnp.zeros_like(mark)
    normal, rstd = unit_rows(tokens[...])
    d_normal = (d_own[...] + d_other[...]) * gain[...]
    inner = jnp.mean(d_normal * normal, axis=1, keepdims=True)
    centre = jnp.mean(d_normal, axis=1, keepdims=True)
    out[...] = (d_normal - centre - normal * inner) * rstd + cot[...]


def shape(*dims, dtype=F32):
    return jax.ShapeDtypeStruct(dims, dtype)


def pairs(*dims):
    return [shape(*dims, dtype=BF16)] * 2


def call(kernel, inputs, outputs, scratch=(), scalars=0, limit=4, us=1):
    return pl.pallas_call(
        kernel,
        out_shape=outputs,
        in_specs=[SMEM] * scalars + [VMEM] * (len(inputs) - scalars),
        out_specs=[VMEM] * len(outputs),
        scratch_shapes=[pltpu.VMEM(s.shape, s.dtype) for s in scratch],
        compiler_params=pltpu.CompilerParams(vmem_limit_bytes=limit * 2**20),
        cost_estimate=pl.CostEstimate(flops=int(us * 10**9), bytes_accessed=0, transcendentals=0),
    )(*inputs)


MARK = shape(8, 128)


def along_space(value, target):
    count = lax.axis_size("space")
    return lax.ppermute(value, "space", [(i, target(i) % count) for i in range(count)])


def across(value):
    return along_space(value, lambda i: i ^ 1)


def onward(value):
    return along_space(value, lambda i: i + 2 - 4 * (i % 2))


def homeward(value):
    return along_space(value, lambda i: i - 2 + 4 * (i % 2))


def devices():
    return lax.axis_size("space") * lax.axis_size("slab")


def swapped(value, mask):
    return lax.ppermute(value, ("space", "slab"), [(i, i ^ mask) for i in range(devices())])


ORDERS = ((4, 2, 8), (2, 8, 4), (8, 4, 2))
LAST = 16


def summed(me, keep_1, others_1, keep_2, others_2, mark, weights, gain, result_of, side_of, tokens_of):
    count, width = keep_1.shape
    total = 2 * count
    unit = 8 * 8
    sizes = [total // unit // 3 * unit] * 2
    sizes.append(total - sum(sizes))
    parts = call(
        functools.partial(cut_kernel, [order[0] for order in ORDERS]),
        (me, keep_1, keep_2, mark, *others_1, *others_2),
        [shape(size // 2, width) for size in sizes for _ in range(2)],
        [shape(total, width)],
        scalars=1, limit=8,
    )
    d_given, d_own, mark = side_of(parts[0])
    parts = [[parts[2 * i], swapped(parts[2 * i + 1], ORDERS[i][0])] for i in range(3)]
    for step in (1, 2):
        for i in range(3):
            half, mask = shape(sizes[i] >> (step + 1), width), ORDERS[i][step]
            place = (mark,) if step == 1 else ()
            keep, send = call(
                functools.partial(halve_kernel, mask), (me, *parts[i], *place), [half, half], scalars=1
            )
            parts[i] = [keep, swapped(send, mask)]
    for i in (0, 2, 1):
        if i == 1:
            part, d_going = call(first_kernel, (*parts[i], d_given), [parts[i][0], d_given])
            d_other = across(d_going)
        else:
            (part,) = call(add_kernel, parts[i], [parts[i][0]])
        if i == 0:
            result, mark = result_of(part)
        mask, other = LAST, swapped(part, LAST)
        while 2 * mask < devices():
            (part,) = call(add_kernel, (part, other), [part])
            mask *= 2
            other = swapped(part, mask)
        place = (mark,) if i == 1 else ()
        (parts[i],) = call(last_kernel, (part, other, *place), [part])
    for step in (2, 1, 0):
        for i in range(3):
            mask = ORDERS[i][step]
            place = {(2, 1): (d_other,), (0, 2): (mark,)}.get((step, i), ())
            (parts[i],) = call(
                functools.partial(double_kernel, mask), (me, parts[i], swapped(parts[i], mask), *place),
                [shape(2 * parts[i].shape[0], width)], scalars=1,
            )
        if step == 1:
            d_tokens, mark = tokens_of(parts[0], d_own, d_other)
    others = [swapped(part, 1) for part in parts]
    ranges, at = [], 0
    for i, size in enumerate(sizes):
        for exchange in range(2):
            start, stop = max(at, exchange * count), min(at + size, (exchange + 1) * count)
            if start < stop:
                ranges.append((i, start - at, stop - start, exchange, start - exchange * count))
        at += size
    held = written(me, gain, weights, parts, ranges, count, 0)
    *gradients, d_gain = written(me, gain, weights, others, ranges, count, 1, held)
    return gradients, d_gain.reshape(width), d_tokens, result


def body(tokens, gain, wq, wk, wv, wo, neighbour_list, neighbour_count, cotangent):
    rows, width = tokens.shape
    me = (lax.axis_index("space") * lax.axis_size("slab") + lax.axis_index("slab")).astype(jnp.int32)[None]
    parity = (lax.axis_index("space") % 2).astype(jnp.int32)[None]
    counts = neighbour_count[None, :]
    near = [across(tokens[i * PT : (i + 1) * PT]) for i in range(2)]
    far = [onward(near[0])]
    gain_row = gain[None, :]
    stack_rows, stack_columns = shape(HEADS * 4 * HD, rows, dtype=BF16), shape(rows, HEADS * 4 * HD, dtype=BF16)
    turned, square, pair = pairs(width, rows), pairs(width, width), pairs(rows, width)
    whole, whole_t, scalars = shape(rows, width), shape(width, rows), shape(HEADS, rows)
    weights = call(weight_kernel, (me, parity, wq, wk, wv, wo), square * 4, scalars=2, limit=20)
    wq_h, wq_l, wk_h, wk_l, wv_h, wv_l, wo_h, wo_l = weights
    (
        ht_h, ht_l, q_t, q_stack, k_stack, v_stack, kt_h, kt_l, vt_h, vt_l, d_mixed_t, d_stack,
    ) = call(
        own_kernel,
        (near[0], tokens, gain_row, cotangent, *weights),
        [*turned, whole_t, stack_rows, stack_columns, stack_columns, *turned, *turned, whole_t, stack_rows],
        limit=LIMITS[0], us=1,
    )
    near[1], q_stack = lax.optimization_barrier((near[1], q_stack))
    far.append(onward(near[1]))
    w_k, w_v = (wk_h, wk_l), (wv_h, wv_l)
    ht2_h, ht2_l, kt2_h, kt2_l, k_near, v_near, vt2_h, vt2_l = call(
        near_side_kernel,
        (*near, gain_row, *w_k, *w_v),
        [*turned, *turned, stack_columns, stack_columns, *turned],
        limit=LIMITS[1], us=1,
    )
    e_h, e_l, d_scores, mixed, tops, totals = call(
        near_kernel,
        (
            parity, neighbour_list, counts, far[0], q_stack, k_stack, v_stack, vt_h, vt_l, d_stack, k_near, v_near,
            vt2_h, vt2_l,
        ),
        [*pairs(HEADS, 2 * rows, rows), shape(HEADS, 2 * rows, rows), whole_t, scalars, scalars],
        [shape(8, rows)],
        scalars=3, limit=LIMITS[1], us=1,
    )
    (
        hidden3, key3, u_h, u_l, mixed_t, deltas, shares, shares_1, dk3_h, dk3_l, dv3_h, dv3_l,
        d_far,
    ) = call(
        far_kernel,
        (
            parity, neighbour_list, counts, *far, gain_row, q_t, q_stack, d_mixed_t, d_stack, mixed, tops, totals,
            *w_k, *w_v,
        ),
        [
            whole, whole, *pairs(HEADS, rows, rows), whole_t, scalars, scalars, scalars, *pair, *pair,
            whole,
        ],
        [shape(8, rows), stack_columns, stack_columns, *turned, *pairs(2, rows, rows)],
        scalars=3, limit=LIMITS[2], us=1,
    )
    d_back = homeward(d_far)
    dq_t, dk_h, dk_l, dv_h, dv_l = call(
        back_kernel,
        (
            q_t, d_mixed_t, kt_h, kt_l, kt2_h, kt2_l, key3, e_h, e_l, d_scores, u_h, u_l, deltas, shares,
            shares_1,
        ),
        [whole_t, *pairs(2 * rows, width), *pairs(2 * rows, width)],
        [*pairs(2, 2 * rows, rows), *turned],
        limit=LIMITS[4], us=0.001,
    )
    pieces = [shape(width // PIECES, width)] * PIECES
    ht3_h, ht3_l, keep_1, *sends_1 = call(
        mix_kernel,
        (me, mixed_t, ht_h, ht_l, ht2_h, ht2_l, hidden3, dv_h, dv_l, dv3_h, dv3_l, cotangent),
        [*turned, shape(width, width), *pieces],
        [shape(width, width), shape(width, width)],
        scalars=1, limit=LIMITS[3], us=0.001,
    )
    others_1 = [swapped(send, 1) for send in sends_1]
    grad_q, grad_k, dq_h, dq_l = call(
        grad_kernel,
        (ht_h, ht_l, ht2_h, ht2_l, ht3_h, ht3_l, dq_t, dk_h, dk_l, dk3_h, dk3_l),
        [shape(width, width), shape(width, width), *pair],
        limit=LIMITS[5], us=0.001,
    )
    keep_2, *sends_2 = call(
        core_kernel, (me, grad_q, grad_k, keep_1), [shape(width, width), *pieces], scalars=1, limit=8, us=0.001
    )
    others_2 = [swapped(send, 1) for send in sends_2]
    d_back, mark = call(arrive_kernel, (d_back,), [whole, MARK], us=20)

    def result_of(place):
        return call(result_kernel, (place, mixed_t, tokens, wo_h, wo_l), [whole, MARK], limit=LIMITS[3], us=1)

    def side_of(place):
        inputs = (place, d_back, dq_h, dq_l, dk_h, dk_l, dv_h, dv_l, wq_h, wq_l, *w_k, *w_v)
        return call(side_kernel, inputs, [whole, whole, MARK], limit=LIMITS[3], us=1)

    def tokens_of(place, d_own, d_other):
        inputs = (place, tokens, gain_row, cotangent, d_own, d_other)
        return call(tokens_kernel, inputs, [whole, MARK], limit=8)

    (grad_o, grad_v, grad_q, grad_k), d_gain, d_tokens, result = summed(
        me, keep_1, others_1, keep_2, others_2, mark, (wv_h, wv_l, wq_h, wq_l, *w_k), gain_row, result_of, side_of, tokens_of
    )
    return (result, d_tokens, d_gain, grad_q, grad_k, grad_v, grad_o)


UNROLL = True
PIECES = 1
LIMITS = (8, 8, 8, 8, 8, 8)


def solution(mesh):
    tokens = P(("space", "slab"), None)
    return jax.shard_map(
        body,
        mesh=mesh,
        in_specs=(tokens, P(), P(), P(), P(), P(), tokens, P(("space", "slab")), tokens),
        out_specs=(tokens, tokens, P(), P(), P(), P(), P()),
        check_vma=False,
    )
```

```python
import functools

import jax
import jax.numpy as jnp
from jax import lax
from jax.experimental import pallas as pl
from jax.experimental.pallas import tpu as pltpu
from jax.sharding import PartitionSpec as P

HEADS = 8
PT = 128
HD = 64
PAIRS = HEADS // 2
F32 = jnp.float32
BF16 = jnp.bfloat16
NN = (((1,), (0,)), ((), ()))
NT = (((1,), (1,)), ((), ()))
VMEM = pl.BlockSpec(memory_space=pltpu.VMEM)
SMEM = pl.BlockSpec(memory_space=pltpu.SMEM)


def pair_of(x):
    high = x.astype(BF16)
    return high, (x - high.astype(F32)).astype(BF16)


def dot(left, right, dims=NN):
    return lax.dot_general(left, right, dims, preferred_element_type=F32)


def dot3(left, right, dims=NN):
    return dot(left[0], right[0], dims) + (dot(left[0], right[1], dims) + dot(left[1], right[0], dims))


def load(refs, *index):
    return refs[0][index], refs[1][index]


def store(refs, pair, *index):
    refs[0][index] = pair[0]
    refs[1][index] = pair[1]


def unit_rows(tokens):
    centred = tokens - jnp.mean(tokens, axis=1, keepdims=True)
    variance = jnp.mean(centred * centred, axis=1, keepdims=True)
    rstd = lax.rsqrt(variance + 1e-05)
    return centred * rstd, rstd


def store_stacked(ref, row, rows):
    count = rows.shape[0]
    left_half = lax.broadcasted_iota(jnp.int32, (count, 2 * HD), 1) < HD
    for p in range(PAIRS):
        part = rows[:, p * 2 * HD : (p + 1) * 2 * HD]
        swapped = pltpu.roll(part, HD, 1)
        for a in range(2):
            both = jnp.where(left_half == (a == 0), part, swapped)
            high, low = pair_of(both)
            base = (2 * p + a) * 4 * HD
            ref[pl.ds(row, count), base : base + 2 * HD] = high
            ref[pl.ds(row, count), base + 2 * HD : base + 4 * HD] = low


def store_interleaved(ref, columns):
    high, low = pair_of(columns)
    for h in range(HEADS):
        for i, piece in enumerate((high, low, high, low)):
            at = h * 4 * HD + i * HD
            ref[at : at + HD, :] = piece[h * HD : (h + 1) * HD]


def sums_of(left, right, dims=NN):
    return sum(dot3(a, b, dims) for a, b in zip(left[1:], right[1:], strict=True)) + dot3(left[0], right[0], dims)


def weight_kernel(_me, _parity, wq, wk, wv, wo, wq_h, wq_l, wk_h, wk_l, wv_h, wv_l, wo_h, wo_l):
    for source, high, low in ((wq, wq_h, wq_l), (wk, wk_h, wk_l), (wv, wv_h, wv_l), (wo, wo_h, wo_l)):
        store((high, low), pair_of(source[...]), ...)


def own_kernel(
    _, tokens, gain, cot, wq_h, wq_l, wk_h, wk_l, wv_h, wv_l, wo_h, wo_l,
    ht_h, ht_l, q_t, q_stack, k_stack, v_stack, kt_h, kt_l, vt_h, vt_l, d_mixed_t, d_stack,
):
    hidden = unit_rows(tokens[...])[0] * gain[...]
    store((ht_h, ht_l), pair_of(hidden.T), ...)
    rows = pair_of(hidden)
    query = dot3(rows, load((wq_h, wq_l), ...)) * HD ** (-0.5)
    q_t[...] = query.T
    store_interleaved(q_stack, q_t[...])
    key = dot3(rows, load((wk_h, wk_l), ...))
    store_stacked(k_stack, 0, key)
    store((kt_h, kt_l), pair_of(key.T), ...)
    value = dot3(rows, load((wv_h, wv_l), ...))
    store_stacked(v_stack, 0, value)
    store((vt_h, vt_l), pair_of(value.T), ...)
    d_mixed = dot3(load((wo_h, wo_l), ...), pair_of(cot[...]), NT)
    d_mixed_t[...] = d_mixed
    store_interleaved(d_stack, d_mixed)


def store_bias(bias, listed, counts, parity, patches):
    queries = bias.shape[1]
    lane = lax.broadcasted_iota(jnp.int32, (1, queries), 1)
    near = jnp.where(parity[0] == 0, 4, 0)
    windows = (2, 3, near, near + 1, 4 - near, 5 - near)
    for place in patches:
        level = []
        for p in range(2):
            live = jnp.int32(1 if place == p else 0)
            for j in range(listed.shape[1]):
                hit = jnp.logical_and(j < counts[0, p], listed[p, j] == windows[place])
                live = jnp.where(hit, 1, live)
            level.append(jnp.where(live == 1, 0.0, -1e30).astype(F32))
        bias[place : place + 1, :] = jnp.where(lane < PT, level[0], level[1])


def biased(scores, bias, first):
    count = scores.shape[0] // PT
    return jnp.concatenate(
        [scores[i * PT : (i + 1) * PT] + bias[first + i : first + i + 1, :] for i in range(count)], axis=0
    )


def key_side(patches, gain, wk, wv, k_stack, v_stack, vt):
    hidden = jnp.concatenate([unit_rows(tokens[...])[0] * gain[...] for tokens in patches], axis=0)
    rows = pair_of(hidden)
    key = dot3(rows, load(wk, ...))
    store_stacked(k_stack, 0, key)
    value = dot3(rows, load(wv, ...))
    store_stacked(v_stack, 0, value)
    store(vt, pair_of(value.T), ...)
    return hidden, key


def head_rows(h):
    return pl.ds(pl.multiple_of(h * HD, HD), HD)


def head_stack(h):
    return pl.ds(pl.multiple_of(h * 4 * HD, 4 * HD), 4 * HD)


def weighed(highs, lows, rows, right):
    high = jnp.concatenate([r[rows, :] for r in highs], axis=1)
    low = jnp.concatenate([r[rows, :] for r in lows], axis=1)
    left = jnp.concatenate([high, low], axis=0)
    both = dot(left, right[0]) + dot(left, right[1])
    return both[:HD] + both[HD:]


def near_side_kernel(
    patch_0, patch_1, gain, wk_h, wk_l, wv_h, wv_l,
    ht_h, ht_l, kt_h, kt_l, k_stack, v_stack, vt_h, vt_l,
):
    hidden, key = key_side((patch_0, patch_1), gain, (wk_h, wk_l), (wv_h, wv_l), k_stack, v_stack, (vt_h, vt_l))
    store((ht_h, ht_l), pair_of(hidden.T), ...)
    store((kt_h, kt_l), pair_of(key.T), ...)


def near_kernel(
    parity, listed, counts, _, q_stack, k_stack, v_stack, vt_h, vt_l, d_stack, k_near, v_near, vt2_h, vt2_l,
    e_h, e_l, d_scores, mixed, tops, totals,
    bias,
):
    store_bias(bias, listed, counts, parity, range(4))

    def one_head(h, carry):
        stack, rows = head_stack(h), head_rows(h)
        q_now, d_now = q_stack[stack, :], d_stack[stack, :]
        scores = jnp.concatenate(
            [biased(dot(k_stack[:, stack], q_now), bias, 0), biased(dot(k_near[:, stack], q_now), bias, 2)], axis=0
        )
        top = jnp.max(scores, axis=0, keepdims=True)
        weights = jnp.exp(scores - top)
        tops[pl.ds(h, 1), :] = top
        totals[pl.ds(h, 1), :] = jnp.sum(weights, axis=0, keepdims=True)
        pair = pair_of(weights)
        e_h[h] = pair[0]
        e_l[h] = pair[1]
        mixed[rows, :] = weighed((vt_h, vt2_h), (vt_l, vt2_l), rows, pair)
        d_scores[h] = jnp.concatenate([dot(v_stack[:, stack], d_now), dot(v_near[:, stack], d_now)], axis=0)
        return carry

    lax.fori_loop(0, HEADS, one_head, 0, unroll=UNROLL)


def gathered(left_h, left_l, right):
    left_half = lax.broadcasted_iota(jnp.int32, right[0].shape, 1) < HD
    zero = jnp.zeros_like(right[0])
    one = [jnp.where(left_half, x, zero) for x in right]
    two = [jnp.where(left_half, zero, x) for x in right]
    one, two = jnp.concatenate(one, axis=1), jnp.concatenate(two, axis=1)
    wide = (dot(left_h[0], one) + dot(left_h[1], two)) + (dot(left_l[0], one) + dot(left_l[1], two))
    return wide[:, : 2 * HD] + wide[:, 2 * HD :]


def pair_lanes(p):
    return pl.ds(pl.multiple_of(p * 2 * HD, 2 * HD), 2 * HD)


def kept_and_sent(me, pair, keep, sends):
    rows = sends[0].shape[0]
    for bit in range(2):

        @pl.when(me[0] % 2 == bit)
        def _():
            keep[...] = pair[bit][...]
            for i, send in enumerate(sends):
                send[...] = pair[1 - bit][i * rows : (i + 1) * rows, :]


def far_side_kernel(
    _, patch, gain, wk_h, wk_l, wv_h, wv_l,
    hidden, key, k_stack, v_stack, vt_h, vt_l,
):
    hidden[...], key[...] = key_side((patch,), gain, (wk_h, wk_l), (wv_h, wv_l), k_stack, v_stack, (vt_h, vt_l))


def far_kernel(
    parity, listed, counts, hidden_0, key_0, k_far_0, v_far_0, vt_0_h, vt_0_l, patch_1, gain, q_t, q_stack, d_mixed_t, d_stack, mixed_1, tops, totals,
    wk_h, wk_l, wv_h, wv_l,
    hidden, key, u_h, u_l, mixed_t, deltas, shares, shares_1, dk_h, dk_l, dv_h, dv_l, d_far,
    bias, k_far, v_far, vt_h, vt_l, e_h, e_l,
):
    store_bias(bias, listed, counts, parity, range(4, 6))
    hidden[:PT, :], key[:PT, :] = hidden_0[...], key_0[...]
    hidden[PT:, :], key[PT:, :] = key_side(
        (patch_1,), gain, (wk_h, wk_l), (wv_h, wv_l), k_far, v_far, (vt_h, vt_l)
    )

    def both_patches(one, two, stack, right):
        return jnp.concatenate([dot(one[:, stack], right), dot(two[:, stack], right)], axis=0)

    def one_pair(p, carry):
        d_scaled, q_scaled = [], []
        for a in range(2):
            h = 2 * p + a
            stack, rows, row = head_stack(h), head_rows(h), pl.ds(h, 1)
            scores = biased(both_patches(k_far_0, k_far, stack, q_stack[stack, :]), bias, 4)
            top_1 = tops[row, :]
            top = jnp.maximum(top_1, jnp.max(scores, axis=0, keepdims=True))
            weights = jnp.exp(scores - top)
            shrink = jnp.exp(top_1 - top)
            share = 1.0 / (shrink * totals[row, :] + jnp.sum(weights, axis=0, keepdims=True))
            share_1 = shrink * share
            pair = pair_of(weights)
            e_h[a] = pair[0]
            e_l[a] = pair[1]
            mixed = share_1 * mixed_1[rows, :] + share * weighed((vt_0_h, vt_h), (vt_0_l, vt_l), rows, pair)
            mixed_t[rows, :] = mixed
            d_mixed = d_mixed_t[rows, :]
            delta = jnp.sum(d_mixed * mixed, axis=0, keepdims=True)
            deltas[row, :] = delta
            shares[row, :] = share
            shares_1[row, :] = share_1
            pair = pair_of(weights * (both_patches(v_far_0, v_far, stack, d_stack[stack, :]) - delta))
            u_h[h] = pair[0]
            u_l[h] = pair[1]
            d_scaled.append(d_mixed * share)
            q_scaled.append(q_t[rows, :] * share)
        lanes = pair_lanes(p)
        right = pair_of(jnp.concatenate(d_scaled, axis=0).T)
        d_value = gathered((e_h[0], e_h[1]), (e_l[0], e_l[1]), right)
        store((dv_h, dv_l), pair_of(d_value), slice(None), lanes)
        right = pair_of(jnp.concatenate(q_scaled, axis=0).T)
        d_key = gathered((u_h[2 * p], u_h[2 * p + 1]), (u_l[2 * p], u_l[2 * p + 1]), right)
        store((dk_h, dk_l), pair_of(d_key), slice(None), lanes)
        return carry

    lax.fori_loop(0, PAIRS, one_pair, 0, unroll=UNROLL)
    d_far[...] = sums_of(
        [load((dk_h, dk_l), ...), load((dv_h, dv_l), ...)], [load((wk_h, wk_l), ...), load((wv_h, wv_l), ...)], NT
    )


def back_kernel(
    q_t, d_mixed_t, kt_h, kt_l, kt2_h, kt2_l, key3, e_h, e_l, d_scores, u_h, u_l, deltas, shares, shares_1,
    dq_t, dk_h, dk_l, dv_h, dv_l,
    s_h, s_l, kt3_h, kt3_l,
):
    store((kt3_h, kt3_l), pair_of(key3[...].T), ...)

    def one_pair(p, carry):
        q_scaled, d_scaled = [], []
        for a in range(2):
            h = 2 * p + a
            rows, row = head_rows(h), pl.ds(h, 1)
            weights = e_h[h].astype(F32) + e_l[h].astype(F32)
            pair = pair_of(weights * (d_scores[h] - deltas[row, :]))
            s_h[a] = pair[0]
            s_l[a] = pair[1]
            share_1 = shares_1[row, :]
            one = weighed((kt_h, kt2_h), (kt_l, kt2_l), rows, pair)
            two = weighed((kt3_h,), (kt3_l,), rows, (u_h[h], u_l[h]))
            dq_t[rows, :] = (share_1 * one + shares[row, :] * two) * HD ** (-0.5)
            q_scaled.append(q_t[rows, :] * share_1)
            d_scaled.append(d_mixed_t[rows, :] * share_1)
        lanes = pair_lanes(p)
        right = pair_of(jnp.concatenate(q_scaled, axis=0).T)
        d_key = gathered((s_h[0], s_h[1]), (s_l[0], s_l[1]), right)
        store((dk_h, dk_l), pair_of(d_key), slice(None), lanes)
        right = pair_of(jnp.concatenate(d_scaled, axis=0).T)
        d_value = gathered((e_h[2 * p], e_h[2 * p + 1]), (e_l[2 * p], e_l[2 * p + 1]), right)
        store((dv_h, dv_l), pair_of(d_value), slice(None), lanes)
        return carry

    lax.fori_loop(0, PAIRS, one_pair, 0, unroll=UNROLL)


def mix_kernel(
    me, mixed_t, ht_h, ht_l, ht2_h, ht2_l, hidden3, dv_h, dv_l, dv3_h, dv3_l, cot, ht3_h, ht3_l, keep, *refs
):
    *sends, grad_o, grad_v = refs
    own = cot.shape[0]
    store((ht3_h, ht3_l), pair_of(hidden3[...].T), ...)
    grad_o[...] = dot3(pair_of(mixed_t[...]), pair_of(cot[...]))
    turned = [load(t, ...) for t in ((ht_h, ht_l), (ht2_h, ht2_l), (ht3_h, ht3_l))]
    d_values = [load((dv_h, dv_l), slice(0, own)), load((dv_h, dv_l), slice(own, 2 * own)), load((dv3_h, dv3_l), ...)]
    grad_v[...] = sums_of(turned, d_values)
    kept_and_sent(me, (grad_o, grad_v), keep, sends)


def result_kernel(_, mixed_t, tokens, wo_h, wo_l, result, mark):
    mark[...] = jnp.zeros_like(mark)
    result[...] = dot3(pair_of(mixed_t[...].T), load((wo_h, wo_l), ...)) + tokens[...]


def grad_kernel(
    ht_h, ht_l, ht2_h, ht2_l, ht3_h, ht3_l, dq_t, dk_h, dk_l, dk3_h, dk3_l,
    grad_q, grad_k, dq_h, dq_l,
):
    own = dq_h.shape[0]
    d_query = pair_of(dq_t[...].T)
    store((dq_h, dq_l), d_query, ...)
    turned = [load(t, ...) for t in ((ht_h, ht_l), (ht2_h, ht2_l), (ht3_h, ht3_l))]
    d_keys = [load((dk_h, dk_l), slice(0, own)), load((dk_h, dk_l), slice(own, 2 * own)), load((dk3_h, dk3_l), ...)]
    grad_q[...] = dot3(turned[0], d_query)
    grad_k[...] = sums_of(turned, d_keys)


def core_kernel(me, grad_q, grad_k, _keep, keep, *sends):
    kept_and_sent(me, (grad_q, grad_k), keep, sends)


def arrive_kernel(a, out, mark):
    mark[...] = jnp.zeros_like(mark)
    out[...] = a[...]


def side_kernel(
    _, d_back, dq_h, dq_l, dk_h, dk_l, dv_h, dv_l, wq_h, wq_l, wk_h, wk_l, wv_h, wv_l,
    d_given, d_own, mark,
):
    mark[...] = jnp.zeros_like(mark)
    own = d_own.shape[0]
    first, near = slice(0, own), slice(own, 2 * own)
    w_q, w_k, w_v = load((wq_h, wq_l), ...), load((wk_h, wk_l), ...), load((wv_h, wv_l), ...)
    d_given[...] = d_back[...] + sums_of(
        [load((dk_h, dk_l), near), load((dv_h, dv_l), near)], [w_k, w_v], NT
    )
    d_own[...] = sums_of(
        [load((dq_h, dq_l), ...), load((dk_h, dk_l), first), load((dv_h, dv_l), first)], [w_q, w_k, w_v], NT
    )


def half_of(me, mask, mine, rows):
    index = (me[0] // mask) % 2
    return pl.ds(pl.multiple_of((index if mine else 1 - index) * rows, 8), rows)


def add_kernel(a, b, out, *_):
    out[...] = a[...] + b[...]


def cut_kernel(masks, me, keep_1, keep_2, _, *refs):
    others, outs, sums = refs[: 2 * PIECES], refs[2 * PIECES : -1], refs[-1]
    rows = others[0].shape[0]
    for i, other in enumerate(others):
        keep = (keep_1, keep_2)[i // PIECES]
        first = i % PIECES * rows
        sums[i * rows : (i + 1) * rows, :] = keep[first : first + rows, :] + other[...]
    at = 0
    for i, mask in enumerate(masks):
        rows = outs[2 * i].shape[0]
        for out, mine in ((outs[2 * i], True), (outs[2 * i + 1], False)):
            index = (me[0] // mask) % 2
            start = at + (index if mine else 1 - index) * rows
            out[...] = sums[pl.ds(pl.multiple_of(start, 8), rows), :]
        at += 2 * rows


def halve_kernel(mask, me, keep, other, *rest):
    next_keep, next_send = rest[-2:]
    rows = next_keep.shape[0]
    for out, mine in ((next_keep, True), (next_send, False)):
        at = half_of(me, mask, mine, rows)
        out[...] = keep[at, :] + other[at, :]


def first_kernel(a, b, d_given, out, d_going):
    out[...] = a[...] + b[...]
    d_going[...] = d_given[...]


def last_kernel(a, b, *rest):
    rest[-1][...] = a[...] + b[...]


def double_kernel(mask, me, mine, other, *rest):
    out = rest[-1]
    rows = mine.shape[0]
    out[half_of(me, mask, True, rows), :] = mine[...]
    out[half_of(me, mask, False, rows), :] = other[...]


def write_kernel(ranges, core, me, gain, wv_h, wv_l, wq_h, wq_l, wk_h, wk_l, *refs):
    parts, refs = refs[:3], refs[3:]
    before = refs[4] if core else None
    refs = refs[5 * core :]
    outs, last, (partial, total, sent) = refs[:4], refs[4], refs[5:] if core else (refs[4], None, refs[5])
    weights = (None, (wv_h, wv_l), (wq_h, wq_l), (wk_h, wk_l))
    lanes = partial.shape[1]
    partial[...] = before[...] if core else jnp.zeros_like(partial)
    for bit in range(2):

        @pl.when(me[0] % 2 == bit)
        def _():
            pieces = [
                (parts[i].at[pl.ds(first, rows)], 2 * exchange + (bit + core) % 2, to, rows)
                for i, first, rows, exchange, to in ranges
            ]
            copies = [
                pltpu.make_async_copy(piece, outs[matrix].at[pl.ds(to, rows)], sent.at[n])
                for n, (piece, matrix, to, rows) in enumerate(pieces)
            ]
            for copy in copies:
                copy.start()
            for piece, matrix, to, rows in pieces:
                if matrix:
                    high, low = weights[matrix]
                    for lane in range(0, piece.shape[1], lanes):
                        at = (slice(to, to + rows), slice(lane, lane + lanes))
                        weight = high[at].astype(F32) + low[at].astype(F32)
                        partial[to : to + rows, :] += weight * piece[:, lane : lane + lanes]
            if core:
                total[...] = jnp.sum(partial[...].T, axis=0, keepdims=True) / gain[...]
                copies.append(pltpu.make_async_copy(total, last, sent.at[len(copies)]))
                copies[-1].start()
            for copy in copies:
                copy.wait()


def written(me, gain, weights, parts, ranges, count, core, held=()):
    width = parts[0].shape[1]
    anywhere = pl.BlockSpec(memory_space=pl.ANY)
    partial = shape(count, 128)
    semaphores = pltpu.SemaphoreType.DMA((len(ranges) + core,))
    return pl.pallas_call(
        functools.partial(write_kernel, ranges, core),
        out_shape=[shape(count, width)] * 4 + [shape(1, width) if core else partial],
        in_specs=[SMEM] + [VMEM] * 10 + ([anywhere] * 4 + [VMEM] if core else []),
        out_specs=[anywhere] * 4 + [anywhere if core else VMEM],
        scratch_shapes=([pltpu.VMEM(partial.shape, F32), pltpu.VMEM((1, width), F32)] if core else []) + [semaphores],
        input_output_aliases={11 + i: i for i in range(4)} if core else {},
        compiler_params=pltpu.CompilerParams(vmem_limit_bytes=2**23),
        cost_estimate=pl.CostEstimate(flops=10**9, bytes_accessed=0, transcendentals=0),
    )(me, gain, *weights, *parts, *held)


def tokens_kernel(_, tokens, gain, cot, d_own, d_other, out, mark):
    mark[...] = jnp.zeros_like(mark)
    normal, rstd = unit_rows(tokens[...])
    d_normal = (d_own[...] + d_other[...]) * gain[...]
    inner = jnp.mean(d_normal * normal, axis=1, keepdims=True)
    centre = jnp.mean(d_normal, axis=1, keepdims=True)
    out[...] = (d_normal - centre - normal * inner) * rstd + cot[...]


def shape(*dims, dtype=F32):
    return jax.ShapeDtypeStruct(dims, dtype)


def pairs(*dims):
    return [shape(*dims, dtype=BF16)] * 2


def call(kernel, inputs, outputs, scratch=(), scalars=0, limit=4, us=1):
    return pl.pallas_call(
        kernel,
        out_shape=outputs,
        in_specs=[SMEM] * scalars + [VMEM] * (len(inputs) - scalars),
        out_specs=[VMEM] * len(outputs),
        scratch_shapes=[pltpu.VMEM(s.shape, s.dtype) for s in scratch],
        compiler_params=pltpu.CompilerParams(vmem_limit_bytes=limit * 2**20),
        cost_estimate=pl.CostEstimate(flops=int(us * 10**9), bytes_accessed=0, transcendentals=0),
    )(*inputs)


MARK = shape(8, 128)


def along_space(value, target):
    count = lax.axis_size("space")
    return lax.ppermute(value, "space", [(i, target(i) % count) for i in range(count)])


def across(value):
    return along_space(value, lambda i: i ^ 1)


def onward(value):
    return along_space(value, lambda i: i + 2 - 4 * (i % 2))


def homeward(value):
    return along_space(value, lambda i: i - 2 + 4 * (i % 2))


def devices():
    return lax.axis_size("space") * lax.axis_size("slab")


def swapped(value, mask):
    return lax.ppermute(value, ("space", "slab"), [(i, i ^ mask) for i in range(devices())])


ORDERS = ((4, 2, 8), (2, 8, 4), (8, 4, 2))
LAST = 16


def summed(me, keep_1, others_1, keep_2, others_2, mark, weights, gain, result_of, side_of, tokens_of):
    count, width = keep_1.shape
    total = 2 * count
    unit = 8 * 8
    sizes = [total // unit // 3 * unit] * 2
    sizes.append(total - sum(sizes))
    parts = call(
        functools.partial(cut_kernel, [order[0] for order in ORDERS]),
        (me, keep_1, keep_2, mark, *others_1, *others_2),
        [shape(size // 2, width) for size in sizes for _ in range(2)],
        [shape(total, width)],
        scalars=1, limit=8,
    )
    d_given, d_own, mark = side_of(parts[0])
    result, mark_2 = result_of(parts[0])
    parts = [[parts[2 * i], swapped(parts[2 * i + 1], ORDERS[i][0])] for i in range(3)]
    for step in (1, 2):
        for i in range(3):
            half, mask = shape(sizes[i] >> (step + 1), width), ORDERS[i][step]
            place = (mark, mark_2) if step == 1 else ()
            keep, send = call(
                functools.partial(halve_kernel, mask), (me, *parts[i], *place), [half, half], scalars=1
            )
            parts[i] = [keep, swapped(send, mask)]
    for i in (0, 2, 1):
        if i == 1:
            part, d_going = call(first_kernel, (*parts[i], d_given), [parts[i][0], d_given])
            d_other = across(d_going)
        else:
            (part,) = call(add_kernel, parts[i], [parts[i][0]])
        mask, other = LAST, swapped(part, LAST)
        while 2 * mask < devices():
            (part,) = call(add_kernel, (part, other), [part])
            mask *= 2
            other = swapped(part, mask)
        (parts[i],) = call(last_kernel, (part, other), [part])
    for step in (2, 1, 0):
        for i in range(3):
            mask = ORDERS[i][step]
            place = {(2, 1): (d_other,), (0, 2): (mark,)}.get((step, i), ())
            (parts[i],) = call(
                functools.partial(double_kernel, mask), (me, parts[i], swapped(parts[i], mask), *place),
                [shape(2 * parts[i].shape[0], width)], scalars=1,
            )
        if step == 1:
            d_tokens, mark = tokens_of(parts[0], d_own, d_other)
    others = [swapped(part, 1) for part in parts]
    ranges, at = [], 0
    for i, size in enumerate(sizes):
        for exchange in range(2):
            start, stop = max(at, exchange * count), min(at + size, (exchange + 1) * count)
            if start < stop:
                ranges.append((i, start - at, stop - start, exchange, start - exchange * count))
        at += size
    held = written(me, gain, weights, parts, ranges, count, 0)
    *gradients, d_gain = written(me, gain, weights, others, ranges, count, 1, held)
    return gradients, d_gain.reshape(width), d_tokens, result


def body(tokens, gain, wq, wk, wv, wo, neighbour_list, neighbour_count, cotangent):
    rows, width = tokens.shape
    me = (lax.axis_index("space") * lax.axis_size("slab") + lax.axis_index("slab")).astype(jnp.int32)[None]
    parity = (lax.axis_index("space") % 2).astype(jnp.int32)[None]
    counts = neighbour_count[None, :]
    near = [across(tokens[i * PT : (i + 1) * PT]) for i in range(2)]
    gain_row = gain[None, :]
    stack_rows, stack_columns = shape(HEADS * 4 * HD, rows, dtype=BF16), shape(rows, HEADS * 4 * HD, dtype=BF16)
    turned, square, pair = pairs(width, rows), pairs(width, width), pairs(rows, width)
    whole, whole_t, scalars = shape(rows, width), shape(width, rows), shape(HEADS, rows)
    weights = call(weight_kernel, (me, parity, wq, wk, wv, wo), square * 4, scalars=2, limit=20)
    near[0], *weights = lax.optimization_barrier((near[0], *weights))
    far = [onward(near[0])]
    wq_h, wq_l, wk_h, wk_l, wv_h, wv_l, wo_h, wo_l = weights
    (
        ht_h, ht_l, q_t, q_stack, k_stack, v_stack, kt_h, kt_l, vt_h, vt_l, d_mixed_t, d_stack,
    ) = call(
        own_kernel,
        (near[0], tokens, gain_row, cotangent, *weights),
        [*turned, whole_t, stack_rows, stack_columns, stack_columns, *turned, *turned, whole_t, stack_rows],
        limit=LIMITS[0], us=1,
    )
    near[1], q_stack = lax.optimization_barrier((near[1], q_stack))
    far.append(onward(near[1]))
    w_k, w_v = (wk_h, wk_l), (wv_h, wv_l)
    ht2_h, ht2_l, kt2_h, kt2_l, k_near, v_near, vt2_h, vt2_l = call(
        near_side_kernel,
        (*near, gain_row, *w_k, *w_v),
        [*turned, *turned, stack_columns, stack_columns, *turned],
        limit=LIMITS[1], us=1,
    )
    e_h, e_l, d_scores, mixed, tops, totals = call(
        near_kernel,
        (
            parity, neighbour_list, counts, far[0], q_stack, k_stack, v_stack, vt_h, vt_l, d_stack, k_near, v_near,
            vt2_h, vt2_l,
        ),
        [*pairs(HEADS, 2 * rows, rows), shape(HEADS, 2 * rows, rows), whole_t, scalars, scalars],
        [shape(8, rows)],
        scalars=3, limit=LIMITS[1], us=1,
    )
    half_stack, half_t = shape(PT, HEADS * 4 * HD, dtype=BF16), pairs(width, PT)
    first = call(
        far_side_kernel,
        (tops, far[0], gain_row, *w_k, *w_v),
        [shape(PT, width), shape(PT, width), half_stack, half_stack, *half_t],
        limit=LIMITS[1], us=1,
    )
    (
        hidden3, key3, u_h, u_l, mixed_t, deltas, shares, shares_1, dk3_h, dk3_l, dv3_h, dv3_l,
        d_far,
    ) = call(
        far_kernel,
        (
            parity, neighbour_list, counts, *first, far[1], gain_row, q_t, q_stack, d_mixed_t, d_stack, mixed, tops, totals,
            *w_k, *w_v,
        ),
        [
            whole, whole, *pairs(HEADS, rows, rows), whole_t, scalars, scalars, scalars, *pair, *pair,
            whole,
        ],
        [shape(8, rows), half_stack, half_stack, *half_t, *pairs(2, rows, rows)],
        scalars=3, limit=LIMITS[2], us=1,
    )
    d_back = homeward(d_far)
    dq_t, dk_h, dk_l, dv_h, dv_l = call(
        back_kernel,
        (
            q_t, d_mixed_t, kt_h, kt_l, kt2_h, kt2_l, key3, e_h, e_l, d_scores, u_h, u_l, deltas, shares,
            shares_1,
        ),
        [whole_t, *pairs(2 * rows, width), *pairs(2 * rows, width)],
        [*pairs(2, 2 * rows, rows), *turned],
        limit=LIMITS[4], us=0.001,
    )
    pieces = [shape(width // PIECES, width)] * PIECES
    ht3_h, ht3_l, keep_1, *sends_1 = call(
        mix_kernel,
        (me, mixed_t, ht_h, ht_l, ht2_h, ht2_l, hidden3, dv_h, dv_l, dv3_h, dv3_l, cotangent),
        [*turned, shape(width, width), *pieces],
        [shape(width, width), shape(width, width)],
        scalars=1, limit=LIMITS[3], us=0.001,
    )
    others_1 = [swapped(send, 1) for send in sends_1]
    grad_q, grad_k, dq_h, dq_l = call(
        grad_kernel,
        (ht_h, ht_l, ht2_h, ht2_l, ht3_h, ht3_l, dq_t, dk_h, dk_l, dk3_h, dk3_l),
        [shape(width, width), shape(width, width), *pair],
        limit=LIMITS[5], us=0.001,
    )
    keep_2, *sends_2 = call(
        core_kernel, (me, grad_q, grad_k, keep_1), [shape(width, width), *pieces], scalars=1, limit=8, us=0.001
    )
    others_2 = [swapped(send, 1) for send in sends_2]
    d_back, mark = call(arrive_kernel, (d_back,), [whole, MARK], us=20)

    def result_of(place):
        return call(result_kernel, (place, mixed_t, tokens, wo_h, wo_l), [whole, MARK], limit=LIMITS[3], us=1)

    def side_of(place):
        inputs = (place, d_back, dq_h, dq_l, dk_h, dk_l, dv_h, dv_l, wq_h, wq_l, *w_k, *w_v)
        return call(side_kernel, inputs, [whole, whole, MARK], limit=LIMITS[3], us=1)

    def tokens_of(place, d_own, d_other):
        inputs = (place, tokens, gain_row, cotangent, d_own, d_other)
        return call(tokens_kernel, inputs, [whole, MARK], limit=8)

    (grad_o, grad_v, grad_q, grad_k), d_gain, d_tokens, result = summed(
        me, keep_1, others_1, keep_2, others_2, mark, (wv_h, wv_l, wq_h, wq_l, *w_k), gain_row, result_of, side_of, tokens_of
    )
    return (result, d_tokens, d_gain, grad_q, grad_k, grad_v, grad_o)


UNROLL = True
PIECES = 1
LIMITS = (8, 8, 8, 8, 8, 8)


def solution(mesh):
    tokens = P(("space", "slab"), None)
    return jax.shard_map(
        body,
        mesh=mesh,
        in_specs=(tokens, P(), P(), P(), P(), P(), tokens, P(("space", "slab")), tokens),
        out_specs=(tokens, tokens, P(), P(), P(), P(), P()),
        check_vma=False,
    )
```

```python
import functools

import jax
import jax.numpy as jnp
from jax import lax
from jax.experimental import pallas as pl
from jax.experimental.pallas import tpu as pltpu
from jax.sharding import PartitionSpec as P

HEADS = 8
PT = 128
HD = 64
PAIRS = HEADS // 2
F32 = jnp.float32
BF16 = jnp.bfloat16
NN = (((1,), (0,)), ((), ()))
NT = (((1,), (1,)), ((), ()))
VMEM = pl.BlockSpec(memory_space=pltpu.VMEM)
SMEM = pl.BlockSpec(memory_space=pltpu.SMEM)


def pair_of(x):
    high = x.astype(BF16)
    return high, (x - high.astype(F32)).astype(BF16)


def dot(left, right, dims=NN):
    return lax.dot_general(left, right, dims, preferred_element_type=F32)


def dot3(left, right, dims=NN):
    return dot(left[0], right[0], dims) + (dot(left[0], right[1], dims) + dot(left[1], right[0], dims))


def load(refs, *index):
    return refs[0][index], refs[1][index]


def store(refs, pair, *index):
    refs[0][index] = pair[0]
    refs[1][index] = pair[1]


def unit_rows(tokens):
    centred = tokens - jnp.mean(tokens, axis=1, keepdims=True)
    variance = jnp.mean(centred * centred, axis=1, keepdims=True)
    rstd = lax.rsqrt(variance + 1e-05)
    return centred * rstd, rstd


def store_stacked(ref, row, rows):
    count = rows.shape[0]
    left_half = lax.broadcasted_iota(jnp.int32, (count, 2 * HD), 1) < HD
    for p in range(PAIRS):
        part = rows[:, p * 2 * HD : (p + 1) * 2 * HD]
        swapped = pltpu.roll(part, HD, 1)
        for a in range(2):
            both = jnp.where(left_half == (a == 0), part, swapped)
            high, low = pair_of(both)
            base = (2 * p + a) * 4 * HD
            ref[pl.ds(row, count), base : base + 2 * HD] = high
            ref[pl.ds(row, count), base + 2 * HD : base + 4 * HD] = low


def store_interleaved(ref, columns):
    high, low = pair_of(columns)
    for h in range(HEADS):
        for i, piece in enumerate((high, low, high, low)):
            at = h * 4 * HD + i * HD
            ref[at : at + HD, :] = piece[h * HD : (h + 1) * HD]


def sums_of(left, right, dims=NN):
    return sum(dot3(a, b, dims) for a, b in zip(left[1:], right[1:], strict=True)) + dot3(left[0], right[0], dims)


def weight_kernel(_me, _parity, wq, wk, wv, wo, wq_h, wq_l, wk_h, wk_l, wv_h, wv_l, wo_h, wo_l):
    for source, high, low in ((wq, wq_h, wq_l), (wk, wk_h, wk_l), (wv, wv_h, wv_l), (wo, wo_h, wo_l)):
        store((high, low), pair_of(source[...]), ...)


def own_kernel(
    _, tokens, gain, cot, wq_h, wq_l, wk_h, wk_l, wv_h, wv_l, wo_h, wo_l,
    ht_h, ht_l, q_t, q_stack, k_stack, v_stack, kt_h, kt_l, vt_h, vt_l, d_mixed_t, d_stack,
):
    hidden = unit_rows(tokens[...])[0] * gain[...]
    store((ht_h, ht_l), pair_of(hidden.T), ...)
    rows = pair_of(hidden)
    query = dot3(rows, load((wq_h, wq_l), ...)) * HD ** (-0.5)
    q_t[...] = query.T
    store_interleaved(q_stack, q_t[...])
    key = dot3(rows, load((wk_h, wk_l), ...))
    store_stacked(k_stack, 0, key)
    store((kt_h, kt_l), pair_of(key.T), ...)
    value = dot3(rows, load((wv_h, wv_l), ...))
    store_stacked(v_stack, 0, value)
    store((vt_h, vt_l), pair_of(value.T), ...)
    d_mixed = dot3(load((wo_h, wo_l), ...), pair_of(cot[...]), NT)
    d_mixed_t[...] = d_mixed
    store_interleaved(d_stack, d_mixed)


def store_bias(bias, listed, counts, parity, patches):
    queries = bias.shape[1]
    lane = lax.broadcasted_iota(jnp.int32, (1, queries), 1)
    near = jnp.where(parity[0] == 0, 4, 0)
    windows = (2, 3, near, near + 1, 4 - near, 5 - near)
    for place in patches:
        level = []
        for p in range(2):
            live = jnp.int32(1 if place == p else 0)
            for j in range(listed.shape[1]):
                hit = jnp.logical_and(j < counts[0, p], listed[p, j] == windows[place])
                live = jnp.where(hit, 1, live)
            level.append(jnp.where(live == 1, 0.0, -1e30).astype(F32))
        bias[place : place + 1, :] = jnp.where(lane < PT, level[0], level[1])


def biased(scores, bias, first):
    count = scores.shape[0] // PT
    return jnp.concatenate(
        [scores[i * PT : (i + 1) * PT] + bias[first + i : first + i + 1, :] for i in range(count)], axis=0
    )


def key_side(patches, gain, wk, wv, k_stack, v_stack, vt):
    hidden = jnp.concatenate([unit_rows(tokens[...])[0] * gain[...] for tokens in patches], axis=0)
    rows = pair_of(hidden)
    key = dot3(rows, load(wk, ...))
    store_stacked(k_stack, 0, key)
    value = dot3(rows, load(wv, ...))
    store_stacked(v_stack, 0, value)
    store(vt, pair_of(value.T), ...)
    return hidden, key


def head_rows(h):
    return pl.ds(pl.multiple_of(h * HD, HD), HD)


def head_stack(h):
    return pl.ds(pl.multiple_of(h * 4 * HD, 4 * HD), 4 * HD)


def weighed(highs, lows, rows, right):
    high = jnp.concatenate([r[rows, :] for r in highs], axis=1)
    low = jnp.concatenate([r[rows, :] for r in lows], axis=1)
    left = jnp.concatenate([high, low], axis=0)
    both = dot(left, right[0]) + dot(left, right[1])
    return both[:HD] + both[HD:]


def near_side_kernel(
    patch_0, patch_1, gain, wk_h, wk_l, wv_h, wv_l,
    ht_h, ht_l, kt_h, kt_l, k_stack, v_stack, vt_h, vt_l,
):
    hidden, key = key_side((patch_0, patch_1), gain, (wk_h, wk_l), (wv_h, wv_l), k_stack, v_stack, (vt_h, vt_l))
    store((ht_h, ht_l), pair_of(hidden.T), ...)
    store((kt_h, kt_l), pair_of(key.T), ...)


def near_kernel(
    parity, listed, counts, _, q_stack, k_stack, v_stack, vt_h, vt_l, d_stack, k_near, v_near, vt2_h, vt2_l,
    e_h, e_l, d_scores, mixed, tops, totals,
    bias,
):
    store_bias(bias, listed, counts, parity, range(4))

    def one_head(h, carry):
        stack, rows = head_stack(h), head_rows(h)
        q_now, d_now = q_stack[stack, :], d_stack[stack, :]
        scores = jnp.concatenate(
            [biased(dot(k_stack[:, stack], q_now), bias, 0), biased(dot(k_near[:, stack], q_now), bias, 2)], axis=0
        )
        top = jnp.max(scores, axis=0, keepdims=True)
        weights = jnp.exp(scores - top)
        tops[pl.ds(h, 1), :] = top
        totals[pl.ds(h, 1), :] = jnp.sum(weights, axis=0, keepdims=True)
        pair = pair_of(weights)
        e_h[h] = pair[0]
        e_l[h] = pair[1]
        mixed[rows, :] = weighed((vt_h, vt2_h), (vt_l, vt2_l), rows, pair)
        d_scores[h] = jnp.concatenate([dot(v_stack[:, stack], d_now), dot(v_near[:, stack], d_now)], axis=0)
        return carry

    lax.fori_loop(0, HEADS, one_head, 0, unroll=UNROLL)


def gathered(left_h, left_l, right):
    left_half = lax.broadcasted_iota(jnp.int32, right[0].shape, 1) < HD
    zero = jnp.zeros_like(right[0])
    one = [jnp.where(left_half, x, zero) for x in right]
    two = [jnp.where(left_half, zero, x) for x in right]
    one, two = jnp.concatenate(one, axis=1), jnp.concatenate(two, axis=1)
    wide = (dot(left_h[0], one) + dot(left_h[1], two)) + (dot(left_l[0], one) + dot(left_l[1], two))
    return wide[:, : 2 * HD] + wide[:, 2 * HD :]


def pair_lanes(p):
    return pl.ds(pl.multiple_of(p * 2 * HD, 2 * HD), 2 * HD)


def kept_and_sent(me, pair, keep, sends):
    rows = sends[0].shape[0]
    for bit in range(2):

        @pl.when(me[0] % 2 == bit)
        def _():
            keep[...] = pair[bit][...]
            for i, send in enumerate(sends):
                send[...] = pair[1 - bit][i * rows : (i + 1) * rows, :]


def far_side_kernel(
    _, patch, gain, wk_h, wk_l, wv_h, wv_l,
    hidden, key, k_stack, v_stack, vt_h, vt_l,
):
    hidden[...], key[...] = key_side((patch,), gain, (wk_h, wk_l), (wv_h, wv_l), k_stack, v_stack, (vt_h, vt_l))


def far_kernel(
    parity, listed, counts, hidden_0, key_0, k_far_0, v_far_0, vt_0_h, vt_0_l, patch_1, gain, q_t, q_stack, d_mixed_t, d_stack, mixed_1, tops, totals,
    wk_h, wk_l, wv_h, wv_l,
    hidden, key, u_h, u_l, mixed_t, deltas, shares, shares_1, dk_h, dk_l, dv_h, dv_l, d_far,
    bias, k_far, v_far, vt_h, vt_l, e_h, e_l,
):
    store_bias(bias, listed, counts, parity, range(4, 6))
    hidden[:PT, :], key[:PT, :] = hidden_0[...], key_0[...]
    hidden[PT:, :], key[PT:, :] = key_side(
        (patch_1,), gain, (wk_h, wk_l), (wv_h, wv_l), k_far, v_far, (vt_h, vt_l)
    )

    def both_patches(one, two, stack, right):
        return jnp.concatenate([dot(one[:, stack], right), dot(two[:, stack], right)], axis=0)

    def one_pair(p, carry):
        d_scaled, q_scaled = [], []
        for a in range(2):
            h = 2 * p + a
            stack, rows, row = head_stack(h), head_rows(h), pl.ds(h, 1)
            scores = biased(both_patches(k_far_0, k_far, stack, q_stack[stack, :]), bias, 4)
            top_1 = tops[row, :]
            top = jnp.maximum(top_1, jnp.max(scores, axis=0, keepdims=True))
            weights = jnp.exp(scores - top)
            shrink = jnp.exp(top_1 - top)
            share = 1.0 / (shrink * totals[row, :] + jnp.sum(weights, axis=0, keepdims=True))
            share_1 = shrink * share
            pair = pair_of(weights)
            e_h[a] = pair[0]
            e_l[a] = pair[1]
            mixed = share_1 * mixed_1[rows, :] + share * weighed((vt_0_h, vt_h), (vt_0_l, vt_l), rows, pair)
            mixed_t[rows, :] = mixed
            d_mixed = d_mixed_t[rows, :]
            delta = jnp.sum(d_mixed * mixed, axis=0, keepdims=True)
            deltas[row, :] = delta
            shares[row, :] = share
            shares_1[row, :] = share_1
            pair = pair_of(weights * (both_patches(v_far_0, v_far, stack, d_stack[stack, :]) - delta))
            u_h[h] = pair[0]
            u_l[h] = pair[1]
            d_scaled.append(d_mixed * share)
            q_scaled.append(q_t[rows, :] * share)
        lanes = pair_lanes(p)
        right = pair_of(jnp.concatenate(d_scaled, axis=0).T)
        d_value = gathered((e_h[0], e_h[1]), (e_l[0], e_l[1]), right)
        store((dv_h, dv_l), pair_of(d_value), slice(None), lanes)
        right = pair_of(jnp.concatenate(q_scaled, axis=0).T)
        d_key = gathered((u_h[2 * p], u_h[2 * p + 1]), (u_l[2 * p], u_l[2 * p + 1]), right)
        store((dk_h, dk_l), pair_of(d_key), slice(None), lanes)
        return carry

    lax.fori_loop(0, PAIRS, one_pair, 0, unroll=UNROLL)
    d_far[...] = sums_of(
        [load((dk_h, dk_l), ...), load((dv_h, dv_l), ...)], [load((wk_h, wk_l), ...), load((wv_h, wv_l), ...)], NT
    )


def back_kernel(
    q_t, d_mixed_t, kt_h, kt_l, kt2_h, kt2_l, key3, e_h, e_l, d_scores, u_h, u_l, deltas, shares, shares_1,
    dq_t, dk_h, dk_l, dv_h, dv_l,
    s_h, s_l, kt3_h, kt3_l,
):
    store((kt3_h, kt3_l), pair_of(key3[...].T), ...)

    def one_pair(p, carry):
        q_scaled, d_scaled = [], []
        for a in range(2):
            h = 2 * p + a
            rows, row = head_rows(h), pl.ds(h, 1)
            weights = e_h[h].astype(F32) + e_l[h].astype(F32)
            pair = pair_of(weights * (d_scores[h] - deltas[row, :]))
            s_h[a] = pair[0]
            s_l[a] = pair[1]
            share_1 = shares_1[row, :]
            one = weighed((kt_h, kt2_h), (kt_l, kt2_l), rows, pair)
            two = weighed((kt3_h,), (kt3_l,), rows, (u_h[h], u_l[h]))
            dq_t[rows, :] = (share_1 * one + shares[row, :] * two) * HD ** (-0.5)
            q_scaled.append(q_t[rows, :] * share_1)
            d_scaled.append(d_mixed_t[rows, :] * share_1)
        lanes = pair_lanes(p)
        right = pair_of(jnp.concatenate(q_scaled, axis=0).T)
        d_key = gathered((s_h[0], s_h[1]), (s_l[0], s_l[1]), right)
        store((dk_h, dk_l), pair_of(d_key), slice(None), lanes)
        right = pair_of(jnp.concatenate(d_scaled, axis=0).T)
        d_value = gathered((e_h[2 * p], e_h[2 * p + 1]), (e_l[2 * p], e_l[2 * p + 1]), right)
        store((dv_h, dv_l), pair_of(d_value), slice(None), lanes)
        return carry

    lax.fori_loop(0, PAIRS, one_pair, 0, unroll=UNROLL)


def mix_kernel(
    me, mixed_t, ht_h, ht_l, ht2_h, ht2_l, hidden3, dv_h, dv_l, dv3_h, dv3_l, cot, ht3_h, ht3_l, keep, *refs
):
    *sends, grad_o, grad_v = refs
    own = cot.shape[0]
    store((ht3_h, ht3_l), pair_of(hidden3[...].T), ...)
    grad_o[...] = dot3(pair_of(mixed_t[...]), pair_of(cot[...]))
    turned = [load(t, ...) for t in ((ht_h, ht_l), (ht2_h, ht2_l), (ht3_h, ht3_l))]
    d_values = [load((dv_h, dv_l), slice(0, own)), load((dv_h, dv_l), slice(own, 2 * own)), load((dv3_h, dv3_l), ...)]
    grad_v[...] = sums_of(turned, d_values)
    kept_and_sent(me, (grad_o, grad_v), keep, sends)


def result_kernel(_, mixed_t, tokens, wo_h, wo_l, result, mark):
    mark[...] = jnp.zeros_like(mark)
    result[...] = dot3(pair_of(mixed_t[...].T), load((wo_h, wo_l), ...)) + tokens[...]


def grad_kernel(
    ht_h, ht_l, ht2_h, ht2_l, ht3_h, ht3_l, dq_t, dk_h, dk_l, dk3_h, dk3_l,
    grad_q, grad_k, dq_h, dq_l,
):
    own = dq_h.shape[0]
    d_query = pair_of(dq_t[...].T)
    store((dq_h, dq_l), d_query, ...)
    turned = [load(t, ...) for t in ((ht_h, ht_l), (ht2_h, ht2_l), (ht3_h, ht3_l))]
    d_keys = [load((dk_h, dk_l), slice(0, own)), load((dk_h, dk_l), slice(own, 2 * own)), load((dk3_h, dk3_l), ...)]
    grad_q[...] = dot3(turned[0], d_query)
    grad_k[...] = sums_of(turned, d_keys)


def core_kernel(me, grad_q, grad_k, _keep, keep, *sends):
    kept_and_sent(me, (grad_q, grad_k), keep, sends)


def arrive_kernel(a, out, mark):
    mark[...] = jnp.zeros_like(mark)
    out[...] = a[...]


def side_kernel(
    _, d_back, dq_h, dq_l, dk_h, dk_l, dv_h, dv_l, wq_h, wq_l, wk_h, wk_l, wv_h, wv_l,
    d_given, d_own, mark,
):
    mark[...] = jnp.zeros_like(mark)
    own = d_own.shape[0]
    first, near = slice(0, own), slice(own, 2 * own)
    w_q, w_k, w_v = load((wq_h, wq_l), ...), load((wk_h, wk_l), ...), load((wv_h, wv_l), ...)
    d_given[...] = d_back[...] + sums_of(
        [load((dk_h, dk_l), near), load((dv_h, dv_l), near)], [w_k, w_v], NT
    )
    d_own[...] = sums_of(
        [load((dq_h, dq_l), ...), load((dk_h, dk_l), first), load((dv_h, dv_l), first)], [w_q, w_k, w_v], NT
    )


def half_of(me, mask, mine, rows):
    index = (me[0] // mask) % 2
    return pl.ds(pl.multiple_of((index if mine else 1 - index) * rows, 8), rows)


def add_kernel(a, b, out, *_):
    out[...] = a[...] + b[...]


def cut_kernel(masks, me, keep_1, keep_2, _, *refs):
    others, outs, sums = refs[: 2 * PIECES], refs[2 * PIECES : -1], refs[-1]
    rows = others[0].shape[0]
    for i, other in enumerate(others):
        keep = (keep_1, keep_2)[i // PIECES]
        first = i % PIECES * rows
        sums[i * rows : (i + 1) * rows, :] = keep[first : first + rows, :] + other[...]
    at = 0
    for i, mask in enumerate(masks):
        rows = outs[2 * i].shape[0]
        for out, mine in ((outs[2 * i], True), (outs[2 * i + 1], False)):
            index = (me[0] // mask) % 2
            start = at + (index if mine else 1 - index) * rows
            out[...] = sums[pl.ds(pl.multiple_of(start, 8), rows), :]
        at += 2 * rows


def halve_kernel(mask, me, keep, other, *rest):
    next_keep, next_send = rest[-2:]
    rows = next_keep.shape[0]
    for out, mine in ((next_keep, True), (next_send, False)):
        at = half_of(me, mask, mine, rows)
        out[...] = keep[at, :] + other[at, :]


def first_kernel(a, b, d_given, out, d_going):
    out[...] = a[...] + b[...]
    d_going[...] = d_given[...]


def last_kernel(a, b, *rest):
    rest[-1][...] = a[...] + b[...]


def double_kernel(mask, me, mine, other, *rest):
    out = rest[-1]
    rows = mine.shape[0]
    out[half_of(me, mask, True, rows), :] = mine[...]
    out[half_of(me, mask, False, rows), :] = other[...]


def write_kernel(ranges, core, me, gain, wv_h, wv_l, wq_h, wq_l, wk_h, wk_l, *refs):
    parts, refs = refs[:3], refs[3:]
    before = refs[4] if core else None
    refs = refs[5 * core :]
    outs, last, (partial, total, sent) = refs[:4], refs[4], refs[5:] if core else (refs[4], None, refs[5])
    weights = (None, (wv_h, wv_l), (wq_h, wq_l), (wk_h, wk_l))
    lanes = partial.shape[1]
    partial[...] = before[...] if core else jnp.zeros_like(partial)
    for bit in range(2):

        @pl.when(me[0] % 2 == bit)
        def _():
            pieces = [
                (parts[i].at[pl.ds(first, rows)], 2 * exchange + (bit + core) % 2, to, rows)
                for i, first, rows, exchange, to in ranges
            ]
            copies = [
                pltpu.make_async_copy(piece, outs[matrix].at[pl.ds(to, rows)], sent.at[n])
                for n, (piece, matrix, to, rows) in enumerate(pieces)
            ]
            for copy in copies:
                copy.start()
            for piece, matrix, to, rows in pieces:
                if matrix:
                    high, low = weights[matrix]
                    for lane in range(0, piece.shape[1], lanes):
                        at = (slice(to, to + rows), slice(lane, lane + lanes))
                        weight = high[at].astype(F32) + low[at].astype(F32)
                        partial[to : to + rows, :] += weight * piece[:, lane : lane + lanes]
            if core:
                total[...] = jnp.sum(partial[...].T, axis=0, keepdims=True) / gain[...]
                copies.append(pltpu.make_async_copy(total, last, sent.at[len(copies)]))
                copies[-1].start()
            for copy in copies:
                copy.wait()


def written(me, gain, weights, parts, ranges, count, core, held=()):
    width = parts[0].shape[1]
    anywhere = pl.BlockSpec(memory_space=pl.ANY)
    partial = shape(count, 128)
    semaphores = pltpu.SemaphoreType.DMA((len(ranges) + core,))
    return pl.pallas_call(
        functools.partial(write_kernel, ranges, core),
        out_shape=[shape(count, width)] * 4 + [shape(1, width) if core else partial],
        in_specs=[SMEM] + [VMEM] * 10 + ([anywhere] * 4 + [VMEM] if core else []),
        out_specs=[anywhere] * 4 + [anywhere if core else VMEM],
        scratch_shapes=([pltpu.VMEM(partial.shape, F32), pltpu.VMEM((1, width), F32)] if core else []) + [semaphores],
        input_output_aliases={11 + i: i for i in range(4)} if core else {},
        compiler_params=pltpu.CompilerParams(vmem_limit_bytes=2**23),
        cost_estimate=pl.CostEstimate(flops=10**9, bytes_accessed=0, transcendentals=0),
    )(me, gain, *weights, *parts, *held)


def tokens_kernel(_, tokens, gain, cot, d_own, d_other, out, mark):
    mark[...] = jnp.zeros_like(mark)
    normal, rstd = unit_rows(tokens[...])
    d_normal = (d_own[...] + d_other[...]) * gain[...]
    inner = jnp.mean(d_normal * normal, axis=1, keepdims=True)
    centre = jnp.mean(d_normal, axis=1, keepdims=True)
    out[...] = (d_normal - centre - normal * inner) * rstd + cot[...]


def shape(*dims, dtype=F32):
    return jax.ShapeDtypeStruct(dims, dtype)


def pairs(*dims):
    return [shape(*dims, dtype=BF16)] * 2


def call(kernel, inputs, outputs, scratch=(), scalars=0, limit=4, us=1):
    return pl.pallas_call(
        kernel,
        out_shape=outputs,
        in_specs=[SMEM] * scalars + [VMEM] * (len(inputs) - scalars),
        out_specs=[VMEM] * len(outputs),
        scratch_shapes=[pltpu.VMEM(s.shape, s.dtype) for s in scratch],
        compiler_params=pltpu.CompilerParams(vmem_limit_bytes=limit * 2**20),
        cost_estimate=pl.CostEstimate(flops=int(us * 10**9), bytes_accessed=0, transcendentals=0),
    )(*inputs)


MARK = shape(8, 128)


def along_space(value, target):
    count = lax.axis_size("space")
    return lax.ppermute(value, "space", [(i, target(i) % count) for i in range(count)])


def across(value):
    return along_space(value, lambda i: i ^ 1)


def onward(value):
    return along_space(value, lambda i: i + 2 - 4 * (i % 2))


def homeward(value):
    return along_space(value, lambda i: i - 2 + 4 * (i % 2))


def devices():
    return lax.axis_size("space") * lax.axis_size("slab")


def swapped(value, mask):
    return lax.ppermute(value, ("space", "slab"), [(i, i ^ mask) for i in range(devices())])


ORDERS = ((4, 2, 8), (2, 8, 4), (8, 4, 2))
LAST = 16


def summed(me, keep_1, others_1, keep_2, others_2, mark, weights, gain, result_of, side_of, tokens_of):
    count, width = keep_1.shape
    total = 2 * count
    unit = 8 * 8
    sizes = [total // unit // 3 * unit] * 2
    sizes.append(total - sum(sizes))
    parts = call(
        functools.partial(cut_kernel, [order[0] for order in ORDERS]),
        (me, keep_1, keep_2, mark, *others_1, *others_2),
        [shape(size // 2, width) for size in sizes for _ in range(2)],
        [shape(total, width)],
        scalars=1, limit=8,
    )
    d_given, d_own, mark = side_of(parts[0])
    result, mark_2 = result_of(parts[0])
    parts = [[parts[2 * i], swapped(parts[2 * i + 1], ORDERS[i][0])] for i in range(3)]
    for step in (1, 2):
        for i in range(3):
            half, mask = shape(sizes[i] >> (step + 1), width), ORDERS[i][step]
            place = (mark, mark_2) if step == 1 else ()
            keep, send = call(
                functools.partial(halve_kernel, mask), (me, *parts[i], *place), [half, half], scalars=1
            )
            parts[i] = [keep, swapped(send, mask)]
    for i in (0, 2, 1):
        if i == 1:
            part, d_going = call(first_kernel, (*parts[i], d_given), [parts[i][0], d_given])
            d_other = across(d_going)
        else:
            (part,) = call(add_kernel, parts[i], [parts[i][0]])
        mask, other = LAST, swapped(part, LAST)
        while 2 * mask < devices():
            (part,) = call(add_kernel, (part, other), [part])
            mask *= 2
            other = swapped(part, mask)
        (parts[i],) = call(last_kernel, (part, other), [part])
    for step in (2, 1, 0):
        for i in range(3):
            mask = ORDERS[i][step]
            place = {(2, 1): (d_other,), (0, 2): (mark,)}.get((step, i), ())
            (parts[i],) = call(
                functools.partial(double_kernel, mask), (me, parts[i], swapped(parts[i], mask), *place),
                [shape(2 * parts[i].shape[0], width)], scalars=1,
            )
        if step == 2:
            d_tokens, mark = tokens_of(parts[0], d_own, d_other)
    others = [swapped(part, 1) for part in parts]
    ranges, at = [], 0
    for i, size in enumerate(sizes):
        for exchange in range(2):
            start, stop = max(at, exchange * count), min(at + size, (exchange + 1) * count)
            if start < stop:
                ranges.append((i, start - at, stop - start, exchange, start - exchange * count))
        at += size
    held = written(me, gain, weights, parts, ranges, count, 0)
    *gradients, d_gain = written(me, gain, weights, others, ranges, count, 1, held)
    return gradients, d_gain.reshape(width), d_tokens, result


def body(tokens, gain, wq, wk, wv, wo, neighbour_list, neighbour_count, cotangent):
    rows, width = tokens.shape
    me = (lax.axis_index("space") * lax.axis_size("slab") + lax.axis_index("slab")).astype(jnp.int32)[None]
    parity = (lax.axis_index("space") % 2).astype(jnp.int32)[None]
    counts = neighbour_count[None, :]
    near = [across(tokens[i * PT : (i + 1) * PT]) for i in range(2)]
    gain_row = gain[None, :]
    stack_rows, stack_columns = shape(HEADS * 4 * HD, rows, dtype=BF16), shape(rows, HEADS * 4 * HD, dtype=BF16)
    turned, square, pair = pairs(width, rows), pairs(width, width), pairs(rows, width)
    whole, whole_t, scalars = shape(rows, width), shape(width, rows), shape(HEADS, rows)
    weights = call(weight_kernel, (me, parity, wq, wk, wv, wo), square * 4, scalars=2, limit=20)
    near[0], *weights = lax.optimization_barrier((near[0], *weights))
    far = [onward(near[0])]
    wq_h, wq_l, wk_h, wk_l, wv_h, wv_l, wo_h, wo_l = weights
    (
        ht_h, ht_l, q_t, q_stack, k_stack, v_stack, kt_h, kt_l, vt_h, vt_l, d_mixed_t, d_stack,
    ) = call(
        own_kernel,
        (near[0], tokens, gain_row, cotangent, *weights),
        [*turned, whole_t, stack_rows, stack_columns, stack_columns, *turned, *turned, whole_t, stack_rows],
        limit=LIMITS[0], us=1,
    )
    near[1], q_stack = lax.optimization_barrier((near[1], q_stack))
    far.append(onward(near[1]))
    w_k, w_v = (wk_h, wk_l), (wv_h, wv_l)
    ht2_h, ht2_l, kt2_h, kt2_l, k_near, v_near, vt2_h, vt2_l = call(
        near_side_kernel,
        (*near, gain_row, *w_k, *w_v),
        [*turned, *turned, stack_columns, stack_columns, *turned],
        limit=LIMITS[1], us=1,
    )
    e_h, e_l, d_scores, mixed, tops, totals = call(
        near_kernel,
        (
            parity, neighbour_list, counts, far[0], q_stack, k_stack, v_stack, vt_h, vt_l, d_stack, k_near, v_near,
            vt2_h, vt2_l,
        ),
        [*pairs(HEADS, 2 * rows, rows), shape(HEADS, 2 * rows, rows), whole_t, scalars, scalars],
        [shape(8, rows)],
        scalars=3, limit=LIMITS[1], us=1,
    )
    half_stack, half_t = shape(PT, HEADS * 4 * HD, dtype=BF16), pairs(width, PT)
    first = call(
        far_side_kernel,
        (tops, far[0], gain_row, *w_k, *w_v),
        [shape(PT, width), shape(PT, width), half_stack, half_stack, *half_t],
        limit=LIMITS[1], us=1,
    )
    (
        hidden3, key3, u_h, u_l, mixed_t, deltas, shares, shares_1, dk3_h, dk3_l, dv3_h, dv3_l,
        d_far,
    ) = call(
        far_kernel,
        (
            parity, neighbour_list, counts, *first, far[1], gain_row, q_t, q_stack, d_mixed_t, d_stack, mixed, tops, totals,
            *w_k, *w_v,
        ),
        [
            whole, whole, *pairs(HEADS, rows, rows), whole_t, scalars, scalars, scalars, *pair, *pair,
            whole,
        ],
        [shape(8, rows), half_stack, half_stack, *half_t, *pairs(2, rows, rows)],
        scalars=3, limit=LIMITS[2], us=1,
    )
    d_back = homeward(d_far)
    dq_t, dk_h, dk_l, dv_h, dv_l = call(
        back_kernel,
        (
            q_t, d_mixed_t, kt_h, kt_l, kt2_h, kt2_l, key3, e_h, e_l, d_scores, u_h, u_l, deltas, shares,
            shares_1,
        ),
        [whole_t, *pairs(2 * rows, width), *pairs(2 * rows, width)],
        [*pairs(2, 2 * rows, rows), *turned],
        limit=LIMITS[4], us=0.001,
    )
    pieces = [shape(width // PIECES, width)] * PIECES
    ht3_h, ht3_l, keep_1, *sends_1 = call(
        mix_kernel,
        (me, mixed_t, ht_h, ht_l, ht2_h, ht2_l, hidden3, dv_h, dv_l, dv3_h, dv3_l, cotangent),
        [*turned, shape(width, width), *pieces],
        [shape(width, width), shape(width, width)],
        scalars=1, limit=LIMITS[3], us=0.001,
    )
    others_1 = [swapped(send, 1) for send in sends_1]
    grad_q, grad_k, dq_h, dq_l = call(
        grad_kernel,
        (ht_h, ht_l, ht2_h, ht2_l, ht3_h, ht3_l, dq_t, dk_h, dk_l, dk3_h, dk3_l),
        [shape(width, width), shape(width, width), *pair],
        limit=LIMITS[5], us=0.001,
    )
    keep_2, *sends_2 = call(
        core_kernel, (me, grad_q, grad_k, keep_1), [shape(width, width), *pieces], scalars=1, limit=8, us=0.001
    )
    others_2 = [swapped(send, 1) for send in sends_2]
    d_back, mark = call(arrive_kernel, (d_back,), [whole, MARK], us=20)

    def result_of(place):
        return call(result_kernel, (place, mixed_t, tokens, wo_h, wo_l), [whole, MARK], limit=LIMITS[3], us=1)

    def side_of(place):
        inputs = (place, d_back, dq_h, dq_l, dk_h, dk_l, dv_h, dv_l, wq_h, wq_l, *w_k, *w_v)
        return call(side_kernel, inputs, [whole, whole, MARK], limit=LIMITS[3], us=1)

    def tokens_of(place, d_own, d_other):
        inputs = (place, tokens, gain_row, cotangent, d_own, d_other)
        return call(tokens_kernel, inputs, [whole, MARK], limit=8)

    (grad_o, grad_v, grad_q, grad_k), d_gain, d_tokens, result = summed(
        me, keep_1, others_1, keep_2, others_2, mark, (wv_h, wv_l, wq_h, wq_l, *w_k), gain_row, result_of, side_of, tokens_of
    )
    return (result, d_tokens, d_gain, grad_q, grad_k, grad_v, grad_o)


UNROLL = True
PIECES = 1
LIMITS = (8, 8, 8, 8, 8, 8)


def solution(mesh):
    tokens = P(("space", "slab"), None)
    return jax.shard_map(
        body,
        mesh=mesh,
        in_specs=(tokens, P(), P(), P(), P(), P(), tokens, P(("space", "slab")), tokens),
        out_specs=(tokens, tokens, P(), P(), P(), P(), P()),
        check_vma=False,
    )
```
